32 devices in a mesh: dp: 4 (over x, core), seq: 4 (over z), mp: 2 (over y).
Axes of the slice: x: 2, y: 2, z: 4, core: 2. Of those that a mesh axis runs over, the one named last changes fastest.
Arguments:
- queries: bfloat16 [4, 512, 2048], P('dp', 'seq', 'mp'), may hold values from -6 to 6
- keys: bfloat16 [4, 512, 2048], P('dp', 'seq', 'mp'), may hold values from -6 to 6
- values: bfloat16 [4, 512, 2048], P('dp', 'seq', 'mp'), may hold values from -6 to 6
- cross_queries: bfloat16 [4, 512, 2048], P('dp', 'seq', 'mp'), may hold values from -6 to 6
- neighbour_ids: int32 [4, 8, 2, 2], P('dp', 'seq'), may hold values from 0 to 5, as said below
- database: bfloat16 [4, 2, 6, 128, 2048], P('dp', None, None, None, 'mp'), may hold values from -6 to 6
- out_weight: bfloat16 [2048, 4096], P('mp'), may hold values from -2.5 to 2.5
Outputs:
- mixed: bfloat16 [4, 512, 4096], P('dp', 'seq', 'mp')
The draws below stay inside these ranges and needn't reach their ends.
Inputs may be any that keep to these rules, and one draw needn't show every extreme that they name: `neighbour_ids`: entry [b, c, n, 0] is the database shard and [b, c, n, 1] the block of the n-th neighbour of span c of sequence b. Among the neighbours of the 2 spans held by one index of dp and seq, at most 3 name one shard; in every draw, for some seq index, the spans of every dp index name exactly 3 neighbours of one common shard.
All inputs are finite; a program needn't handle non-finite values.
Results may differ from the reference program's by a relative error of at most 0.012.
Values may be sent and summed in bfloat16 or wider, within the bound.
A program may use at most 128 MiB of HBM per device.

```python
import math
import jax
import jax.numpy as jnp
from jax import lax

D = 4096
HD = 128
SPAN = 64
NEIGH = 2
RETR = 128
HEADS = 16
TOK_DEV = 128
DB_BLOCKS = 6
FEAT = 2048
LENGTH = 512
SPANS = 8
BATCH = 4
SHARDS = 4
CAP = 3


def neighbour_table(key):
    base = jax.random.fold_in(key, 7001)
    splits = jax.random.split(base, 7)
    spans_here = TOK_DEV // SPAN
    per_device = spans_here * NEIGH
    groups = SPANS // spans_here
    hottest = jax.random.randint(splits[0], (groups,), 0, SHARDS)
    flagged = jax.random.randint(splits[1], (BATCH, groups), 0, 2)
    forced = jax.random.randint(splits[2], (), 0, groups)
    flagged = jnp.where(jnp.arange(groups)[None, :] == forced, 1, flagged)
    rank_list = jnp.arange(per_device)
    hot_wide = hottest[None, :, None]
    others = (hot_wide + 1 + jax.random.randint(splits[3], (BATCH, groups, per_device), 0, SHARDS - 1)) % SHARDS
    shifts = jax.random.randint(splits[4], (BATCH, groups, 1), 0, SHARDS - 1)
    cycled = (hot_wide + 1 + (rank_list[None, None, :] + shifts) % (SHARDS - 1)) % SHARDS
    hot_heavy = jnp.where(rank_list[None, None, :] < CAP, hot_wide, others)
    shard_ids = jnp.where(flagged[:, :, None] == 1, hot_heavy, cycled)
    shuffle_keys = jax.random.randint(splits[5], (BATCH, groups, per_device), 0, 1 << 20) * per_device + rank_list[None, None, :]
    ordering = jnp.argsort(shuffle_keys, axis=-1, stable=True)
    shard_ids = jnp.take_along_axis(shard_ids, ordering, axis=-1)
    block_ids = jax.random.randint(splits[6], (BATCH, groups, per_device), 0, DB_BLOCKS)
    id_table = jnp.stack([shard_ids, block_ids], axis=-1)
    return id_table.reshape(BATCH, SPANS, NEIGH, 2).astype(jnp.int32)


def self_pair(key):
    base = jax.random.fold_in(key, 7005)
    first_key, second_key = jax.random.split(base, 2)
    query_draw = jnp.clip(jax.random.normal(first_key, (BATCH, LENGTH, FEAT), jnp.float32) * 1.3, -6.0, 6.0)
    key_draw = jnp.clip(jax.random.normal(second_key, (BATCH, LENGTH, FEAT), jnp.float32) * 1.3, -6.0, 6.0)
    return (query_draw, key_draw)


def draw_queries(key, part):
    return self_pair(key)[0].astype(jnp.bfloat16)


def draw_keys(key, part):
    return self_pair(key)[1].astype(jnp.bfloat16)


def draw_neighbour_ids(key, part):
    return neighbour_table(key)


def draw_cross_queries(key, part):
    base = jax.random.fold_in(key, 7003)
    cross_draw = jnp.clip(jax.random.normal(base, (BATCH, LENGTH, FEAT), jnp.float32) * 1.3, -6.0, 6.0)
    return cross_draw.astype(jnp.bfloat16)


def draw_database(key, part):
    base = jax.random.fold_in(key, 7002)
    first_key, second_key = jax.random.split(base, 2)
    key_part = jnp.clip(jax.random.normal(first_key, (SHARDS, DB_BLOCKS, RETR, FEAT), jnp.float32) * 1.3, -6.0, 6.0)
    value_part = jnp.clip(jax.random.normal(second_key, (SHARDS, DB_BLOCKS, RETR, FEAT), jnp.float32), -6.0, 6.0)
    return jnp.stack([key_part, value_part], axis=1).astype(jnp.bfloat16)


def levels(key, dims, pieces, least, top_value):
    level = 1.0
    for dim, shards_of in pieces:
        draws = jax.random.uniform(jax.random.fold_in(jax.random.fold_in(key, 6), dim), (shards_of,), jnp.float32, least / len(pieces), top_value / len(pieces))
        level = level * jnp.repeat(jnp.exp(draws), dims[dim] // shards_of).reshape((-1,) + (1,) * (len(dims) - 1 - dim))
    return level


def bell_draw(rng, extent, deviation, bound, cuts=(), kind=jnp.bfloat16):
    entries = jax.random.normal(rng, extent, jnp.float32) * deviation
    if len(cuts) > 0:
        entries = levels(rng, extent, cuts, -0.22, 0.18) * entries
    return jnp.clip(entries, min=-bound, max=bound).astype(kind)


def setup_inputs(seed: int = 0) -> dict:
    streams_of = jax.random.split(jax.random.key(seed), 8)
    queries = draw_queries(jax.random.fold_in(streams_of[7], 71), 0)
    keys = draw_keys(jax.random.fold_in(streams_of[7], 71), 0)
    values = bell_draw(streams_of[2], (BATCH, LENGTH, FEAT), 1.0, 6.0, ((0, 4), (1, 4), (2, 2)))
    cross_queries = draw_cross_queries(jax.random.fold_in(streams_of[7], 71), 0)
    neighbour_ids = draw_neighbour_ids(jax.random.fold_in(streams_of[7], 71), 0)
    database = draw_database(jax.random.fold_in(streams_of[7], 71), 0)
    out_weight = bell_draw(streams_of[6], (FEAT, D), 0.2, 2.5, ((0, 2),))
    return dict(queries=queries, keys=keys, values=values, cross_queries=cross_queries, neighbour_ids=neighbour_ids, database=database, out_weight=out_weight)


masked_score = -1e+30

def self_attend(query_seq, key_seq, value_seq):
    score_scale = 1.0 / math.sqrt(HD)
    key_heads = key_seq.reshape(LENGTH, HEADS, HD).astype(jnp.float32)
    value_heads = value_seq.reshape(LENGTH, HEADS, HD).astype(jnp.float32)
    query_blocks = query_seq.reshape(LENGTH // TOK_DEV, TOK_DEV, HEADS, HD)
    block_starts = (jnp.arange(LENGTH // TOK_DEV) * TOK_DEV).astype(jnp.int32)
    key_pos = jnp.arange(LENGTH).astype(jnp.int32)

    def one_block(operands):
        block_rows, block_start = operands
        scores = jnp.einsum('qhe,khe->hqk', block_rows.astype(jnp.float32), key_heads) * score_scale
        query_pos = block_start + jnp.arange(TOK_DEV).astype(jnp.int32)
        allowed = (key_pos[None, :] <= query_pos[:, None])[None]
        scores = jnp.where(allowed, scores, masked_score)
        row_max = lax.optimization_barrier(jnp.max(scores, axis=2, keepdims=True))
        weights = jnp.where(allowed, jnp.exp(scores - row_max), 0.0)
        totals = lax.optimization_barrier(jnp.sum(weights, axis=2))
        rounded = lax.optimization_barrier(weights.astype(jnp.bfloat16)).astype(jnp.float32)
        summed = jnp.einsum('hqk,khe->qhe', rounded, value_heads)
        return (summed / jnp.transpose(totals)[:, :, None]).reshape(TOK_DEV, HEADS * HD)
    return lax.map(one_block, (query_blocks, block_starts)).reshape(LENGTH, HEADS * HD)

def cross_attend(cross_seq, id_seq, database):
    score_scale = 1.0 / math.sqrt(HD)
    padded = jnp.concatenate([jnp.zeros((1, FEAT), cross_seq.dtype), cross_seq, jnp.zeros((SPAN - 1, FEAT), cross_seq.dtype)], axis=0)
    padded = padded.reshape(SPANS + 1, SPAN, HEADS, HD)

    def one_group(operands):
        group_rows, group_index = operands
        source = jnp.maximum(group_index - 1, 0)
        chosen = id_seq[source]
        picked_keys = database[chosen[:, 0], 0, chosen[:, 1]].reshape(NEIGH * RETR, HEADS, HD).astype(jnp.float32)
        picked_values = database[chosen[:, 0], 1, chosen[:, 1]].reshape(NEIGH * RETR, HEADS, HD).astype(jnp.float32)
        scores = jnp.einsum('qhe,khe->hqk', group_rows.astype(jnp.float32), picked_keys) * score_scale
        row_max = lax.optimization_barrier(jnp.max(scores, axis=2, keepdims=True))
        weights = jnp.exp(scores - row_max)
        totals = lax.optimization_barrier(jnp.sum(weights, axis=2))
        rounded = lax.optimization_barrier(weights.astype(jnp.bfloat16)).astype(jnp.float32)
        summed = jnp.einsum('hqk,khe->qhe', rounded, picked_values)
        live = (group_index >= 1).astype(jnp.float32)
        return (summed / jnp.transpose(totals)[:, :, None]).reshape(SPAN, FEAT) * live
    group_ids = jnp.arange(SPANS + 1).astype(jnp.int32)
    outputs = lax.map(one_group, (padded, group_ids))
    return outputs.reshape((SPANS + 1) * SPAN, FEAT)[1:1 + LENGTH]

def reference(queries, keys, values, cross_queries, neighbour_ids, database, out_weight):
    results = []
    for batch_index in range(BATCH):
        self_out = self_attend(queries[batch_index], keys[batch_index], values[batch_index])
        cross_out = cross_attend(cross_queries[batch_index], neighbour_ids[batch_index], database)
        attended = (self_out + cross_out).astype(jnp.bfloat16)
        results.append(jnp.dot(attended, out_weight, preferred_element_type=jnp.float32).astype(jnp.bfloat16))
    return jnp.stack(results)
```

```python
import functools
import math

import jax
import jax.numpy as jnp
from jax import lax
from jax.experimental import pallas as pl
from jax.experimental.pallas import tpu as pltpu
from jax.sharding import PartitionSpec as P

HD = 128
SPAN = 64
NEIGH = 2
RETR = 128


masked_score = -1e30


def passed_along(value, axis, steps):
    count = lax.axis_size(axis)
    leading, last = (max(0, -steps), min(count, count - steps))
    return lax.ppermute(value, axis, [(source, source + steps) for source in range(leading, last)])


def fold_block(carry_state, query_rows, query_pos, key_rows, value_rows, key_pos, score_scale):
    summed, running_max, totals = carry_state
    scores = (
        jnp.einsum("qhe,khe->hqk", query_rows, key_rows, preferred_element_type=jnp.float32)
        * score_scale
    )
    allowed = (key_pos[None, :] <= query_pos[:, None])[None]
    scores = jnp.where(allowed, scores, masked_score)
    new_max = jnp.maximum(running_max, jnp.max(scores, axis=2))
    weights = jnp.where(allowed, jnp.exp(scores - new_max[:, :, None]), 0.0)
    totals = jnp.sum(weights, axis=2)
    summed = jnp.einsum(
        "hqk,khe->hqe", weights.astype(jnp.bfloat16), value_rows, preferred_element_type=jnp.float32
    )
    return (summed, new_max, totals)


def empty_state(heads_here, row_total):
    return (
        jnp.zeros((heads_here, row_total, HD), jnp.float32),
        jnp.full((heads_here, row_total), masked_score, jnp.float32),
        jnp.zeros((heads_here, row_total), jnp.float32),
    )


def finish_state(carry_state):
    summed, running_max, totals = carry_state
    normed = summed / totals[:, :, None]
    return jnp.transpose(normed, (1, 0, 2)).reshape(
        normed.shape[1], normed.shape[0] * normed.shape[2]
    )


def per_device(queries, keys, values, cross_queries, neighbour_ids, database, out_weight):
    row_count = queries.shape[1]
    feat_here = queries.shape[2]
    heads_here = feat_here // HD
    score_scale = 1.0 / math.sqrt(HD)
    seq_index = lax.axis_index("seq")
    own_first = seq_index * row_count
    own_pos = own_first + jnp.arange(row_count, dtype=jnp.int32)
    query_rows = queries[0].reshape(row_count, heads_here, HD)
    groups_list = [(query_rows, own_pos)]
    start_states = tuple(
        (empty_state(heads_here, group_pos.shape[0]) for group_rows, group_pos in groups_list)
    )
    key_block = lax.all_gather(keys, "seq", axis=1, tiled=True)[0]
    block_rows = key_block.shape[0]
    key_rows = key_block.reshape(block_rows, heads_here, HD)
    value_rows = lax.all_gather(values, "seq", axis=1, tiled=True)[0].reshape(
        block_rows, heads_here, HD
    )
    key_pos = jnp.arange(block_rows, dtype=jnp.int32)
    updated = []
    for carry_state, (group_rows, group_pos) in zip(start_states, groups_list):

        def visit_block(kept_state, group_rows=group_rows, group_pos=group_pos):
            return fold_block(
                kept_state, group_rows, group_pos, key_rows, value_rows, key_pos, score_scale
            )

        updated.append(visit_block(carry_state))
    states = tuple(updated)
    self_out = finish_state(states[0])
    id_pairs = neighbour_ids[0].reshape(-1, 2)
    shard_of = id_pairs[:, 0]
    block_of = id_pairs[:, 1]
    spans_here = neighbour_ids.shape[1]
    every_shard = lax.all_gather(database, "dp", axis=0, tiled=True)
    fetched = jnp.stack([every_shard[shard_of, 0, block_of], every_shard[shard_of, 1, block_of]])
    neighbour_rows = NEIGH * RETR
    grouped = fetched.reshape(2, spans_here, neighbour_rows, heads_here, HD)
    previous = passed_along(grouped[:, spans_here - 1], "seq", 1)
    extended = jnp.concatenate([previous[:, None], grouped], axis=1)
    padded = jnp.concatenate(
        [
            jnp.zeros((1, feat_here), jnp.bfloat16),
            cross_queries[0],
            jnp.zeros((SPAN - 1, feat_here), jnp.bfloat16),
        ],
        axis=0,
    )
    padded = padded.reshape(spans_here + 1, SPAN, heads_here, HD)
    scores = (
        jnp.einsum("gqhe,gkhe->ghqk", padded, extended[0], preferred_element_type=jnp.float32)
        * score_scale
    )
    row_max = jnp.max(scores, axis=3, keepdims=True)
    weights = jnp.exp(scores - row_max)
    totals = jnp.sum(weights, axis=3)
    summed_cross = jnp.einsum(
        "ghqk,gkhe->gqhe",
        weights.astype(jnp.bfloat16),
        extended[1],
        preferred_element_type=jnp.float32,
    )
    cross_out = summed_cross / jnp.transpose(totals, (0, 2, 1))[:, :, :, None]
    valid = ((jnp.arange(spans_here + 1) > 0) | (seq_index > 0)).astype(jnp.float32)
    cross_out = cross_out * valid[:, None, None, None]
    cross_out = cross_out.reshape((spans_here + 1) * SPAN, feat_here)[1 : 1 + row_count]
    attended = (self_out + cross_out).astype(jnp.bfloat16)
    own_sums = lax.psum_scatter(
        lax.dot_general(
            out_weight, attended, (((0,), (1,)), ((), ())), preferred_element_type=jnp.float32
        ).astype(jnp.bfloat16),
        "mp",
        scatter_dimension=0,
        tiled=True,
    )
    return jnp.transpose(own_sums)[None]

NEG = -1e30
LOG2E = 1.4426950408889634
PAIR = 2 * HD
PIECE = PAIR + 16
TILE = 512
MESH = pl.DeviceIdType.MESH


def nt_dot(a, b):
    return lax.dot_general(a, b, (((1,), (1,)), ((), ())), preferred_element_type=jnp.float32)


def tn_dot(a, b):
    return lax.dot_general(a, b, (((0,), (0,)), ((), ())), preferred_element_type=jnp.float32)


def pack_piece(parts):
    row = lax.broadcasted_iota(jnp.int32, (16, HD), 0)
    stats = jnp.zeros((16, HD), jnp.float32)
    for index, (_, lse) in enumerate(parts):
        rest = lse
        for term in range(3):
            rounded = rest.astype(jnp.bfloat16).astype(jnp.float32)
            stats = jnp.where(row == 3 * index + term, rounded, stats)
            rest = rest - rounded
    return jnp.concatenate(
        [parts[0][0].astype(jnp.bfloat16), parts[1][0].astype(jnp.bfloat16), stats.astype(jnp.bfloat16)],
        axis=0,
    )


def attend_pair(q, k, v, scale, allowed=None):
    parts = []
    for h in range(2):
        cols = slice(h * HD, (h + 1) * HD)
        scores = nt_dot(k[:, cols], q[:, cols]) * scale
        if allowed is not None:
            scores = jnp.where(allowed, scores, NEG)
        top = jnp.max(scores, axis=0, keepdims=True)
        weights = jnp.exp2(scores - top)
        total = jnp.sum(weights, axis=0, keepdims=True)
        summed = tn_dot(v[:, cols], weights.astype(jnp.bfloat16)) / total
        parts.append((summed, top + jnp.log2(total)))
    return pack_piece(parts)


def cross_pair(q, keys, vals, owned, in_first, in_last, scale):
    parts = []
    for h in range(2):
        cols = slice(h * HD, (h + 1) * HD)
        qh = q[:, cols]
        s0, s1, s2 = [nt_dot(k[:, cols], qh) for k in keys]
        scores = jnp.where(in_first, s0, jnp.where(in_last, s2, s1)) * scale
        scores = jnp.where(owned, scores, NEG)
        top = jnp.max(scores, axis=0, keepdims=True)
        weights = jnp.where(owned, jnp.exp2(scores - top), 0.0)
        total = jnp.sum(weights, axis=0, keepdims=True)
        some = total > 0.0
        safe = jnp.where(some, total, 1.0)
        low = weights.astype(jnp.bfloat16)
        o0, o1, o2 = [tn_dot(v[:, cols], low) for v in vals]
        summed = jnp.where(in_first, o0, jnp.where(in_last, o2, o1)) / safe
        parts.append((summed, jnp.where(some, top + jnp.log2(safe), NEG)))
    return pack_piece(parts)


def merge_pieces(pieces, h):
    lses = []
    for piece in pieces:
        stats = piece[PAIR:, :].astype(jnp.float32)
        lses.append(stats[3 * h : 3 * h + 1] + stats[3 * h + 1 : 3 * h + 2] + stats[3 * h + 2 : 3 * h + 3])
    top = functools.reduce(jnp.maximum, lses)
    shares = [jnp.exp2(lse - top) for lse in lses]
    total = functools.reduce(jnp.add, shares)
    summed = 0.0
    for piece, share in zip(pieces, shares):
        summed = summed + piece[h * HD : (h + 1) * HD, :].astype(jnp.float32) * (share / total)
    return summed


def layer_kernel(
    q, k, v, cq, ids, db_hbm, w_hbm, out,
    db, w, kv0, qin, cqin, sp, stx, cp, ctx, att, ptx, prx, ids_tx, ids_rx, ids_s,
    db_sem, w_sem, ids_sem, kv_ss, kv_rs, q_ss, q_rs, cq_ss, cq_rs, sp_ss, sp_rs, cp_ss, cp_rs,
    i1_ss, i1_rs, i2_ss, i2_rs, p_ss, p_rs,
):
    d = lax.axis_index("dp")
    s = lax.axis_index("seq")
    m = lax.axis_index("mp")
    dps = cqin.shape[0]
    chunks = cqin.shape[1]
    rows = q.shape[0]
    half = out.shape[1]
    tiles = half // TILE
    scale = LOG2E / math.sqrt(HD)
    other = 1 - m

    def cols_of(c):
        return pl.ds(pl.multiple_of(c * PAIR, PAIR), PAIR)

    def remote(src, dst, ss, rs, **where):
        return pltpu.make_async_remote_copy(
            src_ref=src, dst_ref=dst, send_sem=ss, recv_sem=rs, device_id=where, device_id_type=MESH
        )

    db_copy = pltpu.make_async_copy(db_hbm, db, db_sem)
    db_copy.start()
    w_copies = [
        pltpu.make_async_copy(
            w_hbm.at[:, pl.ds(pl.multiple_of(side * half, TILE), half)], w.at[i], w_sem.at[i]
        )
        for i, side in enumerate((other, m))
    ]

    barrier = pltpu.get_barrier_semaphore()
    for j in range(1, dps):
        pl.semaphore_signal(barrier, inc=1, device_id={"dp": lax.rem(d + j, dps)}, device_id_type=MESH)
    for j in range(1, 4):
        pl.semaphore_signal(barrier, inc=1, device_id={"seq": lax.rem(s + j, 4)}, device_id_type=MESH)
    pl.semaphore_signal(barrier, inc=1, device_id={"mp": other}, device_id_type=MESH)
    pl.semaphore_wait(barrier, dps + 3)

    def id_hop():
        return remote(ids, ids_tx.at[1], i1_ss, i1_rs, seq=lax.rem(s + 1, 4))

    def kv_hop(c, which):
        return remote((k, v)[which].at[:, cols_of(c)], kv0.at[c, which], kv_ss.at[c, which], kv_rs.at[c, which], seq=1)

    def q_hop(c, dest):
        slot = jnp.maximum(s - 2, 0)
        return remote(q.at[:, cols_of(c)], qin.at[slot, c], q_ss.at[dest - 1, c], q_rs.at[slot, c], seq=dest)

    def q_arrived(c, slot):
        remote(q.at[:, cols_of(c)], qin.at[slot, c], q_ss.at[0, c], q_rs.at[slot, c], seq=1).wait_recv()

    def cq_hop(c, j):
        return remote(
            cq.at[:, cols_of(c)], cqin.at[j, c], cq_ss.at[j, c], cq_rs.at[j, c], dp=lax.rem(d + j, dps)
        )

    def sp_hop(c, slot, dest, place):
        return remote(stx.at[slot, c], sp.at[place, c], sp_ss.at[slot, c], sp_rs.at[place, c], seq=dest)

    def cp_hop(c, j):
        return remote(
            ctx.at[j, c], cp.at[j, c], cp_ss.at[j, c], cp_rs.at[j, c], dp=lax.rem(d - j + dps, dps)
        )

    def id_share(j):
        return remote(ids_tx, ids_rx.at[j], i2_ss.at[j], i2_rs.at[j], dp=lax.rem(d + j, dps))

    def p_hop(t):
        return remote(ptx.at[t], prx.at[t], p_ss.at[t], p_rs.at[t], mp=other)

    @pl.when(s < 3)
    def _():
        id_hop().start()

    @pl.loop(0, chunks)
    def _(c):
        @pl.when(s == 0)
        def _():
            kv_hop(c, 0).start()
            kv_hop(c, 1).start()

        @pl.when(s >= 2)
        def _():
            q_hop(c, 1).start()

        @pl.when(s == 3)
        def _():
            q_hop(c, 2).start()

        @pl.loop(1, dps)
        def _(j):
            cq_hop(c, j).start()

        cqin[0, c] = cq[:, cols_of(c)]

    for copy in w_copies:
        copy.start()

    ids_tx[0] = ids[...]

    @pl.when(s == 0)
    def _():
        ids_tx[1] = jnp.zeros_like(ids)

    @pl.when(s > 0)
    def _():
        id_hop().wait_recv()

    for j in range(1, dps):
        id_share(j).start()
    ids_rx[0] = ids_tx[...]

    neutral = jnp.concatenate(
        [jnp.zeros((PAIR, HD), jnp.bfloat16), jnp.full((16, HD), NEG, jnp.bfloat16)], axis=0
    )
    key_at = lax.broadcasted_iota(jnp.int32, (rows, HD), 0)
    query_at = lax.broadcasted_iota(jnp.int32, (rows, HD), 1)
    causal = key_at <= query_at

    @pl.loop(0, chunks)
    def _(c):
        cols = cols_of(c)
        sp[0, c] = attend_pair(q[:, cols], k[:, cols], v[:, cols], scale, causal)

        @pl.when(s < 1)
        def _():
            sp[1, c] = neutral

        @pl.when(s < 3)
        def _():
            sp[2, c] = neutral

    for j in range(1, dps):
        id_share(j).wait_recv()
    ids_copy = pltpu.make_async_copy(ids_rx, ids_s, ids_sem)
    ids_copy.start()
    ids_copy.wait()
    db_copy.wait()

    lane = lax.broadcasted_iota(jnp.int32, (1, HD), 1)
    in_first = lane < SPAN - 1
    in_last = lane == 2 * SPAN - 1
    live = jnp.logical_or(lane >= SPAN - 1, s > 0)

    @pl.loop(0, chunks)
    def _(c):
        cols = cols_of(c)

        @pl.when(s == 1)
        def _():
            kv_hop(c, 0).wait_recv()
            kv_hop(c, 1).wait_recv()
            k0 = kv0[c, 0]
            v0 = kv0[c, 1]
            sp[1, c] = attend_pair(q[:, cols], k0, v0, scale)

            @pl.loop(0, 2)
            def _(slot):
                q_arrived(c, slot)
                both_k = jnp.concatenate([kv0[c, 0], k[:, cols]], axis=0)
                both_v = jnp.concatenate([kv0[c, 1], v[:, cols]], axis=0)
                stx[slot, c] = attend_pair(qin[slot, c], both_k, both_v, scale)
                sp_hop(c, slot, 2 + slot, 1).start()

        @pl.when(s == 2)
        def _():
            q_arrived(c, 1)
            stx[1, c] = attend_pair(qin[1, c], k[:, cols], v[:, cols], scale)
            sp_hop(c, 1, 3, 2).start()

        @pl.loop(0, dps)
        def _(turn):
            j = lax.rem(turn + 1, dps)

            @pl.when(j > 0)
            def _():
                cq_hop(c, j).wait_recv()

            keys, vals, shards = [], [], []
            for which, span in ((1, 1), (0, 0), (0, 1)):
                blocks = [ids_s[j, which, 0, span * 4 + n * 2 + 1] for n in range(NEIGH)]
                shards.append([ids_s[j, which, 0, span * 4 + n * 2] for n in range(NEIGH)])
                keys.append(jnp.concatenate([db[0, b, :, cols] for b in blocks], axis=0))
                vals.append(jnp.concatenate([db[1, b, :, cols] for b in blocks], axis=0))
            owned = []
            for n in range(NEIGH):
                shard = jnp.where(in_first, shards[0][n], jnp.where(in_last, shards[2][n], shards[1][n]))
                row = jnp.where(jnp.logical_and(shard == d, live), 1, 0)
                owned.append(jnp.broadcast_to(row, (RETR, HD)))
            owned = jnp.concatenate(owned, axis=0) > 0
            ctx[j, c] = cross_pair(cqin[j, c], keys, vals, owned, in_first, in_last, scale)

            @pl.when(j > 0)
            def _():
                cp_hop(c, j).start()

    @pl.loop(0, chunks)
    def _(c):
        @pl.when(s >= 2)
        def _():
            sp_hop(c, 0, 2, 1).wait_recv()

        @pl.when(s == 3)
        def _():
            sp_hop(c, 0, 3, 2).wait_recv()

        for j in range(1, dps):
            cp_hop(c, j).wait_recv()
        self_pieces = [sp[i, c] for i in range(3)]
        cross_pieces = [ctx[0, c]] + [cp[j, c] for j in range(1, dps)]
        for h in range(2):
            both = merge_pieces(self_pieces, h) + merge_pieces(cross_pieces, h)
            att[:, pl.ds(pl.multiple_of(c * PAIR + h * HD, HD), HD)] = both.T.astype(jnp.bfloat16)

    def tile_cols(t):
        return pl.ds(pl.multiple_of(t * TILE, TILE), TILE)

    w_copies[0].wait()

    @pl.loop(0, tiles)
    def _(t):
        ptx[t] = jnp.dot(
            att[...], w[0, :, tile_cols(t)], preferred_element_type=jnp.float32
        ).astype(jnp.bfloat16)
        p_hop(t).start()

    w_copies[1].wait()

    @pl.loop(0, tiles)
    def _(t):
        own = jnp.dot(att[...], w[1, :, tile_cols(t)], preferred_element_type=jnp.float32)
        p_hop(t).wait_recv()
        out[:, tile_cols(t)] = (own + prx[t].astype(jnp.float32)).astype(jnp.bfloat16)

    @pl.when(s < 3)
    def _():
        id_hop().wait_send()

    for j in range(1, dps):
        id_share(j).wait_send()

    @pl.loop(0, chunks)
    def _(c):
        @pl.when(s == 0)
        def _():
            kv_hop(c, 0).wait_send()
            kv_hop(c, 1).wait_send()

        @pl.when(s >= 2)
        def _():
            q_hop(c, 1).wait_send()

        @pl.when(s == 3)
        def _():
            q_hop(c, 2).wait_send()

        @pl.when(s == 1)
        def _():
            sp_hop(c, 0, 2, 1).wait_send()
            sp_hop(c, 1, 3, 1).wait_send()

        @pl.when(s == 2)
        def _():
            sp_hop(c, 1, 3, 2).wait_send()

        @pl.loop(1, dps)
        def _(j):
            cq_hop(c, j).wait_send()
            cp_hop(c, j).wait_send()

    @pl.loop(0, tiles)
    def _(t):
        p_hop(t).wait_send()


def fused_device(queries, keys, values, cross_queries, neighbour_ids, database, out_weight):
    rows, feat = queries.shape[1:]
    dps = lax.axis_size("dp")
    chunks = feat // PAIR
    width = out_weight.shape[1]
    half = width // 2
    tiles = half // TILE
    ids = neighbour_ids.reshape(1, -1)
    ids = jnp.pad(ids, ((0, 7), (0, 128 - ids.shape[1])))
    bf16 = jnp.bfloat16
    dma = pltpu.SemaphoreType.DMA
    vmem = pl.BlockSpec(memory_space=pltpu.VMEM)
    anywhere = pl.BlockSpec(memory_space=pl.ANY)
    scratch = [
        pltpu.VMEM(database.shape[1:], bf16),
        pltpu.VMEM((2, feat, half), bf16),
        pltpu.VMEM((chunks, 2, rows, PAIR), bf16),
        pltpu.VMEM((2, chunks, rows, PAIR), bf16),
        pltpu.VMEM((dps, chunks, rows, PAIR), bf16),
        pltpu.VMEM((3, chunks, PIECE, rows), bf16),
        pltpu.VMEM((2, chunks, PIECE, rows), bf16),
        pltpu.VMEM((dps, chunks, PIECE, rows), bf16),
        pltpu.VMEM((dps, chunks, PIECE, rows), bf16),
        pltpu.VMEM((rows, feat), bf16),
        pltpu.VMEM((tiles, rows, TILE), bf16),
        pltpu.VMEM((tiles, rows, TILE), bf16),
        pltpu.VMEM((2, 8, 128), jnp.int32),
        pltpu.VMEM((dps, 2, 8, 128), jnp.int32),
        pltpu.SMEM((dps, 2, 8, 128), jnp.int32),
        dma, dma((2,)), dma,
        dma((chunks, 2)), dma((chunks, 2)),
        dma((2, chunks)), dma((2, chunks)),
        dma((dps, chunks)), dma((dps, chunks)),
        dma((2, chunks)), dma((3, chunks)),
        dma((dps, chunks)), dma((dps, chunks)),
        dma, dma, dma((dps,)), dma((dps,)),
        dma((tiles,)), dma((tiles,)),
    ]
    flops = 2 * rows * feat * width + 2 * 2 * rows * feat * (8 * rows + dps * 6 * RETR)
    result = pl.pallas_call(
        layer_kernel,
        out_shape=jax.ShapeDtypeStruct((rows, half), bf16),
        in_specs=[vmem] * 5 + [anywhere] * 2,
        out_specs=vmem,
        scratch_shapes=scratch,
        compiler_params=pltpu.CompilerParams(
            collective_id=0, has_side_effects=True, vmem_limit_bytes=50 * 1024 * 1024
        ),
        cost_estimate=pl.CostEstimate(
            flops=flops, bytes_accessed=2 * (feat * width + database.size), transcendentals=0
        ),
    )(queries[0], keys[0], values[0], cross_queries[0], ids, database[0], out_weight)
    return result[None]


def solution(mesh):
    placed = (
        P("dp", "seq", "mp"),
        P("dp", "seq", "mp"),
        P("dp", "seq", "mp"),
        P("dp", "seq", "mp"),
        P("dp", "seq", None, None),
        P("dp", None, None, None, "mp"),
        P("mp", None),
    )
    fits = mesh.shape["seq"] == 4 and mesh.shape["mp"] == 2
    return jax.shard_map(
        fused_device if fits else per_device,
        mesh=mesh,
        in_specs=placed,
        out_specs=P("dp", "seq", "mp"),
        check_vma=False,
    )
```

```python
import functools
import math

import jax
import jax.numpy as jnp
from jax import lax
from jax.experimental import pallas as pl
from jax.experimental.pallas import tpu as pltpu
from jax.sharding import PartitionSpec as P

HD = 128
SPAN = 64
NEIGH = 2
RETR = 128


masked_score = -1e30


def passed_along(value, axis, steps):
    count = lax.axis_size(axis)
    leading, last = (max(0, -steps), min(count, count - steps))
    return lax.ppermute(value, axis, [(source, source + steps) for source in range(leading, last)])


def fold_block(carry_state, query_rows, query_pos, key_rows, value_rows, key_pos, score_scale):
    summed, running_max, totals = carry_state
    scores = (
        jnp.einsum("qhe,khe->hqk", query_rows, key_rows, preferred_element_type=jnp.float32)
        * score_scale
    )
    allowed = (key_pos[None, :] <= query_pos[:, None])[None]
    scores = jnp.where(allowed, scores, masked_score)
    new_max = jnp.maximum(running_max, jnp.max(scores, axis=2))
    weights = jnp.where(allowed, jnp.exp(scores - new_max[:, :, None]), 0.0)
    totals = jnp.sum(weights, axis=2)
    summed = jnp.einsum(
        "hqk,khe->hqe", weights.astype(jnp.bfloat16), value_rows, preferred_element_type=jnp.float32
    )
    return (summed, new_max, totals)


def empty_state(heads_here, row_total):
    return (
        jnp.zeros((heads_here, row_total, HD), jnp.float32),
        jnp.full((heads_here, row_total), masked_score, jnp.float32),
        jnp.zeros((heads_here, row_total), jnp.float32),
    )


def finish_state(carry_state):
    summed, running_max, totals = carry_state
    normed = summed / totals[:, :, None]
    return jnp.transpose(normed, (1, 0, 2)).reshape(
        normed.shape[1], normed.shape[0] * normed.shape[2]
    )


def per_device(queries, keys, values, cross_queries, neighbour_ids, database, out_weight):
    row_count = queries.shape[1]
    feat_here = queries.shape[2]
    heads_here = feat_here // HD
    score_scale = 1.0 / math.sqrt(HD)
    seq_index = lax.axis_index("seq")
    own_first = seq_index * row_count
    own_pos = own_first + jnp.arange(row_count, dtype=jnp.int32)
    query_rows = queries[0].reshape(row_count, heads_here, HD)
    groups_list = [(query_rows, own_pos)]
    start_states = tuple(
        (empty_state(heads_here, group_pos.shape[0]) for group_rows, group_pos in groups_list)
    )
    key_block = lax.all_gather(keys, "seq", axis=1, tiled=True)[0]
    block_rows = key_block.shape[0]
    key_rows = key_block.reshape(block_rows, heads_here, HD)
    value_rows = lax.all_gather(values, "seq", axis=1, tiled=True)[0].reshape(
        block_rows, heads_here, HD
    )
    key_pos = jnp.arange(block_rows, dtype=jnp.int32)
    updated = []
    for carry_state, (group_rows, group_pos) in zip(start_states, groups_list):

        def visit_block(kept_state, group_rows=group_rows, group_pos=group_pos):
            return fold_block(
                kept_state, group_rows, group_pos, key_rows, value_rows, key_pos, score_scale
            )

        updated.append(visit_block(carry_state))
    states = tuple(updated)
    self_out = finish_state(states[0])
    id_pairs = neighbour_ids[0].reshape(-1, 2)
    shard_of = id_pairs[:, 0]
    block_of = id_pairs[:, 1]
    spans_here = neighbour_ids.shape[1]
    every_shard = lax.all_gather(database, "dp", axis=0, tiled=True)
    fetched = jnp.stack([every_shard[shard_of, 0, block_of], every_shard[shard_of, 1, block_of]])
    neighbour_rows = NEIGH * RETR
    grouped = fetched.reshape(2, spans_here, neighbour_rows, heads_here, HD)
    previous = passed_along(grouped[:, spans_here - 1], "seq", 1)
    extended = jnp.concatenate([previous[:, None], grouped], axis=1)
    padded = jnp.concatenate(
        [
            jnp.zeros((1, feat_here), jnp.bfloat16),
            cross_queries[0],
            jnp.zeros((SPAN - 1, feat_here), jnp.bfloat16),
        ],
        axis=0,
    )
    padded = padded.reshape(spans_here + 1, SPAN, heads_here, HD)
    scores = (
        jnp.einsum("gqhe,gkhe->ghqk", padded, extended[0], preferred_element_type=jnp.float32)
        * score_scale
    )
    row_max = jnp.max(scores, axis=3, keepdims=True)
    weights = jnp.exp(scores - row_max)
    totals = jnp.sum(weights, axis=3)
    summed_cross = jnp.einsum(
        "ghqk,gkhe->gqhe",
        weights.astype(jnp.bfloat16),
        extended[1],
        preferred_element_type=jnp.float32,
    )
    cross_out = summed_cross / jnp.transpose(totals, (0, 2, 1))[:, :, :, None]
    valid = ((jnp.arange(spans_here + 1) > 0) | (seq_index > 0)).astype(jnp.float32)
    cross_out = cross_out * valid[:, None, None, None]
    cross_out = cross_out.reshape((spans_here + 1) * SPAN, feat_here)[1 : 1 + row_count]
    attended = (self_out + cross_out).astype(jnp.bfloat16)
    own_sums = lax.psum_scatter(
        lax.dot_general(
            out_weight, attended, (((0,), (1,)), ((), ())), preferred_element_type=jnp.float32
        ).astype(jnp.bfloat16),
        "mp",
        scatter_dimension=0,
        tiled=True,
    )
    return jnp.transpose(own_sums)[None]

NEG = -1e30
LOG2E = 1.4426950408889634
PAIR = 2 * HD
PIECE = PAIR + 16
TILE = 512
MESH = pl.DeviceIdType.MESH


def nt_dot(a, b):
    return lax.dot_general(a, b, (((1,), (1,)), ((), ())), preferred_element_type=jnp.float32)


def nn_dot(a, b):
    return jnp.dot(a, b, preferred_element_type=jnp.float32)


def pack_piece(parts):
    row = lax.broadcasted_iota(jnp.int32, (16, HD), 0)
    stats = jnp.zeros((16, HD), jnp.float32)
    for index, (_, lse) in enumerate(parts):
        rest = lse
        for term in range(3):
            rounded = rest.astype(jnp.bfloat16).astype(jnp.float32)
            stats = jnp.where(row == 3 * index + term, rounded, stats)
            rest = rest - rounded
    return jnp.concatenate(
        [parts[0][0].astype(jnp.bfloat16), parts[1][0].astype(jnp.bfloat16), stats.astype(jnp.bfloat16)],
        axis=0,
    )


def by_head(q):
    blank = jnp.zeros((q.shape[0], HD), q.dtype)
    return jnp.concatenate(
        [
            jnp.concatenate([q[:, :HD], blank], axis=1),
            jnp.concatenate([blank, q[:, HD:]], axis=1),
        ],
        axis=0,
    )


def weigh(scores, scale):
    top = jnp.max(scores, axis=0, keepdims=True)
    weights = jnp.exp2((scores - top) * scale)
    total = jnp.sum(weights, axis=0, keepdims=True)
    return weights.astype(jnp.bfloat16), top, total


def attend_pair(q, k, vt, scale, allowed=None):
    scores = nt_dot(k, by_head(q))
    if allowed is not None:
        scores = jnp.where(allowed, scores, NEG)
    low, top, total = weigh(scores, scale)
    lse = top * scale + jnp.log2(total)
    inverse = 1.0 / total
    rows = q.shape[0]
    parts = []
    for h in range(2):
        lanes = slice(h * rows, (h + 1) * rows)
        summed = nn_dot(vt[h * HD : (h + 1) * HD], low[:, lanes]) * inverse[:, lanes]
        parts.append((summed, lse[:, lanes]))
    return pack_piece(parts)


def cross_pair(q, keys, vts, owned, in_first, in_last, scale):
    both = by_head(q)
    s0, s1, s2 = [nt_dot(k, both) for k in keys]
    scores = jnp.where(in_first, s0, jnp.where(in_last, s2, s1))
    scores = jnp.where(owned, scores, NEG)
    low, top, total = weigh(scores, scale)
    some = top > 0.5 * NEG
    lse = jnp.where(some, top * scale + jnp.log2(total), NEG)
    inverse = jnp.where(some, 1.0 / total, 0.0)
    rows = q.shape[0]
    parts = []
    for h in range(2):
        lanes = slice(h * rows, (h + 1) * rows)
        o0, o1, o2 = [nn_dot(vt[h * HD : (h + 1) * HD], low[:, lanes]) for vt in vts]
        summed = jnp.where(in_first[:, lanes], o0, jnp.where(in_last[:, lanes], o2, o1))
        parts.append((summed * inverse[:, lanes], lse[:, lanes]))
    return pack_piece(parts)


def merge_pieces(pieces, h):
    lses = []
    for piece in pieces:
        stats = piece[PAIR:, :].astype(jnp.float32)
        lses.append(stats[3 * h : 3 * h + 1] + stats[3 * h + 1 : 3 * h + 2] + stats[3 * h + 2 : 3 * h + 3])
    top = functools.reduce(jnp.maximum, lses)
    shares = [jnp.exp2(lse - top) for lse in lses]
    total = functools.reduce(jnp.add, shares)
    summed = 0.0
    for piece, share in zip(pieces, shares):
        summed = summed + piece[h * HD : (h + 1) * HD, :].astype(jnp.float32) * (share / total)
    return summed


def layer_kernel(
    q_hbm, k_hbm, v_hbm, cq_hbm, ids, db_hbm, w_hbm, out,
    q, k, v, cq, vt, dvt, db, w, k0, vt0, qin, cqin, sp, stx, cp, ctx, att, ptx, prx, ids_tx, ids_rx, ids_s,
    in_sem, db_sem, w_sem, ids_sem, kv_ss, kv_rs, q_ss, q_rs, cq_ss, cq_rs, sp_ss, sp_rs, cp_ss, cp_rs,
    i1_ss, i1_rs, i2_ss, i2_rs, p_ss, p_rs,
):
    d = lax.axis_index("dp")
    s = lax.axis_index("seq")
    m = lax.axis_index("mp")
    dps = cqin.shape[0]
    chunks = cqin.shape[1]
    rows = q.shape[0]
    half = out.shape[1]
    tiles = half // TILE
    scale = LOG2E / math.sqrt(HD)
    other = 1 - m

    def cols_of(c):
        return pl.ds(pl.multiple_of(c * PAIR, PAIR), PAIR)

    def remote(src, dst, ss, rs, **where):
        return pltpu.make_async_remote_copy(
            src_ref=src, dst_ref=dst, send_sem=ss, recv_sem=rs, device_id=where, device_id_type=MESH
        )

    in_copies = [
        pltpu.make_async_copy(src, dst, in_sem.at[i])
        for i, (src, dst) in enumerate(((v_hbm, v), (cq_hbm, cq), (q_hbm, q), (k_hbm, k)))
    ]
    for copy in in_copies:
        copy.start()
    db_copy = pltpu.make_async_copy(db_hbm, db, db_sem)
    db_copy.start()
    w_copies = [
        pltpu.make_async_copy(
            w_hbm.at[:, pl.ds(pl.multiple_of(side * half, TILE), half)], w.at[i], w_sem.at[i]
        )
        for i, side in enumerate((other, m))
    ]

    barrier = pltpu.get_barrier_semaphore()
    for j in range(1, dps):
        pl.semaphore_signal(barrier, inc=1, device_id={"dp": lax.rem(d + j, dps)}, device_id_type=MESH)
    for j in range(1, 4):
        pl.semaphore_signal(barrier, inc=1, device_id={"seq": lax.rem(s + j, 4)}, device_id_type=MESH)
    pl.semaphore_signal(barrier, inc=1, device_id={"mp": other}, device_id_type=MESH)

    def turned(block):
        return jnp.concatenate([block[:, :HD].T, block[:, HD:].T], axis=0)

    in_copies[0].wait()

    @pl.loop(0, chunks)
    def _(c):
        vt[c] = turned(v[:, cols_of(c)])

    pl.semaphore_wait(barrier, dps + 3)

    def id_hop():
        return remote(ids, ids_tx.at[1], i1_ss, i1_rs, seq=lax.rem(s + 1, 4))

    def kv_hop(c, which):
        src, dst = ((k_hbm.at[:, cols_of(c)], k0), (vt.at[c], vt0))[which]
        return remote(src, dst.at[c], kv_ss.at[c, which], kv_rs.at[c, which], seq=1)

    def q_hop(c, dest):
        slot = jnp.maximum(s - 2, 0)
        return remote(q_hbm.at[:, cols_of(c)], qin.at[slot, c], q_ss.at[dest - 1, c], q_rs.at[slot, c], seq=dest)

    def q_arrived(c, slot):
        remote(q_hbm.at[:, cols_of(c)], qin.at[slot, c], q_ss.at[0, c], q_rs.at[slot, c], seq=1).wait_recv()

    def cq_hop(c, j):
        return remote(
            cq_hbm.at[:, cols_of(c)], cqin.at[j, c], cq_ss.at[j, c], cq_rs.at[j, c], dp=lax.rem(d + j, dps)
        )

    def sp_hop(c, slot, dest, place):
        return remote(stx.at[slot, c], sp.at[place, c], sp_ss.at[slot, c], sp_rs.at[place, c], seq=dest)

    def cp_hop(c, j):
        return remote(
            ctx.at[j, c], cp.at[j, c], cp_ss.at[j, c], cp_rs.at[j, c], dp=lax.rem(d - j + dps, dps)
        )

    def id_share(j):
        return remote(ids_tx, ids_rx.at[j], i2_ss.at[j], i2_rs.at[j], dp=lax.rem(d + j, dps))

    def p_hop(t):
        return remote(ptx.at[t], prx.at[t], p_ss.at[t], p_rs.at[t], mp=other)

    @pl.when(s < 3)
    def _():
        id_hop().start()

    @pl.loop(0, chunks)
    def _(c):
        @pl.when(s == 0)
        def _():
            kv_hop(c, 0).start()
            kv_hop(c, 1).start()

        @pl.when(s >= 2)
        def _():
            q_hop(c, 1).start()

        @pl.when(s == 3)
        def _():
            q_hop(c, 2).start()

        @pl.loop(1, dps)
        def _(j):
            cq_hop(c, j).start()

    for copy in w_copies:
        copy.start()

    ids_tx[0] = ids[...]

    @pl.when(s == 0)
    def _():
        ids_tx[1] = jnp.zeros_like(ids)

    @pl.when(s > 0)
    def _():
        id_hop().wait_recv()

    for j in range(1, dps):
        id_share(j).start()
    ids_rx[0] = ids_tx[...]

    neutral = jnp.concatenate(
        [jnp.zeros((PAIR, HD), jnp.bfloat16), jnp.full((16, HD), NEG, jnp.bfloat16)], axis=0
    )
    key_at = lax.broadcasted_iota(jnp.int32, (rows, 2 * rows), 0)
    query_at = lax.rem(lax.broadcasted_iota(jnp.int32, (rows, 2 * rows), 1), rows)
    causal = key_at <= query_at
    for copy in in_copies[1:]:
        copy.wait()

    @pl.loop(0, chunks)
    def _(c):
        cols = cols_of(c)
        sp[0, c] = attend_pair(q[:, cols], k[:, cols], vt[c], scale, causal)

        @pl.when(s < 1)
        def _():
            sp[1, c] = neutral

        @pl.when(s < 3)
        def _():
            sp[2, c] = neutral

    for j in range(1, dps):
        id_share(j).wait_recv()
    ids_copy = pltpu.make_async_copy(ids_rx, ids_s, ids_sem)
    ids_copy.start()
    ids_copy.wait()
    db_copy.wait()

    lane = lax.rem(lax.broadcasted_iota(jnp.int32, (1, 2 * rows), 1), rows)
    in_first = lane < SPAN - 1
    in_last = lane == 2 * SPAN - 1
    live = jnp.logical_or(lane >= SPAN - 1, s > 0)

    @pl.loop(0, chunks)
    def _(c):
        cols = cols_of(c)

        @pl.when(s == 1)
        def _():
            kv_hop(c, 0).wait_recv()
            kv_hop(c, 1).wait_recv()
            sp[1, c] = attend_pair(q[:, cols], k0[c], vt0[c], scale)

            @pl.loop(0, 2)
            def _(slot):
                q_arrived(c, slot)
                both_k = jnp.concatenate([k0[c], k[:, cols]], axis=0)
                both_v = jnp.concatenate([vt0[c], vt[c]], axis=1)
                stx[slot, c] = attend_pair(qin[slot, c], both_k, both_v, scale)
                sp_hop(c, slot, 2 + slot, 1).start()

        @pl.when(s == 2)
        def _():
            q_arrived(c, 1)
            stx[1, c] = attend_pair(qin[1, c], k[:, cols], vt[c], scale)
            sp_hop(c, 1, 3, 2).start()

        @pl.loop(0, db.shape[1])
        def _(b):
            dvt[b] = turned(db[1, b, :, cols])

        def cross_part(j):
            keys, vts, shards = [], [], []
            for which, span in ((1, 1), (0, 0), (0, 1)):
                blocks = [ids_s[j, which, 0, span * 4 + n * 2 + 1] for n in range(NEIGH)]
                shards.append([ids_s[j, which, 0, span * 4 + n * 2] for n in range(NEIGH)])
                keys.append(jnp.concatenate([db[0, b, :, cols] for b in blocks], axis=0))
                vts.append(jnp.concatenate([dvt[b] for b in blocks], axis=1))
            owned = []
            for n in range(NEIGH):
                shard = jnp.where(in_first, shards[0][n], jnp.where(in_last, shards[2][n], shards[1][n]))
                row = jnp.where(jnp.logical_and(shard == d, live), 1, 0)
                owned.append(jnp.broadcast_to(row, (RETR, 2 * rows)))
            owned = jnp.concatenate(owned, axis=0) > 0
            asked = cq[:, cols] if j == 0 else cqin[j, c]
            return cross_pair(asked, keys, vts, owned, in_first, in_last, scale)

        for group in range(1, dps + 1, 2):
            turns = [turn % dps for turn in range(group, min(group + 2, dps + 1))]
            for j in turns:
                if j > 0:
                    cq_hop(c, j).wait_recv()
            found = [cross_part(j) for j in turns]
            for j, piece in zip(turns, found):
                ctx[j, c] = piece
            for j in turns:
                if j > 0:
                    cp_hop(c, j).start()

    @pl.loop(0, chunks)
    def _(c):
        @pl.when(s >= 2)
        def _():
            sp_hop(c, 0, 2, 1).wait_recv()

        @pl.when(s == 3)
        def _():
            sp_hop(c, 0, 3, 2).wait_recv()

        for j in range(1, dps):
            cp_hop(c, j).wait_recv()
        self_pieces = [sp[i, c] for i in range(3)]
        cross_pieces = [ctx[0, c]] + [cp[j, c] for j in range(1, dps)]
        for h in range(2):
            both = merge_pieces(self_pieces, h) + merge_pieces(cross_pieces, h)
            att[:, pl.ds(pl.multiple_of(c * PAIR + h * HD, HD), HD)] = both.T.astype(jnp.bfloat16)

    def tile_cols(t):
        return pl.ds(pl.multiple_of(t * TILE, TILE), TILE)

    w_copies[0].wait()

    @pl.loop(0, tiles)
    def _(t):
        ptx[t] = jnp.dot(
            att[...], w[0, :, tile_cols(t)], preferred_element_type=jnp.float32
        ).astype(jnp.bfloat16)
        p_hop(t).start()

    w_copies[1].wait()

    @pl.loop(0, tiles)
    def _(t):
        own = jnp.dot(att[...], w[1, :, tile_cols(t)], preferred_element_type=jnp.float32)
        p_hop(t).wait_recv()
        out[:, tile_cols(t)] = (own + prx[t].astype(jnp.float32)).astype(jnp.bfloat16)

    @pl.when(s < 3)
    def _():
        id_hop().wait_send()

    for j in range(1, dps):
        id_share(j).wait_send()

    @pl.loop(0, chunks)
    def _(c):
        @pl.when(s == 0)
        def _():
            kv_hop(c, 0).wait_send()
            kv_hop(c, 1).wait_send()

        @pl.when(s >= 2)
        def _():
            q_hop(c, 1).wait_send()

        @pl.when(s == 3)
        def _():
            q_hop(c, 2).wait_send()

        @pl.when(s == 1)
        def _():
            sp_hop(c, 0, 2, 1).wait_send()
            sp_hop(c, 1, 3, 1).wait_send()

        @pl.when(s == 2)
        def _():
            sp_hop(c, 1, 3, 2).wait_send()

        @pl.loop(1, dps)
        def _(j):
            cq_hop(c, j).wait_send()
            cp_hop(c, j).wait_send()

    @pl.loop(0, tiles)
    def _(t):
        p_hop(t).wait_send()


def fused_device(queries, keys, values, cross_queries, neighbour_ids, database, out_weight):
    rows, feat = queries.shape[1:]
    dps = lax.axis_size("dp")
    chunks = feat // PAIR
    width = out_weight.shape[1]
    half = width // 2
    tiles = half // TILE
    ids = neighbour_ids.reshape(1, -1)
    ids = jnp.pad(ids, ((0, 7), (0, 128 - ids.shape[1])))
    bf16 = jnp.bfloat16
    dma = pltpu.SemaphoreType.DMA
    vmem = pl.BlockSpec(memory_space=pltpu.VMEM)
    anywhere = pl.BlockSpec(memory_space=pl.ANY)
    scratch = [
        pltpu.VMEM((rows, feat), bf16),
        pltpu.VMEM((rows, feat), bf16),
        pltpu.VMEM((rows, feat), bf16),
        pltpu.VMEM((rows, feat), bf16),
        pltpu.VMEM((chunks, PAIR, rows), bf16),
        pltpu.VMEM((database.shape[2], PAIR, RETR), bf16),
        pltpu.VMEM(database.shape[1:], bf16),
        pltpu.VMEM((2, feat, half), bf16),
        pltpu.VMEM((chunks, rows, PAIR), bf16),
        pltpu.VMEM((chunks, PAIR, rows), bf16),
        pltpu.VMEM((2, chunks, rows, PAIR), bf16),
        pltpu.VMEM((dps, chunks, rows, PAIR), bf16),
        pltpu.VMEM((3, chunks, PIECE, rows), bf16),
        pltpu.VMEM((2, chunks, PIECE, rows), bf16),
        pltpu.VMEM((dps, chunks, PIECE, rows), bf16),
        pltpu.VMEM((dps, chunks, PIECE, rows), bf16),
        pltpu.VMEM((rows, feat), bf16),
        pltpu.VMEM((tiles, rows, TILE), bf16),
        pltpu.VMEM((tiles, rows, TILE), bf16),
        pltpu.VMEM((2, 8, 128), jnp.int32),
        pltpu.VMEM((dps, 2, 8, 128), jnp.int32),
        pltpu.SMEM((dps, 2, 8, 128), jnp.int32),
        dma((4,)), dma, dma((2,)), dma,
        dma((chunks, 2)), dma((chunks, 2)),
        dma((2, chunks)), dma((2, chunks)),
        dma((dps, chunks)), dma((dps, chunks)),
        dma((2, chunks)), dma((3, chunks)),
        dma((dps, chunks)), dma((dps, chunks)),
        dma, dma, dma((dps,)), dma((dps,)),
        dma((tiles,)), dma((tiles,)),
    ]
    flops = 2 * rows * feat * width + 2 * 2 * rows * feat * (8 * rows + dps * 6 * RETR)
    result = pl.pallas_call(
        layer_kernel,
        out_shape=jax.ShapeDtypeStruct((rows, half), bf16),
        in_specs=[anywhere] * 4 + [vmem] + [anywhere] * 2,
        out_specs=vmem,
        scratch_shapes=scratch,
        compiler_params=pltpu.CompilerParams(
            collective_id=0, has_side_effects=True, vmem_limit_bytes=60 * 1024 * 1024
        ),
        cost_estimate=pl.CostEstimate(
            flops=flops, bytes_accessed=2 * (feat * width + database.size), transcendentals=0
        ),
    )(queries[0], keys[0], values[0], cross_queries[0], ids, database[0], out_weight)
    return result[None]


def solution(mesh):
    placed = (
        P("dp", "seq", "mp"),
        P("dp", "seq", "mp"),
        P("dp", "seq", "mp"),
        P("dp", "seq", "mp"),
        P("dp", "seq", None, None),
        P("dp", None, None, None, "mp"),
        P("mp", None),
    )
    fits = mesh.shape["seq"] == 4 and mesh.shape["mp"] == 2
    return jax.shard_map(
        fused_device if fits else per_device,
        mesh=mesh,
        in_specs=placed,
        out_specs=P("dp", "seq", "mp"),
        check_vma=False,
    )
```

```python
import functools
import math

import jax
import jax.numpy as jnp
from jax import lax
from jax.experimental import pallas as pl
from jax.experimental.pallas import tpu as pltpu
from jax.sharding import PartitionSpec as P

HD = 128
SPAN = 64
NEIGH = 2
RETR = 128


masked_score = -1e30


def passed_along(value, axis, steps):
    count = lax.axis_size(axis)
    leading, last = (max(0, -steps), min(count, count - steps))
    return lax.ppermute(value, axis, [(source, source + steps) for source in range(leading, last)])


def fold_block(carry_state, query_rows, query_pos, key_rows, value_rows, key_pos, score_scale):
    summed, running_max, totals = carry_state
    scores = (
        jnp.einsum("qhe,khe->hqk", query_rows, key_rows, preferred_element_type=jnp.float32)
        * score_scale
    )
    allowed = (key_pos[None, :] <= query_pos[:, None])[None]
    scores = jnp.where(allowed, scores, masked_score)
    new_max = jnp.maximum(running_max, jnp.max(scores, axis=2))
    weights = jnp.where(allowed, jnp.exp(scores - new_max[:, :, None]), 0.0)
    totals = jnp.sum(weights, axis=2)
    summed = jnp.einsum(
        "hqk,khe->hqe", weights.astype(jnp.bfloat16), value_rows, preferred_element_type=jnp.float32
    )
    return (summed, new_max, totals)


def empty_state(heads_here, row_total):
    return (
        jnp.zeros((heads_here, row_total, HD), jnp.float32),
        jnp.full((heads_here, row_total), masked_score, jnp.float32),
        jnp.zeros((heads_here, row_total), jnp.float32),
    )


def finish_state(carry_state):
    summed, running_max, totals = carry_state
    normed = summed / totals[:, :, None]
    return jnp.transpose(normed, (1, 0, 2)).reshape(
        normed.shape[1], normed.shape[0] * normed.shape[2]
    )


def per_device(queries, keys, values, cross_queries, neighbour_ids, database, out_weight):
    row_count = queries.shape[1]
    feat_here = queries.shape[2]
    heads_here = feat_here // HD
    score_scale = 1.0 / math.sqrt(HD)
    seq_index = lax.axis_index("seq")
    own_first = seq_index * row_count
    own_pos = own_first + jnp.arange(row_count, dtype=jnp.int32)
    query_rows = queries[0].reshape(row_count, heads_here, HD)
    groups_list = [(query_rows, own_pos)]
    start_states = tuple(
        (empty_state(heads_here, group_pos.shape[0]) for group_rows, group_pos in groups_list)
    )
    key_block = lax.all_gather(keys, "seq", axis=1, tiled=True)[0]
    block_rows = key_block.shape[0]
    key_rows = key_block.reshape(block_rows, heads_here, HD)
    value_rows = lax.all_gather(values, "seq", axis=1, tiled=True)[0].reshape(
        block_rows, heads_here, HD
    )
    key_pos = jnp.arange(block_rows, dtype=jnp.int32)
    updated = []
    for carry_state, (group_rows, group_pos) in zip(start_states, groups_list):

        def visit_block(kept_state, group_rows=group_rows, group_pos=group_pos):
            return fold_block(
                kept_state, group_rows, group_pos, key_rows, value_rows, key_pos, score_scale
            )

        updated.append(visit_block(carry_state))
    states = tuple(updated)
    self_out = finish_state(states[0])
    id_pairs = neighbour_ids[0].reshape(-1, 2)
    shard_of = id_pairs[:, 0]
    block_of = id_pairs[:, 1]
    spans_here = neighbour_ids.shape[1]
    every_shard = lax.all_gather(database, "dp", axis=0, tiled=True)
    fetched = jnp.stack([every_shard[shard_of, 0, block_of], every_shard[shard_of, 1, block_of]])
    neighbour_rows = NEIGH * RETR
    grouped = fetched.reshape(2, spans_here, neighbour_rows, heads_here, HD)
    previous = passed_along(grouped[:, spans_here - 1], "seq", 1)
    extended = jnp.concatenate([previous[:, None], grouped], axis=1)
    padded = jnp.concatenate(
        [
            jnp.zeros((1, feat_here), jnp.bfloat16),
            cross_queries[0],
            jnp.zeros((SPAN - 1, feat_here), jnp.bfloat16),
        ],
        axis=0,
    )
    padded = padded.reshape(spans_here + 1, SPAN, heads_here, HD)
    scores = (
        jnp.einsum("gqhe,gkhe->ghqk", padded, extended[0], preferred_element_type=jnp.float32)
        * score_scale
    )
    row_max = jnp.max(scores, axis=3, keepdims=True)
    weights = jnp.exp(scores - row_max)
    totals = jnp.sum(weights, axis=3)
    summed_cross = jnp.einsum(
        "ghqk,gkhe->gqhe",
        weights.astype(jnp.bfloat16),
        extended[1],
        preferred_element_type=jnp.float32,
    )
    cross_out = summed_cross / jnp.transpose(totals, (0, 2, 1))[:, :, :, None]
    valid = ((jnp.arange(spans_here + 1) > 0) | (seq_index > 0)).astype(jnp.float32)
    cross_out = cross_out * valid[:, None, None, None]
    cross_out = cross_out.reshape((spans_here + 1) * SPAN, feat_here)[1 : 1 + row_count]
    attended = (self_out + cross_out).astype(jnp.bfloat16)
    own_sums = lax.psum_scatter(
        lax.dot_general(
            out_weight, attended, (((0,), (1,)), ((), ())), preferred_element_type=jnp.float32
        ).astype(jnp.bfloat16),
        "mp",
        scatter_dimension=0,
        tiled=True,
    )
    return jnp.transpose(own_sums)[None]

NEG = -1e30
LOG2E = 1.4426950408889634
PAIR = 2 * HD
PIECE = PAIR + 16
TILE = 512
MESH = pl.DeviceIdType.MESH


def nt_dot(a, b):
    return lax.dot_general(a, b, (((1,), (1,)), ((), ())), preferred_element_type=jnp.float32)


def nn_dot(a, b):
    return jnp.dot(a, b, preferred_element_type=jnp.float32)


def pack_piece(parts):
    row = lax.broadcasted_iota(jnp.int32, (16, HD), 0)
    stats = jnp.zeros((16, HD), jnp.float32)
    for index, (_, lse) in enumerate(parts):
        rest = lse
        for term in range(3):
            rounded = rest.astype(jnp.bfloat16).astype(jnp.float32)
            stats = jnp.where(row == 3 * index + term, rounded, stats)
            rest = rest - rounded
    return jnp.concatenate(
        [parts[0][0].astype(jnp.bfloat16), parts[1][0].astype(jnp.bfloat16), stats.astype(jnp.bfloat16)],
        axis=0,
    )


def by_head(q):
    blank = jnp.zeros((q.shape[0], HD), q.dtype)
    return jnp.concatenate(
        [
            jnp.concatenate([q[:, :HD], blank], axis=1),
            jnp.concatenate([blank, q[:, HD:]], axis=1),
        ],
        axis=0,
    )


def weigh(scores, scale):
    top = jnp.max(scores, axis=0, keepdims=True)
    weights = jnp.exp2((scores - top) * scale)
    total = jnp.sum(weights, axis=0, keepdims=True)
    return weights.astype(jnp.bfloat16), top, total


def attend_pair(q, k, vt, scale, allowed=None):
    scores = nt_dot(k, by_head(q))
    if allowed is not None:
        scores = jnp.where(allowed, scores, NEG)
    low, top, total = weigh(scores, scale)
    lse = top * scale + jnp.log2(total)
    inverse = 1.0 / total
    rows = q.shape[0]
    parts = []
    for h in range(2):
        lanes = slice(h * rows, (h + 1) * rows)
        summed = nn_dot(vt[h * HD : (h + 1) * HD], low[:, lanes]) * inverse[:, lanes]
        parts.append((summed, lse[:, lanes]))
    return pack_piece(parts)


def cross_pair(q, keys, vts, owned, in_first, in_last, scale):
    both = by_head(q)
    s0, s1, s2 = [nt_dot(k, both) for k in keys]
    scores = jnp.where(in_first, s0, jnp.where(in_last, s2, s1))
    scores = jnp.where(owned, scores, NEG)
    low, top, total = weigh(scores, scale)
    some = top > 0.5 * NEG
    lse = jnp.where(some, top * scale + jnp.log2(total), NEG)
    inverse = jnp.where(some, 1.0 / total, 0.0)
    rows = q.shape[0]
    parts = []
    for h in range(2):
        lanes = slice(h * rows, (h + 1) * rows)
        o0, o1, o2 = [nn_dot(vt[h * HD : (h + 1) * HD], low[:, lanes]) for vt in vts]
        summed = jnp.where(in_first[:, lanes], o0, jnp.where(in_last[:, lanes], o2, o1))
        parts.append((summed * inverse[:, lanes], lse[:, lanes]))
    return pack_piece(parts)


def merge_pieces(pieces, h):
    lses = []
    for piece in pieces:
        stats = piece[PAIR:, :].astype(jnp.float32)
        lses.append(stats[3 * h : 3 * h + 1] + stats[3 * h + 1 : 3 * h + 2] + stats[3 * h + 2 : 3 * h + 3])
    top = functools.reduce(jnp.maximum, lses)
    shares = [jnp.exp2(lse - top) for lse in lses]
    total = functools.reduce(jnp.add, shares)
    inverse = 1.0 / total
    summed = 0.0
    for piece, share in zip(pieces, shares):
        summed = summed + piece[h * HD : (h + 1) * HD, :].astype(jnp.float32) * (share * inverse)
    return summed, jnp.maximum(top + jnp.log2(total), NEG)


def layer_kernel(
    q_hbm, k_hbm, v_hbm, cq_hbm, ids, db_hbm, w_hbm, out,
    q, k, v, cq, vt, dvt, db, w, k0, vt0, qin, cqin, sp, stx, cp, ctx, att, ptx, prx, ids_tx, ids_rx, ids_s,
    in_sem, db_sem, w_sem, ids_sem, kv_ss, kv_rs, q_ss, q_rs, cq_ss, cq_rs, sp_ss, sp_rs, cp_ss, cp_rs,
    i1_ss, i1_rs, i2_ss, i2_rs, p_ss, p_rs,
):
    d = lax.axis_index("dp")
    s = lax.axis_index("seq")
    m = lax.axis_index("mp")
    dps = cqin.shape[0]
    chunks = cqin.shape[1]
    rows = q.shape[0]
    half = out.shape[1]
    tiles = half // TILE
    scale = LOG2E / math.sqrt(HD)
    other = 1 - m

    def cols_of(c):
        return pl.ds(pl.multiple_of(c * PAIR, PAIR), PAIR)

    def remote(src, dst, ss, rs, **where):
        return pltpu.make_async_remote_copy(
            src_ref=src, dst_ref=dst, send_sem=ss, recv_sem=rs, device_id=where, device_id_type=MESH
        )

    in_copies = [
        pltpu.make_async_copy(src, dst, in_sem.at[i])
        for i, (src, dst) in enumerate(((v_hbm, v), (cq_hbm, cq), (q_hbm, q), (k_hbm, k)))
    ]
    for copy in in_copies:
        copy.start()
    db_copy = pltpu.make_async_copy(db_hbm, db, db_sem)
    db_copy.start()
    w_copies = [
        pltpu.make_async_copy(
            w_hbm.at[:, pl.ds(pl.multiple_of(side * half, TILE), half)], w.at[i], w_sem.at[i]
        )
        for i, side in enumerate((other, m))
    ]

    def peer(j):
        return (d, d + 1 - 2 * lax.rem(d, 2), lax.rem(d + 2, 4), 3 - d)[j]

    barrier = pltpu.get_barrier_semaphore()
    for j in range(1, dps):
        pl.semaphore_signal(barrier, inc=1, device_id={"dp": peer(j)}, device_id_type=MESH)
    for j in range(1, 4):
        pl.semaphore_signal(barrier, inc=1, device_id={"seq": lax.rem(s + j, 4)}, device_id_type=MESH)
    pl.semaphore_signal(barrier, inc=1, device_id={"mp": other}, device_id_type=MESH)

    def turned(block):
        return jnp.concatenate([block[:, :HD].T, block[:, HD:].T], axis=0)

    in_copies[0].wait()

    @pl.loop(0, chunks)
    def _(c):
        vt[c] = turned(v[:, cols_of(c)])

    pl.semaphore_wait(barrier, dps + 3)

    def id_hop():
        return remote(ids, ids_tx.at[1], i1_ss, i1_rs, seq=lax.rem(s + 1, 4))

    def kv_hop(c, which):
        src, dst = ((k_hbm.at[:, cols_of(c)], k0), (vt.at[c], vt0))[which]
        return remote(src, dst.at[c], kv_ss.at[c, which], kv_rs.at[c, which], seq=1)

    def q_hop(c, dest):
        slot = jnp.maximum(s - 2, 0)
        return remote(q_hbm.at[:, cols_of(c)], qin.at[slot, c], q_ss.at[dest - 1, c], q_rs.at[slot, c], seq=dest)

    def q_arrived(c, slot):
        remote(q_hbm.at[:, cols_of(c)], qin.at[slot, c], q_ss.at[0, c], q_rs.at[slot, c], seq=1).wait_recv()

    def cq_hop(c, j):
        src = cqin.at[2, c] if j == 3 else cq_hbm.at[:, cols_of(c)]
        return remote(src, cqin.at[j, c], cq_ss.at[j, c], cq_rs.at[j, c], dp=peer(1 if j == 3 else j))

    def sp_hop(c, slot, dest, place):
        return remote(stx.at[slot, c], sp.at[place, c], sp_ss.at[slot, c], sp_rs.at[place, c], seq=dest)

    def cp_hop(c, j):
        return remote(
            ctx.at[j, c], cp.at[j, c], cp_ss.at[j, c], cp_rs.at[j, c], dp=peer(1 if j == 3 else j)
        )

    def id_share(j):
        return remote(ids_tx, ids_rx.at[j], i2_ss.at[j], i2_rs.at[j], dp=peer(j))

    def p_hop(t):
        return remote(ptx.at[t], prx.at[t], p_ss.at[t], p_rs.at[t], mp=other)

    @pl.when(s < 3)
    def _():
        id_hop().start()

    @pl.loop(0, chunks)
    def _(c):
        @pl.when(s == 0)
        def _():
            kv_hop(c, 0).start()
            kv_hop(c, 1).start()

        @pl.when(s >= 2)
        def _():
            q_hop(c, 1).start()

        @pl.when(s == 3)
        def _():
            q_hop(c, 2).start()

        cq_hop(c, 2).start()
        cq_hop(c, 1).start()

    for copy in w_copies:
        copy.start()

    ids_tx[0] = ids[...]

    @pl.when(s == 0)
    def _():
        ids_tx[1] = jnp.zeros_like(ids)

    @pl.when(s > 0)
    def _():
        id_hop().wait_recv()

    for j in range(1, dps):
        id_share(j).start()
    ids_rx[0] = ids_tx[...]

    neutral = jnp.concatenate(
        [jnp.zeros((PAIR, HD), jnp.bfloat16), jnp.full((16, HD), NEG, jnp.bfloat16)], axis=0
    )
    key_at = lax.broadcasted_iota(jnp.int32, (rows, 2 * rows), 0)
    query_at = lax.rem(lax.broadcasted_iota(jnp.int32, (rows, 2 * rows), 1), rows)
    causal = key_at <= query_at
    for copy in in_copies[1:]:
        copy.wait()

    @pl.loop(0, chunks)
    def _(c):
        cols = cols_of(c)
        sp[0, c] = attend_pair(q[:, cols], k[:, cols], vt[c], scale, causal)

        @pl.when(s < 1)
        def _():
            sp[1, c] = neutral

        @pl.when(s < 3)
        def _():
            sp[2, c] = neutral

    for j in range(1, dps):
        id_share(j).wait_recv()
    ids_copy = pltpu.make_async_copy(ids_rx, ids_s, ids_sem)
    ids_copy.start()
    ids_copy.wait()
    db_copy.wait()

    lane = lax.rem(lax.broadcasted_iota(jnp.int32, (1, 2 * rows), 1), rows)
    in_first = lane < SPAN - 1
    in_last = lane == 2 * SPAN - 1
    live = jnp.logical_or(lane >= SPAN - 1, s > 0)

    @pl.loop(0, chunks)
    def _(c):
        cols = cols_of(c)
        cq_hop(c, 2).wait_recv()
        cq_hop(c, 3).start()

        @pl.when(s == 1)
        def _():
            kv_hop(c, 0).wait_recv()
            kv_hop(c, 1).wait_recv()
            sp[1, c] = attend_pair(q[:, cols], k0[c], vt0[c], scale)

            @pl.loop(0, 2)
            def _(slot):
                q_arrived(c, slot)
                both_k = jnp.concatenate([k0[c], k[:, cols]], axis=0)
                both_v = jnp.concatenate([vt0[c], vt[c]], axis=1)
                stx[slot, c] = attend_pair(qin[slot, c], both_k, both_v, scale)
                sp_hop(c, slot, 2 + slot, 1).start()

        @pl.when(s == 2)
        def _():
            q_arrived(c, 1)
            stx[1, c] = attend_pair(qin[1, c], k[:, cols], vt[c], scale)
            sp_hop(c, 1, 3, 2).start()

        @pl.loop(0, db.shape[1])
        def _(b):
            dvt[b] = turned(db[1, b, :, cols])

        def cross_part(j):
            keys, vts, shards = [], [], []
            for which, span in ((1, 1), (0, 0), (0, 1)):
                blocks = [ids_s[j, which, span, n, 1] for n in range(NEIGH)]
                shards.append([ids_s[j, which, span, n, 0] for n in range(NEIGH)])
                keys.append(jnp.concatenate([db[0, b, :, cols] for b in blocks], axis=0))
                vts.append(jnp.concatenate([dvt[b] for b in blocks], axis=1))
            owned = []
            for n in range(NEIGH):
                shard = jnp.where(in_first, shards[0][n], jnp.where(in_last, shards[2][n], shards[1][n]))
                row = jnp.where(jnp.logical_and(shard == d, live), 1, 0)
                owned.append(jnp.broadcast_to(row, (RETR, 2 * rows)))
            owned = jnp.concatenate(owned, axis=0) > 0
            asked = cq[:, cols] if j == 0 else cqin[j, c]
            return cross_pair(asked, keys, vts, owned, in_first, in_last, scale)

        cq_hop(c, 3).wait_recv()
        across, beside = cross_part(2), cross_part(3)
        ctx[3, c] = beside
        cp_hop(c, 3).start()
        cq_hop(c, 1).wait_recv()
        near, own = cross_part(1), cross_part(0)
        ctx[1, c] = near
        ctx[0, c] = own
        cp_hop(c, 1).start()
        cp_hop(c, 3).wait_recv()
        both = [across, cp[3, c]]
        ctx[2, c] = pack_piece([merge_pieces(both, h) for h in range(2)])
        cp_hop(c, 2).start()

    @pl.loop(0, chunks)
    def _(c):
        @pl.when(s >= 2)
        def _():
            sp_hop(c, 0, 2, 1).wait_recv()

        @pl.when(s == 3)
        def _():
            sp_hop(c, 0, 3, 2).wait_recv()

        cp_hop(c, 1).wait_recv()
        cp_hop(c, 2).wait_recv()
        self_pieces = [sp[i, c] for i in range(3)]
        cross_pieces = [ctx[0, c], cp[1, c], cp[2, c]]
        for h in range(2):
            both = merge_pieces(self_pieces, h)[0] + merge_pieces(cross_pieces, h)[0]
            att[:, pl.ds(pl.multiple_of(c * PAIR + h * HD, HD), HD)] = both.T.astype(jnp.bfloat16)

    def tile_cols(t):
        return pl.ds(pl.multiple_of(t * TILE, TILE), TILE)

    w_copies[0].wait()

    @pl.loop(0, tiles)
    def _(t):
        ptx[t] = jnp.dot(
            att[...], w[0, :, tile_cols(t)], preferred_element_type=jnp.float32
        ).astype(jnp.bfloat16)
        p_hop(t).start()

    w_copies[1].wait()

    @pl.loop(0, tiles)
    def _(t):
        own = jnp.dot(att[...], w[1, :, tile_cols(t)], preferred_element_type=jnp.float32)
        p_hop(t).wait_recv()
        out[:, tile_cols(t)] = (own + prx[t].astype(jnp.float32)).astype(jnp.bfloat16)

    @pl.when(s < 3)
    def _():
        id_hop().wait_send()

    for j in range(1, dps):
        id_share(j).wait_send()

    @pl.loop(0, chunks)
    def _(c):
        @pl.when(s == 0)
        def _():
            kv_hop(c, 0).wait_send()
            kv_hop(c, 1).wait_send()

        @pl.when(s >= 2)
        def _():
            q_hop(c, 1).wait_send()

        @pl.when(s == 3)
        def _():
            q_hop(c, 2).wait_send()

        @pl.when(s == 1)
        def _():
            sp_hop(c, 0, 2, 1).wait_send()
            sp_hop(c, 1, 3, 1).wait_send()

        @pl.when(s == 2)
        def _():
            sp_hop(c, 1, 3, 2).wait_send()

        for j in range(1, dps):
            cq_hop(c, j).wait_send()
            cp_hop(c, j).wait_send()

    @pl.loop(0, tiles)
    def _(t):
        p_hop(t).wait_send()


def fused_device(queries, keys, values, cross_queries, neighbour_ids, database, out_weight):
    rows, feat = queries.shape[1:]
    dps = lax.axis_size("dp")
    chunks = feat // PAIR
    width = out_weight.shape[1]
    half = width // 2
    tiles = half // TILE
    ids = neighbour_ids[0]
    bf16 = jnp.bfloat16
    dma = pltpu.SemaphoreType.DMA
    vmem = pl.BlockSpec(memory_space=pltpu.VMEM)
    anywhere = pl.BlockSpec(memory_space=pl.ANY)
    scratch = [
        pltpu.VMEM((rows, feat), bf16),
        pltpu.VMEM((rows, feat), bf16),
        pltpu.VMEM((rows, feat), bf16),
        pltpu.VMEM((rows, feat), bf16),
        pltpu.VMEM((chunks, PAIR, rows), bf16),
        pltpu.VMEM((database.shape[2], PAIR, RETR), bf16),
        pltpu.VMEM(database.shape[1:], bf16),
        pltpu.VMEM((2, feat, half), bf16),
        pltpu.VMEM((chunks, rows, PAIR), bf16),
        pltpu.VMEM((chunks, PAIR, rows), bf16),
        pltpu.VMEM((2, chunks, rows, PAIR), bf16),
        pltpu.VMEM((dps, chunks, rows, PAIR), bf16),
        pltpu.VMEM((3, chunks, PIECE, rows), bf16),
        pltpu.VMEM((2, chunks, PIECE, rows), bf16),
        pltpu.VMEM((dps, chunks, PIECE, rows), bf16),
        pltpu.VMEM((dps, chunks, PIECE, rows), bf16),
        pltpu.VMEM((rows, feat), bf16),
        pltpu.VMEM((tiles, rows, TILE), bf16),
        pltpu.VMEM((tiles, rows, TILE), bf16),
        pltpu.VMEM((2,) + ids.shape, jnp.int32),
        pltpu.VMEM((dps, 2) + ids.shape, jnp.int32),
        pltpu.SMEM((dps, 2) + ids.shape, jnp.int32),
        dma((4,)), dma, dma((2,)), dma,
        dma((chunks, 2)), dma((chunks, 2)),
        dma((2, chunks)), dma((2, chunks)),
        dma((dps, chunks)), dma((dps, chunks)),
        dma((2, chunks)), dma((3, chunks)),
        dma((dps, chunks)), dma((dps, chunks)),
        dma, dma, dma((dps,)), dma((dps,)),
        dma((tiles,)), dma((tiles,)),
    ]
    flops = 2 * rows * feat * width + 2 * 2 * rows * feat * (8 * rows + dps * 6 * RETR)
    result = pl.pallas_call(
        layer_kernel,
        out_shape=jax.ShapeDtypeStruct((rows, half), bf16),
        in_specs=[anywhere] * 4 + [vmem] + [anywhere] * 2,
        out_specs=vmem,
        scratch_shapes=scratch,
        compiler_params=pltpu.CompilerParams(
            collective_id=0, has_side_effects=True, vmem_limit_bytes=60 * 1024 * 1024
        ),
        cost_estimate=pl.CostEstimate(
            flops=flops, bytes_accessed=2 * (feat * width + database.size), transcendentals=0
        ),
    )(queries[0], keys[0], values[0], cross_queries[0], ids, database[0], out_weight)
    return result[None]


def solution(mesh):
    placed = (
        P("dp", "seq", "mp"),
        P("dp", "seq", "mp"),
        P("dp", "seq", "mp"),
        P("dp", "seq", "mp"),
        P("dp", "seq", None, None),
        P("dp", None, None, None, "mp"),
        P("mp", None),
    )
    fits = mesh.shape["seq"] == 4 and mesh.shape["mp"] == 2 and mesh.shape["dp"] == 4
    return jax.shard_map(
        fused_device if fits else per_device,
        mesh=mesh,
        in_specs=placed,
        out_specs=P("dp", "seq", "mp"),
        check_vma=False,
    )
```

```python
import functools
import math

import jax
import jax.numpy as jnp
from jax import lax
from jax.experimental import pallas as pl
from jax.experimental.pallas import tpu as pltpu
from jax.sharding import PartitionSpec as P

HD = 128
SPAN = 64
NEIGH = 2
RETR = 128


masked_score = -1e30


def passed_along(value, axis, steps):
    count = lax.axis_size(axis)
    leading, last = (max(0, -steps), min(count, count - steps))
    return lax.ppermute(value, axis, [(source, source + steps) for source in range(leading, last)])


def fold_block(carry_state, query_rows, query_pos, key_rows, value_rows, key_pos, score_scale):
    summed, running_max, totals = carry_state
    scores = (
        jnp.einsum("qhe,khe->hqk", query_rows, key_rows, preferred_element_type=jnp.float32)
        * score_scale
    )
    allowed = (key_pos[None, :] <= query_pos[:, None])[None]
    scores = jnp.where(allowed, scores, masked_score)
    new_max = jnp.maximum(running_max, jnp.max(scores, axis=2))
    weights = jnp.where(allowed, jnp.exp(scores - new_max[:, :, None]), 0.0)
    totals = jnp.sum(weights, axis=2)
    summed = jnp.einsum(
        "hqk,khe->hqe", weights.astype(jnp.bfloat16), value_rows, preferred_element_type=jnp.float32
    )
    return (summed, new_max, totals)


def empty_state(heads_here, row_total):
    return (
        jnp.zeros((heads_here, row_total, HD), jnp.float32),
        jnp.full((heads_here, row_total), masked_score, jnp.float32),
        jnp.zeros((heads_here, row_total), jnp.float32),
    )


def finish_state(carry_state):
    summed, running_max, totals = carry_state
    normed = summed / totals[:, :, None]
    return jnp.transpose(normed, (1, 0, 2)).reshape(
        normed.shape[1], normed.shape[0] * normed.shape[2]
    )


def per_device(queries, keys, values, cross_queries, neighbour_ids, database, out_weight):
    row_count = queries.shape[1]
    feat_here = queries.shape[2]
    heads_here = feat_here // HD
    score_scale = 1.0 / math.sqrt(HD)
    seq_index = lax.axis_index("seq")
    own_first = seq_index * row_count
    own_pos = own_first + jnp.arange(row_count, dtype=jnp.int32)
    query_rows = queries[0].reshape(row_count, heads_here, HD)
    groups_list = [(query_rows, own_pos)]
    start_states = tuple(
        (empty_state(heads_here, group_pos.shape[0]) for group_rows, group_pos in groups_list)
    )
    key_block = lax.all_gather(keys, "seq", axis=1, tiled=True)[0]
    block_rows = key_block.shape[0]
    key_rows = key_block.reshape(block_rows, heads_here, HD)
    value_rows = lax.all_gather(values, "seq", axis=1, tiled=True)[0].reshape(
        block_rows, heads_here, HD
    )
    key_pos = jnp.arange(block_rows, dtype=jnp.int32)
    updated = []
    for carry_state, (group_rows, group_pos) in zip(start_states, groups_list):

        def visit_block(kept_state, group_rows=group_rows, group_pos=group_pos):
            return fold_block(
                kept_state, group_rows, group_pos, key_rows, value_rows, key_pos, score_scale
            )

        updated.append(visit_block(carry_state))
    states = tuple(updated)
    self_out = finish_state(states[0])
    id_pairs = neighbour_ids[0].reshape(-1, 2)
    shard_of = id_pairs[:, 0]
    block_of = id_pairs[:, 1]
    spans_here = neighbour_ids.shape[1]
    every_shard = lax.all_gather(database, "dp", axis=0, tiled=True)
    fetched = jnp.stack([every_shard[shard_of, 0, block_of], every_shard[shard_of, 1, block_of]])
    neighbour_rows = NEIGH * RETR
    grouped = fetched.reshape(2, spans_here, neighbour_rows, heads_here, HD)
    previous = passed_along(grouped[:, spans_here - 1], "seq", 1)
    extended = jnp.concatenate([previous[:, None], grouped], axis=1)
    padded = jnp.concatenate(
        [
            jnp.zeros((1, feat_here), jnp.bfloat16),
            cross_queries[0],
            jnp.zeros((SPAN - 1, feat_here), jnp.bfloat16),
        ],
        axis=0,
    )
    padded = padded.reshape(spans_here + 1, SPAN, heads_here, HD)
    scores = (
        jnp.einsum("gqhe,gkhe->ghqk", padded, extended[0], preferred_element_type=jnp.float32)
        * score_scale
    )
    row_max = jnp.max(scores, axis=3, keepdims=True)
    weights = jnp.exp(scores - row_max)
    totals = jnp.sum(weights, axis=3)
    summed_cross = jnp.einsum(
        "ghqk,gkhe->gqhe",
        weights.astype(jnp.bfloat16),
        extended[1],
        preferred_element_type=jnp.float32,
    )
    cross_out = summed_cross / jnp.transpose(totals, (0, 2, 1))[:, :, :, None]
    valid = ((jnp.arange(spans_here + 1) > 0) | (seq_index > 0)).astype(jnp.float32)
    cross_out = cross_out * valid[:, None, None, None]
    cross_out = cross_out.reshape((spans_here + 1) * SPAN, feat_here)[1 : 1 + row_count]
    attended = (self_out + cross_out).astype(jnp.bfloat16)
    own_sums = lax.psum_scatter(
        lax.dot_general(
            out_weight, attended, (((0,), (1,)), ((), ())), preferred_element_type=jnp.float32
        ).astype(jnp.bfloat16),
        "mp",
        scatter_dimension=0,
        tiled=True,
    )
    return jnp.transpose(own_sums)[None]

NEG = -1e30
LOG2E = 1.4426950408889634
PAIR = 2 * HD
PIECE = HD + 16
TILE = 512
MESH = pl.DeviceIdType.MESH


def nt_dot(a, b):
    return lax.dot_general(a, b, (((1,), (1,)), ((), ())), preferred_element_type=jnp.float32)


def nn_dot(a, b):
    return jnp.dot(a, b, preferred_element_type=jnp.float32)


def pack_piece(summed, lse):
    row = lax.broadcasted_iota(jnp.int32, (16, summed.shape[1]), 0)
    stats = jnp.zeros(row.shape, jnp.float32)
    rest = lse
    for term in range(3):
        rounded = rest.astype(jnp.bfloat16).astype(jnp.float32)
        stats = jnp.where(row == term, rounded, stats)
        rest = rest - rounded
    return jnp.concatenate([summed.astype(jnp.bfloat16), stats.astype(jnp.bfloat16)], axis=0)


def by_head(q):
    blank = jnp.zeros((q.shape[0], HD), q.dtype)
    return jnp.concatenate(
        [
            jnp.concatenate([q[:, :HD], blank], axis=1),
            jnp.concatenate([blank, q[:, HD:]], axis=1),
        ],
        axis=0,
    )


def weigh(scores, scale):
    top = jnp.max(scores, axis=0, keepdims=True)
    weights = jnp.exp2((scores - top) * scale)
    total = jnp.sum(weights, axis=0, keepdims=True)
    return weights.astype(jnp.bfloat16), top, total


def sum_values(vt, low):
    both = nn_dot(vt, low)
    lane = lax.broadcasted_iota(jnp.int32, (HD, low.shape[1]), 1)
    return jnp.where(lane < low.shape[1] // 2, both[:HD], both[HD:])


def attend_pair(q, k, vt, scale, allowed=None):
    scores = nt_dot(k, by_head(q))
    if allowed is not None:
        scores = jnp.where(allowed, scores, NEG)
    low, top, total = weigh(scores, scale)
    return pack_piece(sum_values(vt, low) * (1.0 / total), top * scale + jnp.log2(total))


def cross_pair(q, keys, vts, owned, first, scale):
    both = by_head(q)
    scores = nt_dot(keys[0], both)
    if len(keys) > 1:
        scores = jnp.where(first, scores, nt_dot(keys[1], both))
    scores = jnp.where(owned, scores, NEG)
    low, top, total = weigh(scores, scale)
    some = top > 0.5 * NEG
    lse = jnp.where(some, top * scale + jnp.log2(total), NEG)
    inverse = jnp.where(some, 1.0 / total, 0.0)
    summed = sum_values(vts[0], low)
    if len(keys) > 1:
        summed = jnp.where(first, summed, sum_values(vts[1], low))
    return pack_piece(summed * inverse, lse)


def merge_pieces(pieces):
    lses = []
    for piece in pieces:
        stats = piece[HD:, :].astype(jnp.float32)
        lses.append(stats[0:1] + stats[1:2] + stats[2:3])
    top = functools.reduce(jnp.maximum, lses)
    shares = [jnp.exp2(lse - top) for lse in lses]
    total = functools.reduce(jnp.add, shares)
    inverse = 1.0 / total
    summed = 0.0
    for piece, share in zip(pieces, shares):
        summed = summed + piece[:HD, :].astype(jnp.float32) * (share * inverse)
    return summed, jnp.maximum(top + jnp.log2(total), NEG)


def layer_kernel(
    q_hbm, k_hbm, v_hbm, cq_hbm, ids, db_hbm, w_hbm, out,
    q, k, v, cq, qh, cqh, vt, dvt, db, w, k0, vt0, qin, cqin, sp, stx, cp, ctx, att, ptx, prx, ids_tx, ids_rx, ids_s,
    in_sem, db_sem, w_sem, ids_sem, kv_ss, kv_rs, q_ss, q_rs, cq_ss, cq_rs, sp_ss, sp_rs, cp_ss, cp_rs,
    i1_ss, i1_rs, i2_ss, i2_rs, p_ss, p_rs,
):
    d = lax.axis_index("dp")
    s = lax.axis_index("seq")
    m = lax.axis_index("mp")
    dps = cqin.shape[0]
    steps = cqin.shape[1]
    chunks = steps // 2
    rows = q.shape[0]
    few = rows // 2
    turn = SPAN - 1
    half = out.shape[1]
    tiles = half // TILE
    scale = LOG2E / math.sqrt(HD)
    other = 1 - m

    def cols_of(c):
        return pl.ds(pl.multiple_of(c * PAIR, PAIR), PAIR)

    def remote(src, dst, ss, rs, **where):
        return pltpu.make_async_remote_copy(
            src_ref=src, dst_ref=dst, send_sem=ss, recv_sem=rs, device_id=where, device_id_type=MESH
        )

    in_copies = [
        pltpu.make_async_copy(src, dst, in_sem.at[i])
        for i, (src, dst) in enumerate(((cq_hbm, cq), (q_hbm, q), (v_hbm, v), (k_hbm, k)))
    ]
    for copy in in_copies:
        copy.start()
    db_copy = pltpu.make_async_copy(db_hbm, db, db_sem)
    db_copy.start()
    w_copies = [
        pltpu.make_async_copy(
            w_hbm.at[:, pl.ds(pl.multiple_of(side * half, TILE), half)], w.at[i], w_sem.at[i]
        )
        for i, side in enumerate((other, m))
    ]

    def peer(j):
        return (d, d + 1 - 2 * lax.rem(d, 2), lax.rem(d + 2, 4), 3 - d)[j]

    barrier = pltpu.get_barrier_semaphore()
    for j in range(1, dps):
        pl.semaphore_signal(barrier, inc=1, device_id={"dp": peer(j)}, device_id_type=MESH)
    for j in range(1, 4):
        pl.semaphore_signal(barrier, inc=1, device_id={"seq": lax.rem(s + j, 4)}, device_id_type=MESH)
    pl.semaphore_signal(barrier, inc=1, device_id={"mp": other}, device_id_type=MESH)

    def turned(block):
        return jnp.concatenate([block[:, :HD].T, block[:, HD:].T], axis=0)

    for copy in in_copies[:3]:
        copy.wait()

    @pl.loop(0, chunks)
    def _(c):
        for src, dst in ((cq, cqh), (q, qh)):
            moved = pltpu.roll(src[:, cols_of(c)].astype(jnp.float32), rows - turn, axis=0)
            moved = moved.astype(jnp.bfloat16)
            dst[c] = moved[:few]
            dst[chunks + c] = moved[few:]
        vt[c] = turned(v[:, cols_of(c)])

    pl.semaphore_wait(barrier, dps + 3)

    def id_hop():
        return remote(ids, ids_tx.at[1], i1_ss, i1_rs, seq=lax.rem(s + 1, 4))

    def kv_hop(c, which):
        src, dst = ((k_hbm.at[:, cols_of(c)], k0), (vt.at[c], vt0))[which]
        return remote(src, dst.at[c], kv_ss.at[c, which], kv_rs.at[c, which], seq=1)

    def q_hop(c, dest):
        slot = jnp.maximum(s - 2, 0)
        return remote(qh.at[c], qin.at[slot, c], q_ss.at[dest - 1, c], q_rs.at[slot, c], seq=dest)

    def q_arrived(c, slot):
        remote(qh.at[c], qin.at[slot, c], q_ss.at[0, c], q_rs.at[slot, c], seq=1).wait_recv()

    def cq_hop(c, j):
        src = cqin.at[2, c] if j == 3 else cqh.at[c]
        return remote(src, cqin.at[j, c], cq_ss.at[j, c], cq_rs.at[j, c], dp=peer(1 if j == 3 else j))

    def sp_hop(c, slot, dest, place):
        return remote(stx.at[slot, c], sp.at[place, c], sp_ss.at[slot, c], sp_rs.at[place, c], seq=dest)

    def cp_hop(c, j):
        return remote(
            ctx.at[j, c], cp.at[j, c], cp_ss.at[j, c], cp_rs.at[j, c], dp=peer(1 if j == 3 else j)
        )

    def id_share(j):
        return remote(ids_tx, ids_rx.at[j], i2_ss.at[j], i2_rs.at[j], dp=peer(j))

    def p_hop(r, t):
        return remote(ptx.at[r, t], prx.at[r, t], p_ss.at[r, t], p_rs.at[r, t], mp=other)

    @pl.when(s < 3)
    def _():
        id_hop().start()

    @pl.loop(0, steps)
    def _(t):
        @pl.when(jnp.logical_and(s == 0, t < chunks))
        def _():
            kv_hop(t, 0).start()
            kv_hop(t, 1).start()

        @pl.when(s >= 2)
        def _():
            q_hop(t, 1).start()

        @pl.when(s == 3)
        def _():
            q_hop(t, 2).start()

        cq_hop(t, 2).start()
        cq_hop(t, 1).start()

    for copy in w_copies:
        copy.start()

    ids_tx[0] = ids[...]

    @pl.when(s == 0)
    def _():
        ids_tx[1] = jnp.zeros_like(ids)

    @pl.when(s > 0)
    def _():
        id_hop().wait_recv()

    for j in range(1, dps):
        id_share(j).start()
    ids_rx[0] = ids_tx[...]

    neutral = jnp.concatenate(
        [jnp.zeros((HD, rows), jnp.bfloat16), jnp.full((16, rows), NEG, jnp.bfloat16)], axis=0
    )
    key_at = lax.broadcasted_iota(jnp.int32, (rows, rows), 0)
    lane_at = lax.rem(lax.broadcasted_iota(jnp.int32, (rows, rows), 1), few) + turn
    in_copies[3].wait()

    for r in range(2):
        causal = key_at <= lax.rem(lane_at + r * few, rows)

        @pl.loop(0, chunks)
        def _(c):
            t = r * chunks + c
            sp[0, t] = attend_pair(qh[t], k[:, cols_of(c)], vt[c], scale, causal)

            @pl.when(s < 1)
            def _():
                sp[1, t] = neutral

            @pl.when(s < 3)
            def _():
                sp[2, t] = neutral

    for j in range(1, dps):
        id_share(j).wait_recv()
    ids_copy = pltpu.make_async_copy(ids_rx, ids_s, ids_sem)
    ids_copy.start()
    ids_copy.wait()
    db_copy.wait()

    at_start = lax.rem(lax.broadcasted_iota(jnp.int32, (1, rows), 1), few) == 0

    def tile_cols(t):
        return pl.ds(pl.multiple_of(t * TILE, TILE), TILE)

    def send_merged(t):
        cp_hop(t, 3).wait_recv()
        ctx[2, t] = pack_piece(*merge_pieces([ctx[2, t], cp[3, t]]))
        cp_hop(t, 2).start()

    def forward(t):
        cq_hop(t, 2).wait_recv()
        cq_hop(t, 3).start()

    def finish(r):
        @pl.loop(0, chunks)
        def _(c):
            t = r * chunks + c

            @pl.when(s >= 2)
            def _():
                sp_hop(t, 0, 2, 1).wait_recv()

            @pl.when(s == 3)
            def _():
                sp_hop(t, 0, 3, 2).wait_recv()

            cp_hop(t, 1).wait_recv()
            cp_hop(t, 2).wait_recv()
            both = (
                merge_pieces([sp[i, t] for i in range(3)])[0]
                + merge_pieces([ctx[0, t], cp[1, t], cp[2, t]])[0]
            )
            both = both.T.astype(jnp.bfloat16)
            for h in range(2):
                cols = pl.ds(pl.multiple_of(c * PAIR + h * HD, HD), HD)
                att[r * few : (r + 1) * few, cols] = both[h * few : (h + 1) * few]

        if r == 0:
            w_copies[0].wait()

        @pl.loop(0, tiles)
        def _(t):
            ptx[r, t] = nn_dot(att[r * few : (r + 1) * few, :], w[0, :, tile_cols(t)]).astype(jnp.bfloat16)
            p_hop(r, t).start()

    def cross_part(r, c, t, j):
        spans = ((0, 0),) if r == 0 else ((0, 1), (1, 1))
        keys, vts, shards = [], [], []
        for which, span in spans:
            blocks = [ids_s[j, which, span, n, 1] for n in range(NEIGH)]
            shards.append([ids_s[j, which, span, n, 0] for n in range(NEIGH)])
            keys.append(jnp.concatenate([db[0, b, :, cols_of(c)] for b in blocks], axis=0))
            vts.append(jnp.concatenate([dvt[c, b] for b in blocks], axis=1))
        owned = []
        for n in range(NEIGH):
            if r == 0:
                row = jnp.where(jnp.broadcast_to(shards[0][n], (1, rows)) == d, 1, 0)
            else:
                here = jnp.where(at_start, shards[0][n], shards[1][n]) == d
                row = jnp.where(jnp.logical_and(here, jnp.logical_or(at_start, s > 0)), 1, 0)
            owned.append(jnp.broadcast_to(row, (RETR, rows)))
        owned = jnp.concatenate(owned, axis=0) > 0
        asked = cqh[t] if j == 0 else cqin[j, t]
        return cross_pair(asked, keys, vts, owned, at_start, scale)

    forward(0)

    for r in range(2):

        @pl.loop(0, chunks)
        def _(c):
            t = r * chunks + c
            cols = cols_of(c)

            if r == 0:

                @pl.loop(0, db.shape[1])
                def _(b):
                    dvt[c, b] = turned(db[1, b, :, cols])

            @pl.when(t + 1 < steps)
            def _():
                forward(t + 1)

            @pl.when(s == 1)
            def _():
                if r == 0:
                    kv_hop(c, 0).wait_recv()
                    kv_hop(c, 1).wait_recv()
                sp[1, t] = attend_pair(qh[t], k0[c], vt0[c], scale)

                @pl.loop(0, 2)
                def _(slot):
                    q_arrived(t, slot)
                    both_k = jnp.concatenate([k0[c], k[:, cols]], axis=0)
                    both_v = jnp.concatenate([vt0[c], vt[c]], axis=1)
                    stx[slot, t] = attend_pair(qin[slot, t], both_k, both_v, scale)
                    sp_hop(t, slot, 2 + slot, 1).start()

            @pl.when(s == 2)
            def _():
                q_arrived(t, 1)
                stx[1, t] = attend_pair(qin[1, t], k[:, cols], vt[c], scale)
                sp_hop(t, 1, 3, 2).start()

            cq_hop(t, 3).wait_recv()
            across, beside = cross_part(r, c, t, 2), cross_part(r, c, t, 3)
            ctx[2, t] = across
            ctx[3, t] = beside
            cp_hop(t, 3).start()
            cq_hop(t, 1).wait_recv()
            near, own = cross_part(r, c, t, 1), cross_part(r, c, t, 0)
            ctx[1, t] = near
            ctx[0, t] = own
            cp_hop(t, 1).start()

            @pl.when(t > 0)
            def _():
                send_merged(t - 1)

            if r == 1:

                @pl.when(c == chunks // 2 - 1)
                def _():
                    finish(0)

    send_merged(steps - 1)
    finish(1)
    w_copies[1].wait()

    @pl.loop(0, tiles)
    def _(t):
        own = nn_dot(att[...], w[1, :, tile_cols(t)])
        p_hop(0, t).wait_recv()
        p_hop(1, t).wait_recv()
        other_part = jnp.concatenate([prx[0, t], prx[1, t]], axis=0).astype(jnp.float32)
        out[:, tile_cols(t)] = pltpu.roll(own + other_part, turn, axis=0).astype(jnp.bfloat16)

    @pl.when(s < 3)
    def _():
        id_hop().wait_send()

    for j in range(1, dps):
        id_share(j).wait_send()

    @pl.loop(0, steps)
    def _(c):
        @pl.when(jnp.logical_and(s == 0, c < chunks))
        def _():
            kv_hop(c, 0).wait_send()
            kv_hop(c, 1).wait_send()

        @pl.when(s >= 2)
        def _():
            q_hop(c, 1).wait_send()

        @pl.when(s == 3)
        def _():
            q_hop(c, 2).wait_send()

        @pl.when(s == 1)
        def _():
            sp_hop(c, 0, 2, 1).wait_send()
            sp_hop(c, 1, 3, 1).wait_send()

        @pl.when(s == 2)
        def _():
            sp_hop(c, 1, 3, 2).wait_send()

        for j in range(1, dps):
            cq_hop(c, j).wait_send()
            cp_hop(c, j).wait_send()

    @pl.loop(0, tiles)
    def _(t):
        p_hop(0, t).wait_send()
        p_hop(1, t).wait_send()


def fused_device(queries, keys, values, cross_queries, neighbour_ids, database, out_weight):
    rows, feat = queries.shape[1:]
    dps = lax.axis_size("dp")
    chunks = feat // PAIR
    steps = 2 * chunks
    few = rows // 2
    width = out_weight.shape[1]
    half = width // 2
    tiles = half // TILE
    ids = neighbour_ids[0]
    bf16 = jnp.bfloat16
    dma = pltpu.SemaphoreType.DMA
    vmem = pl.BlockSpec(memory_space=pltpu.VMEM)
    anywhere = pl.BlockSpec(memory_space=pl.ANY)
    scratch = [
        pltpu.VMEM((rows, feat), bf16),
        pltpu.VMEM((rows, feat), bf16),
        pltpu.VMEM((rows, feat), bf16),
        pltpu.VMEM((rows, feat), bf16),
        pltpu.VMEM((steps, few, PAIR), bf16),
        pltpu.VMEM((steps, few, PAIR), bf16),
        pltpu.VMEM((chunks, PAIR, rows), bf16),
        pltpu.VMEM((chunks, database.shape[2], PAIR, RETR), bf16),
        pltpu.VMEM(database.shape[1:], bf16),
        pltpu.VMEM((2, feat, half), bf16),
        pltpu.VMEM((chunks, rows, PAIR), bf16),
        pltpu.VMEM((chunks, PAIR, rows), bf16),
        pltpu.VMEM((2, steps, few, PAIR), bf16),
        pltpu.VMEM((dps, steps, few, PAIR), bf16),
        pltpu.VMEM((3, steps, PIECE, rows), bf16),
        pltpu.VMEM((2, steps, PIECE, rows), bf16),
        pltpu.VMEM((dps, steps, PIECE, rows), bf16),
        pltpu.VMEM((dps, steps, PIECE, rows), bf16),
        pltpu.VMEM((rows, feat), bf16),
        pltpu.VMEM((2, tiles, few, TILE), bf16),
        pltpu.VMEM((2, tiles, few, TILE), bf16),
        pltpu.VMEM((2,) + ids.shape, jnp.int32),
        pltpu.VMEM((dps, 2) + ids.shape, jnp.int32),
        pltpu.SMEM((dps, 2) + ids.shape, jnp.int32),
        dma((4,)), dma, dma((2,)), dma,
        dma((chunks, 2)), dma((chunks, 2)),
        dma((2, steps)), dma((2, steps)),
        dma((dps, steps)), dma((dps, steps)),
        dma((2, steps)), dma((3, steps)),
        dma((dps, steps)), dma((dps, steps)),
        dma, dma, dma((dps,)), dma((dps,)),
        dma((2, tiles)), dma((2, tiles)),
    ]
    flops = 2 * rows * feat * width + 2 * 2 * rows * feat * (8 * rows + dps * 6 * RETR)
    result = pl.pallas_call(
        layer_kernel,
        out_shape=jax.ShapeDtypeStruct((rows, half), bf16),
        in_specs=[anywhere] * 4 + [vmem] + [anywhere] * 2,
        out_specs=vmem,
        scratch_shapes=scratch,
        compiler_params=pltpu.CompilerParams(
            collective_id=0, has_side_effects=True, vmem_limit_bytes=60 * 1024 * 1024
        ),
        cost_estimate=pl.CostEstimate(
            flops=flops, bytes_accessed=2 * (feat * width + database.size), transcendentals=0
        ),
    )(queries[0], keys[0], values[0], cross_queries[0], ids, database[0], out_weight)
    return result[None]


def solution(mesh):
    placed = (
        P("dp", "seq", "mp"),
        P("dp", "seq", "mp"),
        P("dp", "seq", "mp"),
        P("dp", "seq", "mp"),
        P("dp", "seq", None, None),
        P("dp", None, None, None, "mp"),
        P("mp", None),
    )
    fits = mesh.shape["seq"] == 4 and mesh.shape["mp"] == 2 and mesh.shape["dp"] == 4
    return jax.shard_map(
        fused_device if fits else per_device,
        mesh=mesh,
        in_specs=placed,
        out_specs=P("dp", "seq", "mp"),
        check_vma=False,
    )
```

```python
import functools
import math

import jax
import jax.numpy as jnp
from jax import lax
from jax.experimental import pallas as pl
from jax.experimental.pallas import tpu as pltpu
from jax.sharding import PartitionSpec as P

HD = 128
SPAN = 64
NEIGH = 2
RETR = 128


masked_score = -1e30


def passed_along(value, axis, steps):
    count = lax.axis_size(axis)
    leading, last = (max(0, -steps), min(count, count - steps))
    return lax.ppermute(value, axis, [(source, source + steps) for source in range(leading, last)])


def fold_block(carry_state, query_rows, query_pos, key_rows, value_rows, key_pos, score_scale):
    summed, running_max, totals = carry_state
    scores = (
        jnp.einsum("qhe,khe->hqk", query_rows, key_rows, preferred_element_type=jnp.float32)
        * score_scale
    )
    allowed = (key_pos[None, :] <= query_pos[:, None])[None]
    scores = jnp.where(allowed, scores, masked_score)
    new_max = jnp.maximum(running_max, jnp.max(scores, axis=2))
    weights = jnp.where(allowed, jnp.exp(scores - new_max[:, :, None]), 0.0)
    totals = jnp.sum(weights, axis=2)
    summed = jnp.einsum(
        "hqk,khe->hqe", weights.astype(jnp.bfloat16), value_rows, preferred_element_type=jnp.float32
    )
    return (summed, new_max, totals)


def empty_state(heads_here, row_total):
    return (
        jnp.zeros((heads_here, row_total, HD), jnp.float32),
        jnp.full((heads_here, row_total), masked_score, jnp.float32),
        jnp.zeros((heads_here, row_total), jnp.float32),
    )


def finish_state(carry_state):
    summed, running_max, totals = carry_state
    normed = summed / totals[:, :, None]
    return jnp.transpose(normed, (1, 0, 2)).reshape(
        normed.shape[1], normed.shape[0] * normed.shape[2]
    )


def per_device(queries, keys, values, cross_queries, neighbour_ids, database, out_weight):
    row_count = queries.shape[1]
    feat_here = queries.shape[2]
    heads_here = feat_here // HD
    score_scale = 1.0 / math.sqrt(HD)
    seq_index = lax.axis_index("seq")
    own_first = seq_index * row_count
    own_pos = own_first + jnp.arange(row_count, dtype=jnp.int32)
    query_rows = queries[0].reshape(row_count, heads_here, HD)
    groups_list = [(query_rows, own_pos)]
    start_states = tuple(
        (empty_state(heads_here, group_pos.shape[0]) for group_rows, group_pos in groups_list)
    )
    key_block = lax.all_gather(keys, "seq", axis=1, tiled=True)[0]
    block_rows = key_block.shape[0]
    key_rows = key_block.reshape(block_rows, heads_here, HD)
    value_rows = lax.all_gather(values, "seq", axis=1, tiled=True)[0].reshape(
        block_rows, heads_here, HD
    )
    key_pos = jnp.arange(block_rows, dtype=jnp.int32)
    updated = []
    for carry_state, (group_rows, group_pos) in zip(start_states, groups_list):

        def visit_block(kept_state, group_rows=group_rows, group_pos=group_pos):
            return fold_block(
                kept_state, group_rows, group_pos, key_rows, value_rows, key_pos, score_scale
            )

        updated.append(visit_block(carry_state))
    states = tuple(updated)
    self_out = finish_state(states[0])
    id_pairs = neighbour_ids[0].reshape(-1, 2)
    shard_of = id_pairs[:, 0]
    block_of = id_pairs[:, 1]
    spans_here = neighbour_ids.shape[1]
    every_shard = lax.all_gather(database, "dp", axis=0, tiled=True)
    fetched = jnp.stack([every_shard[shard_of, 0, block_of], every_shard[shard_of, 1, block_of]])
    neighbour_rows = NEIGH * RETR
    grouped = fetched.reshape(2, spans_here, neighbour_rows, heads_here, HD)
    previous = passed_along(grouped[:, spans_here - 1], "seq", 1)
    extended = jnp.concatenate([previous[:, None], grouped], axis=1)
    padded = jnp.concatenate(
        [
            jnp.zeros((1, feat_here), jnp.bfloat16),
            cross_queries[0],
            jnp.zeros((SPAN - 1, feat_here), jnp.bfloat16),
        ],
        axis=0,
    )
    padded = padded.reshape(spans_here + 1, SPAN, heads_here, HD)
    scores = (
        jnp.einsum("gqhe,gkhe->ghqk", padded, extended[0], preferred_element_type=jnp.float32)
        * score_scale
    )
    row_max = jnp.max(scores, axis=3, keepdims=True)
    weights = jnp.exp(scores - row_max)
    totals = jnp.sum(weights, axis=3)
    summed_cross = jnp.einsum(
        "ghqk,gkhe->gqhe",
        weights.astype(jnp.bfloat16),
        extended[1],
        preferred_element_type=jnp.float32,
    )
    cross_out = summed_cross / jnp.transpose(totals, (0, 2, 1))[:, :, :, None]
    valid = ((jnp.arange(spans_here + 1) > 0) | (seq_index > 0)).astype(jnp.float32)
    cross_out = cross_out * valid[:, None, None, None]
    cross_out = cross_out.reshape((spans_here + 1) * SPAN, feat_here)[1 : 1 + row_count]
    attended = (self_out + cross_out).astype(jnp.bfloat16)
    own_sums = lax.psum_scatter(
        lax.dot_general(
            out_weight, attended, (((0,), (1,)), ((), ())), preferred_element_type=jnp.float32
        ).astype(jnp.bfloat16),
        "mp",
        scatter_dimension=0,
        tiled=True,
    )
    return jnp.transpose(own_sums)[None]

NEG = -1e30
LOG2E = 1.4426950408889634
PAIR = 2 * HD
PIECE = PAIR + 16
TILE = 512
MESH = pl.DeviceIdType.MESH


def nt_dot(a, b):
    return lax.dot_general(a, b, (((1,), (1,)), ((), ())), preferred_element_type=jnp.float32)


def nn_dot(a, b):
    return jnp.dot(a, b, preferred_element_type=jnp.float32)


def pack_piece(parts):
    row = lax.broadcasted_iota(jnp.int32, (16, HD), 0)
    stats = jnp.zeros((16, HD), jnp.float32)
    for index, (_, lse) in enumerate(parts):
        rest = lse
        for term in range(3):
            rounded = rest.astype(jnp.bfloat16).astype(jnp.float32)
            stats = jnp.where(row == 3 * index + term, rounded, stats)
            rest = rest - rounded
    return jnp.concatenate(
        [parts[0][0].astype(jnp.bfloat16), parts[1][0].astype(jnp.bfloat16), stats.astype(jnp.bfloat16)],
        axis=0,
    )


def by_head(q):
    blank = jnp.zeros((q.shape[0], HD), q.dtype)
    return jnp.concatenate(
        [
            jnp.concatenate([q[:, :HD], blank], axis=1),
            jnp.concatenate([blank, q[:, HD:]], axis=1),
        ],
        axis=0,
    )


def weigh(scores, scale):
    top = jnp.max(scores, axis=0, keepdims=True)
    weights = jnp.exp2((scores - top) * scale)
    total = jnp.sum(weights, axis=0, keepdims=True)
    return weights.astype(jnp.bfloat16), top, total


def attend_pair(q, k, vt, scale, allowed=None):
    scores = nt_dot(k, by_head(q))
    if allowed is not None:
        scores = jnp.where(allowed, scores, NEG)
    low, top, total = weigh(scores, scale)
    lse = top * scale + jnp.log2(total)
    inverse = 1.0 / total
    rows = q.shape[0]
    parts = []
    for h in range(2):
        lanes = slice(h * rows, (h + 1) * rows)
        summed = nn_dot(vt[h * HD : (h + 1) * HD], low[:, lanes]) * inverse[:, lanes]
        parts.append((summed, lse[:, lanes]))
    return pack_piece(parts)


def cross_pair(q, keys, vts, owned, in_first, in_last, scale):
    both = by_head(q)
    s0, s1, s2 = [nt_dot(k, both) for k in keys]
    scores = jnp.where(in_first, s0, jnp.where(in_last, s2, s1))
    scores = jnp.where(owned, scores, NEG)
    low, top, total = weigh(scores, scale)
    some = top > 0.5 * NEG
    lse = jnp.where(some, top * scale + jnp.log2(total), NEG)
    inverse = jnp.where(some, 1.0 / total, 0.0)
    rows = q.shape[0]
    parts = []
    for h in range(2):
        lanes = slice(h * rows, (h + 1) * rows)
        o0, o1, o2 = [nn_dot(vt[h * HD : (h + 1) * HD], low[:, lanes]) for vt in vts]
        summed = jnp.where(in_first[:, lanes], o0, jnp.where(in_last[:, lanes], o2, o1))
        parts.append((summed * inverse[:, lanes], lse[:, lanes]))
    return pack_piece(parts)


def merge_pieces(pieces, h):
    lses = []
    for piece in pieces:
        stats = piece[PAIR:, :].astype(jnp.float32)
        lses.append(stats[3 * h : 3 * h + 1] + stats[3 * h + 1 : 3 * h + 2] + stats[3 * h + 2 : 3 * h + 3])
    top = functools.reduce(jnp.maximum, lses)
    shares = [jnp.exp2(lse - top) for lse in lses]
    total = functools.reduce(jnp.add, shares)
    inverse = 1.0 / total
    summed = 0.0
    for piece, share in zip(pieces, shares):
        summed = summed + piece[h * HD : (h + 1) * HD, :].astype(jnp.float32) * (share * inverse)
    return summed, jnp.maximum(top + jnp.log2(total), NEG)


def layer_kernel(
    q_hbm, k_hbm, v_hbm, cq_hbm, ids, db_hbm, w_hbm, out,
    q, k, v, cq, vt, dvt, db, w, k0, vt0, qin, cqin, sp, stx, cp, ctx, att, ptx, prx, ids_tx, ids_rx, ids_s,
    in_sem, db_sem, w_sem, ids_sem, kv_ss, kv_rs, q_ss, q_rs, cq_ss, cq_rs, sp_ss, sp_rs, cp_ss, cp_rs,
    i1_ss, i1_rs, i2_ss, i2_rs, p_ss, p_rs,
):
    d = lax.axis_index("dp")
    s = lax.axis_index("seq")
    m = lax.axis_index("mp")
    dps = cqin.shape[0]
    chunks = cqin.shape[1]
    rows = q.shape[0]
    half = out.shape[1]
    tiles = half // TILE
    scale = LOG2E / math.sqrt(HD)
    other = 1 - m

    def cols_of(c):
        return pl.ds(pl.multiple_of(c * PAIR, PAIR), PAIR)

    def remote(src, dst, ss, rs, **where):
        return pltpu.make_async_remote_copy(
            src_ref=src, dst_ref=dst, send_sem=ss, recv_sem=rs, device_id=where, device_id_type=MESH
        )

    in_copies = [
        pltpu.make_async_copy(src, dst, in_sem.at[i])
        for i, (src, dst) in enumerate(((v_hbm, v), (cq_hbm, cq), (q_hbm, q), (k_hbm, k)))
    ]
    for copy in in_copies:
        copy.start()
    db_copy = pltpu.make_async_copy(db_hbm, db, db_sem)
    db_copy.start()
    w_copies = [
        pltpu.make_async_copy(
            w_hbm.at[:, pl.ds(pl.multiple_of(side * half, TILE), half)], w.at[i], w_sem.at[i]
        )
        for i, side in enumerate((other, m))
    ]

    def peer(j):
        return (d, d + 1 - 2 * lax.rem(d, 2), lax.rem(d + 2, 4), 3 - d)[j]

    barrier = pltpu.get_barrier_semaphore()
    for j in range(1, dps):
        pl.semaphore_signal(barrier, inc=1, device_id={"dp": peer(j)}, device_id_type=MESH)
    for j in range(1, 4):
        pl.semaphore_signal(barrier, inc=1, device_id={"seq": lax.rem(s + j, 4)}, device_id_type=MESH)
    pl.semaphore_signal(barrier, inc=1, device_id={"mp": other}, device_id_type=MESH)

    def turned(block):
        return jnp.concatenate([block[:, :HD].T, block[:, HD:].T], axis=0)

    in_copies[0].wait()

    @pl.loop(0, chunks)
    def _(c):
        vt[c] = turned(v[:, cols_of(c)])

    pl.semaphore_wait(barrier, dps + 3)

    def id_hop():
        return remote(ids, ids_tx.at[1], i1_ss, i1_rs, seq=lax.rem(s + 1, 4))

    def kv_hop(c, which):
        src, dst = ((k_hbm.at[:, cols_of(c)], k0), (vt.at[c], vt0))[which]
        return remote(src, dst.at[c], kv_ss.at[c, which], kv_rs.at[c, which], seq=1)

    def q_hop(c, dest):
        slot = jnp.maximum(s - 2, 0)
        return remote(q_hbm.at[:, cols_of(c)], qin.at[slot, c], q_ss.at[dest - 1, c], q_rs.at[slot, c], seq=dest)

    def q_arrived(c, slot):
        remote(q_hbm.at[:, cols_of(c)], qin.at[slot, c], q_ss.at[0, c], q_rs.at[slot, c], seq=1).wait_recv()

    def cq_hop(c, j):
        src = cqin.at[2, c] if j == 3 else cq_hbm.at[:, cols_of(c)]
        return remote(src, cqin.at[j, c], cq_ss.at[j, c], cq_rs.at[j, c], dp=peer(1 if j == 3 else j))

    def sp_hop(c, slot, dest, place):
        return remote(stx.at[slot, c], sp.at[place, c], sp_ss.at[slot, c], sp_rs.at[place, c], seq=dest)

    def cp_hop(c, j):
        return remote(
            ctx.at[j, c], cp.at[j, c], cp_ss.at[j, c], cp_rs.at[j, c], dp=peer(1 if j == 3 else j)
        )

    def id_share(j):
        return remote(ids_tx, ids_rx.at[j], i2_ss.at[j], i2_rs.at[j], dp=peer(j))

    def p_hop(t):
        return remote(ptx.at[t], prx.at[t], p_ss.at[t], p_rs.at[t], mp=other)

    @pl.when(s < 3)
    def _():
        id_hop().start()

    @pl.loop(0, chunks)
    def _(c):
        @pl.when(s == 0)
        def _():
            kv_hop(c, 0).start()
            kv_hop(c, 1).start()

        @pl.when(s >= 2)
        def _():
            q_hop(c, 1).start()

        @pl.when(s == 3)
        def _():
            q_hop(c, 2).start()

        cq_hop(c, 2).start()
        cq_hop(c, 1).start()

    for copy in w_copies:
        copy.start()

    ids_tx[0] = ids[...]

    @pl.when(s == 0)
    def _():
        ids_tx[1] = jnp.zeros_like(ids)

    @pl.when(s > 0)
    def _():
        id_hop().wait_recv()

    for j in range(1, dps):
        id_share(j).start()
    ids_rx[0] = ids_tx[...]

    neutral = jnp.concatenate(
        [jnp.zeros((PAIR, HD), jnp.bfloat16), jnp.full((16, HD), NEG, jnp.bfloat16)], axis=0
    )
    key_at = lax.broadcasted_iota(jnp.int32, (rows, 2 * rows), 0)
    query_at = lax.rem(lax.broadcasted_iota(jnp.int32, (rows, 2 * rows), 1), rows)
    causal = key_at <= query_at
    for copy in in_copies[1:]:
        copy.wait()

    @pl.loop(0, chunks)
    def _(c):
        cols = cols_of(c)
        sp[0, c] = attend_pair(q[:, cols], k[:, cols], vt[c], scale, causal)

        @pl.when(s < 1)
        def _():
            sp[1, c] = neutral

        @pl.when(s < 3)
        def _():
            sp[2, c] = neutral

    for j in range(1, dps):
        id_share(j).wait_recv()
    ids_copy = pltpu.make_async_copy(ids_rx, ids_s, ids_sem)
    ids_copy.start()
    ids_copy.wait()
    db_copy.wait()

    lane = lax.rem(lax.broadcasted_iota(jnp.int32, (1, 2 * rows), 1), rows)
    in_first = lane < SPAN - 1
    in_last = lane == 2 * SPAN - 1
    live = jnp.logical_or(lane >= SPAN - 1, s > 0)

    def forward(c):
        cq_hop(c, 2).wait_recv()
        cq_hop(c, 3).start()

    def send_merged(c):
        cp_hop(c, 3).wait_recv()
        both = [ctx[2, c], cp[3, c]]
        ctx[2, c] = pack_piece([merge_pieces(both, h) for h in range(2)])
        cp_hop(c, 2).start()

    def finish(c):
        @pl.when(s >= 2)
        def _():
            sp_hop(c, 0, 2, 1).wait_recv()

        @pl.when(s == 3)
        def _():
            sp_hop(c, 0, 3, 2).wait_recv()

        cp_hop(c, 1).wait_recv()
        cp_hop(c, 2).wait_recv()
        self_pieces = [sp[i, c] for i in range(3)]
        cross_pieces = [ctx[0, c], cp[1, c], cp[2, c]]
        for h in range(2):
            both = merge_pieces(self_pieces, h)[0] + merge_pieces(cross_pieces, h)[0]
            att[:, pl.ds(pl.multiple_of(c * PAIR + h * HD, HD), HD)] = both.T.astype(jnp.bfloat16)

    forward(0)

    @pl.loop(0, chunks)
    def _(c):
        cols = cols_of(c)

        @pl.when(c + 1 < chunks)
        def _():
            forward(c + 1)

        @pl.when(s == 1)
        def _():
            kv_hop(c, 0).wait_recv()
            kv_hop(c, 1).wait_recv()
            sp[1, c] = attend_pair(q[:, cols], k0[c], vt0[c], scale)

            @pl.loop(0, 2)
            def _(slot):
                q_arrived(c, slot)
                both_k = jnp.concatenate([k0[c], k[:, cols]], axis=0)
                both_v = jnp.concatenate([vt0[c], vt[c]], axis=1)
                stx[slot, c] = attend_pair(qin[slot, c], both_k, both_v, scale)
                sp_hop(c, slot, 2 + slot, 1).start()

        @pl.when(s == 2)
        def _():
            q_arrived(c, 1)
            stx[1, c] = attend_pair(qin[1, c], k[:, cols], vt[c], scale)
            sp_hop(c, 1, 3, 2).start()

        @pl.loop(0, db.shape[1])
        def _(b):
            dvt[b] = turned(db[1, b, :, cols])

        def cross_part(j):
            keys, vts, shards = [], [], []
            for which, span in ((1, 1), (0, 0), (0, 1)):
                blocks = [ids_s[j, which, span, n, 1] for n in range(NEIGH)]
                shards.append([ids_s[j, which, span, n, 0] for n in range(NEIGH)])
                keys.append(jnp.concatenate([db[0, b, :, cols] for b in blocks], axis=0))
                vts.append(jnp.concatenate([dvt[b] for b in blocks], axis=1))
            owned = []
            for n in range(NEIGH):
                shard = jnp.where(in_first, shards[0][n], jnp.where(in_last, shards[2][n], shards[1][n]))
                row = jnp.where(jnp.logical_and(shard == d, live), 1, 0)
                owned.append(jnp.broadcast_to(row, (RETR, 2 * rows)))
            owned = jnp.concatenate(owned, axis=0) > 0
            asked = cq[:, cols] if j == 0 else cqin[j, c]
            return cross_pair(asked, keys, vts, owned, in_first, in_last, scale)

        cq_hop(c, 3).wait_recv()
        cq_hop(c, 1).wait_recv()
        parts = [cross_part(j) for j in (3, 2, 1, 0)]
        for j, part in zip((3, 2, 1, 0), parts):
            ctx[j, c] = part
        cp_hop(c, 3).start()
        cp_hop(c, 1).start()

        @pl.when(c > 0)
        def _():
            send_merged(c - 1)

        @pl.when(c > 1)
        def _():
            finish(c - 2)

    send_merged(chunks - 1)

    @pl.loop(chunks - 2, chunks)
    def _(c):
        finish(c)

    def tile_cols(t):
        return pl.ds(pl.multiple_of(t * TILE, TILE), TILE)

    w_copies[0].wait()

    @pl.loop(0, tiles)
    def _(t):
        ptx[t] = jnp.dot(
            att[...], w[0, :, tile_cols(t)], preferred_element_type=jnp.float32
        ).astype(jnp.bfloat16)
        p_hop(t).start()

    w_copies[1].wait()

    @pl.loop(0, tiles)
    def _(t):
        own = jnp.dot(att[...], w[1, :, tile_cols(t)], preferred_element_type=jnp.float32)
        p_hop(t).wait_recv()
        out[:, tile_cols(t)] = (own + prx[t].astype(jnp.float32)).astype(jnp.bfloat16)

    @pl.when(s < 3)
    def _():
        id_hop().wait_send()

    for j in range(1, dps):
        id_share(j).wait_send()

    @pl.loop(0, chunks)
    def _(c):
        @pl.when(s == 0)
        def _():
            kv_hop(c, 0).wait_send()
            kv_hop(c, 1).wait_send()

        @pl.when(s >= 2)
        def _():
            q_hop(c, 1).wait_send()

        @pl.when(s == 3)
        def _():
            q_hop(c, 2).wait_send()

        @pl.when(s == 1)
        def _():
            sp_hop(c, 0, 2, 1).wait_send()
            sp_hop(c, 1, 3, 1).wait_send()

        @pl.when(s == 2)
        def _():
            sp_hop(c, 1, 3, 2).wait_send()

        for j in range(1, dps):
            cq_hop(c, j).wait_send()
            cp_hop(c, j).wait_send()

    @pl.loop(0, tiles)
    def _(t):
        p_hop(t).wait_send()


def fused_device(queries, keys, values, cross_queries, neighbour_ids, database, out_weight):
    rows, feat = queries.shape[1:]
    dps = lax.axis_size("dp")
    chunks = feat // PAIR
    width = out_weight.shape[1]
    half = width // 2
    tiles = half // TILE
    ids = neighbour_ids[0]
    bf16 = jnp.bfloat16
    dma = pltpu.SemaphoreType.DMA
    vmem = pl.BlockSpec(memory_space=pltpu.VMEM)
    anywhere = pl.BlockSpec(memory_space=pl.ANY)
    scratch = [
        pltpu.VMEM((rows, feat), bf16),
        pltpu.VMEM((rows, feat), bf16),
        pltpu.VMEM((rows, feat), bf16),
        pltpu.VMEM((rows, feat), bf16),
        pltpu.VMEM((chunks, PAIR, rows), bf16),
        pltpu.VMEM((database.shape[2], PAIR, RETR), bf16),
        pltpu.VMEM(database.shape[1:], bf16),
        pltpu.VMEM((2, feat, half), bf16),
        pltpu.VMEM((chunks, rows, PAIR), bf16),
        pltpu.VMEM((chunks, PAIR, rows), bf16),
        pltpu.VMEM((2, chunks, rows, PAIR), bf16),
        pltpu.VMEM((dps, chunks, rows, PAIR), bf16),
        pltpu.VMEM((3, chunks, PIECE, rows), bf16),
        pltpu.VMEM((2, chunks, PIECE, rows), bf16),
        pltpu.VMEM((dps, chunks, PIECE, rows), bf16),
        pltpu.VMEM((dps, chunks, PIECE, rows), bf16),
        pltpu.VMEM((rows, feat), bf16),
        pltpu.VMEM((tiles, rows, TILE), bf16),
        pltpu.VMEM((tiles, rows, TILE), bf16),
        pltpu.VMEM((2,) + ids.shape, jnp.int32),
        pltpu.VMEM((dps, 2) + ids.shape, jnp.int32),
        pltpu.SMEM((dps, 2) + ids.shape, jnp.int32),
        dma((4,)), dma, dma((2,)), dma,
        dma((chunks, 2)), dma((chunks, 2)),
        dma((2, chunks)), dma((2, chunks)),
        dma((dps, chunks)), dma((dps, chunks)),
        dma((2, chunks)), dma((3, chunks)),
        dma((dps, chunks)), dma((dps, chunks)),
        dma, dma, dma((dps,)), dma((dps,)),
        dma((tiles,)), dma((tiles,)),
    ]
    flops = 2 * rows * feat * width + 2 * 2 * rows * feat * (8 * rows + dps * 6 * RETR)
    result = pl.pallas_call(
        layer_kernel,
        out_shape=jax.ShapeDtypeStruct((rows, half), bf16),
        in_specs=[anywhere] * 4 + [vmem] + [anywhere] * 2,
        out_specs=vmem,
        scratch_shapes=scratch,
        compiler_params=pltpu.CompilerParams(
            collective_id=0, has_side_effects=True, vmem_limit_bytes=60 * 1024 * 1024
        ),
        cost_estimate=pl.CostEstimate(
            flops=flops, bytes_accessed=2 * (feat * width + database.size), transcendentals=0
        ),
    )(queries[0], keys[0], values[0], cross_queries[0], ids, database[0], out_weight)
    return result[None]


def solution(mesh):
    placed = (
        P("dp", "seq", "mp"),
        P("dp", "seq", "mp"),
        P("dp", "seq", "mp"),
        P("dp", "seq", "mp"),
        P("dp", "seq", None, None),
        P("dp", None, None, None, "mp"),
        P("mp", None),
    )
    fits = mesh.shape["seq"] == 4 and mesh.shape["mp"] == 2 and mesh.shape["dp"] == 4
    return jax.shard_map(
        fused_device if fits else per_device,
        mesh=mesh,
        in_specs=placed,
        out_specs=P("dp", "seq", "mp"),
        check_vma=False,
    )
```

```python
import functools
import math

import jax
import jax.numpy as jnp
from jax import lax
from jax.experimental import pallas as pl
from jax.experimental.pallas import tpu as pltpu
from jax.sharding import PartitionSpec as P

HD = 128
SPAN = 64
NEIGH = 2
RETR = 128


masked_score = -1e30


def passed_along(value, axis, steps):
    count = lax.axis_size(axis)
    leading, last = (max(0, -steps), min(count, count - steps))
    return lax.ppermute(value, axis, [(source, source + steps) for source in range(leading, last)])


def fold_block(carry_state, query_rows, query_pos, key_rows, value_rows, key_pos, score_scale):
    summed, running_max, totals = carry_state
    scores = (
        jnp.einsum("qhe,khe->hqk", query_rows, key_rows, preferred_element_type=jnp.float32)
        * score_scale
    )
    allowed = (key_pos[None, :] <= query_pos[:, None])[None]
    scores = jnp.where(allowed, scores, masked_score)
    new_max = jnp.maximum(running_max, jnp.max(scores, axis=2))
    weights = jnp.where(allowed, jnp.exp(scores - new_max[:, :, None]), 0.0)
    totals = jnp.sum(weights, axis=2)
    summed = jnp.einsum(
        "hqk,khe->hqe", weights.astype(jnp.bfloat16), value_rows, preferred_element_type=jnp.float32
    )
    return (summed, new_max, totals)


def empty_state(heads_here, row_total):
    return (
        jnp.zeros((heads_here, row_total, HD), jnp.float32),
        jnp.full((heads_here, row_total), masked_score, jnp.float32),
        jnp.zeros((heads_here, row_total), jnp.float32),
    )


def finish_state(carry_state):
    summed, running_max, totals = carry_state
    normed = summed / totals[:, :, None]
    return jnp.transpose(normed, (1, 0, 2)).reshape(
        normed.shape[1], normed.shape[0] * normed.shape[2]
    )


def per_device(queries, keys, values, cross_queries, neighbour_ids, database, out_weight):
    row_count = queries.shape[1]
    feat_here = queries.shape[2]
    heads_here = feat_here // HD
    score_scale = 1.0 / math.sqrt(HD)
    seq_index = lax.axis_index("seq")
    own_first = seq_index * row_count
    own_pos = own_first + jnp.arange(row_count, dtype=jnp.int32)
    query_rows = queries[0].reshape(row_count, heads_here, HD)
    groups_list = [(query_rows, own_pos)]
    start_states = tuple(
        (empty_state(heads_here, group_pos.shape[0]) for group_rows, group_pos in groups_list)
    )
    key_block = lax.all_gather(keys, "seq", axis=1, tiled=True)[0]
    block_rows = key_block.shape[0]
    key_rows = key_block.reshape(block_rows, heads_here, HD)
    value_rows = lax.all_gather(values, "seq", axis=1, tiled=True)[0].reshape(
        block_rows, heads_here, HD
    )
    key_pos = jnp.arange(block_rows, dtype=jnp.int32)
    updated = []
    for carry_state, (group_rows, group_pos) in zip(start_states, groups_list):

        def visit_block(kept_state, group_rows=group_rows, group_pos=group_pos):
            return fold_block(
                kept_state, group_rows, group_pos, key_rows, value_rows, key_pos, score_scale
            )

        updated.append(visit_block(carry_state))
    states = tuple(updated)
    self_out = finish_state(states[0])
    id_pairs = neighbour_ids[0].reshape(-1, 2)
    shard_of = id_pairs[:, 0]
    block_of = id_pairs[:, 1]
    spans_here = neighbour_ids.shape[1]
    every_shard = lax.all_gather(database, "dp", axis=0, tiled=True)
    fetched = jnp.stack([every_shard[shard_of, 0, block_of], every_shard[shard_of, 1, block_of]])
    neighbour_rows = NEIGH * RETR
    grouped = fetched.reshape(2, spans_here, neighbour_rows, heads_here, HD)
    previous = passed_along(grouped[:, spans_here - 1], "seq", 1)
    extended = jnp.concatenate([previous[:, None], grouped], axis=1)
    padded = jnp.concatenate(
        [
            jnp.zeros((1, feat_here), jnp.bfloat16),
            cross_queries[0],
            jnp.zeros((SPAN - 1, feat_here), jnp.bfloat16),
        ],
        axis=0,
    )
    padded = padded.reshape(spans_here + 1, SPAN, heads_here, HD)
    scores = (
        jnp.einsum("gqhe,gkhe->ghqk", padded, extended[0], preferred_element_type=jnp.float32)
        * score_scale
    )
    row_max = jnp.max(scores, axis=3, keepdims=True)
    weights = jnp.exp(scores - row_max)
    totals = jnp.sum(weights, axis=3)
    summed_cross = jnp.einsum(
        "ghqk,gkhe->gqhe",
        weights.astype(jnp.bfloat16),
        extended[1],
        preferred_element_type=jnp.float32,
    )
    cross_out = summed_cross / jnp.transpose(totals, (0, 2, 1))[:, :, :, None]
    valid = ((jnp.arange(spans_here + 1) > 0) | (seq_index > 0)).astype(jnp.float32)
    cross_out = cross_out * valid[:, None, None, None]
    cross_out = cross_out.reshape((spans_here + 1) * SPAN, feat_here)[1 : 1 + row_count]
    attended = (self_out + cross_out).astype(jnp.bfloat16)
    own_sums = lax.psum_scatter(
        lax.dot_general(
            out_weight, attended, (((0,), (1,)), ((), ())), preferred_element_type=jnp.float32
        ).astype(jnp.bfloat16),
        "mp",
        scatter_dimension=0,
        tiled=True,
    )
    return jnp.transpose(own_sums)[None]

NEG = -1e30
LOG2E = 1.4426950408889634
PAIR = 2 * HD
PIECE = PAIR + 16
TILE = 512
MESH = pl.DeviceIdType.MESH


def nt_dot(a, b):
    return lax.dot_general(a, b, (((1,), (1,)), ((), ())), preferred_element_type=jnp.float32)


def nn_dot(a, b):
    return jnp.dot(a, b, preferred_element_type=jnp.float32)


def pack_piece(parts):
    row = lax.broadcasted_iota(jnp.int32, (16, HD), 0)
    stats = jnp.zeros((16, HD), jnp.float32)
    for index, (_, lse) in enumerate(parts):
        rest = lse
        for term in range(3):
            rounded = rest.astype(jnp.bfloat16).astype(jnp.float32)
            stats = jnp.where(row == 3 * index + term, rounded, stats)
            rest = rest - rounded
    return jnp.concatenate(
        [parts[0][0].astype(jnp.bfloat16), parts[1][0].astype(jnp.bfloat16), stats.astype(jnp.bfloat16)],
        axis=0,
    )


def by_head(q):
    blank = jnp.zeros((q.shape[0], HD), q.dtype)
    return jnp.concatenate(
        [
            jnp.concatenate([q[:, :HD], blank], axis=1),
            jnp.concatenate([blank, q[:, HD:]], axis=1),
        ],
        axis=0,
    )


def weigh(scores, scale):
    top = jnp.max(scores, axis=0, keepdims=True)
    weights = jnp.exp2((scores - top) * scale)
    total = jnp.sum(weights, axis=0, keepdims=True)
    return weights.astype(jnp.bfloat16), top, total


def attend_pair(q, k, vt, scale, allowed=None):
    scores = nt_dot(k, by_head(q))
    if allowed is not None:
        scores = jnp.where(allowed, scores, NEG)
    low, top, total = weigh(scores, scale)
    lse = top * scale + jnp.log2(total)
    inverse = 1.0 / total
    rows = q.shape[0]
    parts = []
    for h in range(2):
        lanes = slice(h * rows, (h + 1) * rows)
        summed = nn_dot(vt[h * HD : (h + 1) * HD], low[:, lanes]) * inverse[:, lanes]
        parts.append((summed, lse[:, lanes]))
    return pack_piece(parts)


def cross_pair(q, keys, vts, owned, first, scale):
    few = q.shape[0] // 2
    early, late = by_head(q[:few]), by_head(q[few:])
    late = jnp.concatenate([late[few:], late[:few]], axis=0)
    scores = jnp.concatenate(
        [nt_dot(keys[0], early), jnp.where(first, nt_dot(keys[1], late), nt_dot(keys[2], late))], axis=1
    )
    scores = jnp.where(owned, scores, NEG)
    low, top, total = weigh(scores, scale)
    some = top > 0.5 * NEG
    lse = jnp.where(some, top * scale + jnp.log2(total), NEG)
    inverse = jnp.where(some, 1.0 / total, 0.0)
    lanes = 2 * few
    early = nn_dot(vts[0], low[:, :lanes]) * inverse[:, :lanes]
    late = jnp.where(first, nn_dot(vts[1], low[:, lanes:]), nn_dot(vts[2], low[:, lanes:]))
    late = late * inverse[:, lanes:]
    left = lax.broadcasted_iota(jnp.int32, (1, lanes), 1) < few
    return pack_piece(
        [
            (jnp.where(left, early[:HD], late[:HD]), jnp.where(left, lse[:, :lanes], lse[:, lanes:])),
            (jnp.where(left, late[HD:], early[HD:]), jnp.where(left, lse[:, lanes:], lse[:, :lanes])),
        ]
    )


def merge_pieces(pieces, h):
    lses = []
    for piece in pieces:
        stats = piece[PAIR:, :].astype(jnp.float32)
        lses.append(stats[3 * h : 3 * h + 1] + stats[3 * h + 1 : 3 * h + 2] + stats[3 * h + 2 : 3 * h + 3])
    top = functools.reduce(jnp.maximum, lses)
    shares = [jnp.exp2(lse - top) for lse in lses]
    total = functools.reduce(jnp.add, shares)
    inverse = 1.0 / total
    summed = 0.0
    for piece, share in zip(pieces, shares):
        summed = summed + piece[h * HD : (h + 1) * HD, :].astype(jnp.float32) * (share * inverse)
    return summed, jnp.maximum(top + jnp.log2(total), NEG)


def layer_kernel(
    q_hbm, k_hbm, v_hbm, cq_hbm, ids, db_hbm, w_hbm, out,
    q, k, v, cq, cqr, vt, dvt, db, w, k0, vt0, qin, cqin, sp, stx, cp, ctx, att, ptx, prx, ids_tx, ids_rx, ids_s,
    in_sem, db_sem, w_sem, ids_sem, kv_ss, kv_rs, q_ss, q_rs, cq_ss, cq_rs, sp_ss, sp_rs, cp_ss, cp_rs,
    i1_ss, i1_rs, i2_ss, i2_rs, p_ss, p_rs,
):
    d = lax.axis_index("dp")
    s = lax.axis_index("seq")
    m = lax.axis_index("mp")
    dps = cqin.shape[0]
    chunks = cqin.shape[1]
    rows = q.shape[0]
    half = out.shape[1]
    tiles = half // TILE
    scale = LOG2E / math.sqrt(HD)
    other = 1 - m

    def cols_of(c):
        return pl.ds(pl.multiple_of(c * PAIR, PAIR), PAIR)

    def remote(src, dst, ss, rs, **where):
        return pltpu.make_async_remote_copy(
            src_ref=src, dst_ref=dst, send_sem=ss, recv_sem=rs, device_id=where, device_id_type=MESH
        )

    in_copies = [
        pltpu.make_async_copy(src, dst, in_sem.at[i])
        for i, (src, dst) in enumerate(((v_hbm, v), (cq_hbm, cq), (q_hbm, q), (k_hbm, k)))
    ]
    for copy in in_copies:
        copy.start()
    db_copy = pltpu.make_async_copy(db_hbm, db, db_sem)
    db_copy.start()
    w_copies = [
        pltpu.make_async_copy(
            w_hbm.at[:, pl.ds(pl.multiple_of(side * half, TILE), half)], w.at[i], w_sem.at[i]
        )
        for i, side in enumerate((other, m))
    ]

    def peer(j):
        return (d, d + 1 - 2 * lax.rem(d, 2), lax.rem(d + 2, 4), 3 - d)[j]

    barrier = pltpu.get_barrier_semaphore()
    for j in range(1, dps):
        pl.semaphore_signal(barrier, inc=1, device_id={"dp": peer(j)}, device_id_type=MESH)
    for j in range(1, 4):
        pl.semaphore_signal(barrier, inc=1, device_id={"seq": lax.rem(s + j, 4)}, device_id_type=MESH)
    pl.semaphore_signal(barrier, inc=1, device_id={"mp": other}, device_id_type=MESH)

    def turned(block):
        return jnp.concatenate([block[:, :HD].T, block[:, HD:].T], axis=0)

    turn = SPAN - 1
    few = rows // 2
    in_copies[0].wait()
    in_copies[1].wait()

    @pl.loop(0, chunks)
    def _(c):
        moved = pltpu.roll(cq[:, cols_of(c)].astype(jnp.float32), rows - turn, axis=0)
        cqr[c] = moved.astype(jnp.bfloat16)
        vt[c] = turned(v[:, cols_of(c)])

    pl.semaphore_wait(barrier, dps + 3)

    def id_hop():
        return remote(ids, ids_tx.at[1], i1_ss, i1_rs, seq=lax.rem(s + 1, 4))

    def kv_hop(c, which):
        src, dst = ((k_hbm.at[:, cols_of(c)], k0), (vt.at[c], vt0))[which]
        return remote(src, dst.at[c], kv_ss.at[c, which], kv_rs.at[c, which], seq=1)

    def q_hop(c, dest):
        slot = jnp.maximum(s - 2, 0)
        return remote(q_hbm.at[:, cols_of(c)], qin.at[slot, c], q_ss.at[dest - 1, c], q_rs.at[slot, c], seq=dest)

    def q_arrived(c, slot):
        remote(q_hbm.at[:, cols_of(c)], qin.at[slot, c], q_ss.at[0, c], q_rs.at[slot, c], seq=1).wait_recv()

    def cq_hop(c, j):
        src = cqin.at[2, c] if j == 3 else cqr.at[c]
        return remote(src, cqin.at[j, c], cq_ss.at[j, c], cq_rs.at[j, c], dp=peer(1 if j == 3 else j))

    def sp_hop(c, slot, dest, place):
        return remote(stx.at[slot, c], sp.at[place, c], sp_ss.at[slot, c], sp_rs.at[place, c], seq=dest)

    def cp_hop(c, j):
        return remote(
            ctx.at[j, c], cp.at[j, c], cp_ss.at[j, c], cp_rs.at[j, c], dp=peer(1 if j == 3 else j)
        )

    def id_share(j):
        return remote(ids_tx, ids_rx.at[j], i2_ss.at[j], i2_rs.at[j], dp=peer(j))

    def p_hop(t):
        return remote(ptx.at[t], prx.at[t], p_ss.at[t], p_rs.at[t], mp=other)

    @pl.when(s < 3)
    def _():
        id_hop().start()

    @pl.loop(0, chunks)
    def _(c):
        @pl.when(s == 0)
        def _():
            kv_hop(c, 0).start()
            kv_hop(c, 1).start()

        @pl.when(s >= 2)
        def _():
            q_hop(c, 1).start()

        @pl.when(s == 3)
        def _():
            q_hop(c, 2).start()

        cq_hop(c, 2).start()
        cq_hop(c, 1).start()

    for copy in w_copies:
        copy.start()

    ids_tx[0] = ids[...]

    @pl.when(s == 0)
    def _():
        ids_tx[1] = jnp.zeros_like(ids)

    @pl.when(s > 0)
    def _():
        id_hop().wait_recv()

    for j in range(1, dps):
        id_share(j).start()
    ids_rx[0] = ids_tx[...]

    neutral = jnp.concatenate(
        [jnp.zeros((PAIR, HD), jnp.bfloat16), jnp.full((16, HD), NEG, jnp.bfloat16)], axis=0
    )
    key_at = lax.broadcasted_iota(jnp.int32, (rows, 2 * rows), 0)
    query_at = lax.rem(lax.broadcasted_iota(jnp.int32, (rows, 2 * rows), 1), rows)
    causal = key_at <= query_at
    for copy in in_copies[2:]:
        copy.wait()

    @pl.loop(0, chunks)
    def _(c):
        cols = cols_of(c)
        sp[0, c] = attend_pair(q[:, cols], k[:, cols], vt[c], scale, causal)

        @pl.when(s < 1)
        def _():
            sp[1, c] = neutral

        @pl.when(s < 3)
        def _():
            sp[2, c] = neutral

    for j in range(1, dps):
        id_share(j).wait_recv()
    ids_copy = pltpu.make_async_copy(ids_rx, ids_s, ids_sem)
    ids_copy.start()
    ids_copy.wait()
    db_copy.wait()

    at_start = lax.rem(lax.broadcasted_iota(jnp.int32, (1, rows), 1), few) == 0

    @pl.loop(0, chunks)
    def _(c):
        cols = cols_of(c)
        cq_hop(c, 2).wait_recv()
        cq_hop(c, 3).start()

        @pl.when(s == 1)
        def _():
            kv_hop(c, 0).wait_recv()
            kv_hop(c, 1).wait_recv()
            sp[1, c] = attend_pair(q[:, cols], k0[c], vt0[c], scale)

            @pl.loop(0, 2)
            def _(slot):
                q_arrived(c, slot)
                both_k = jnp.concatenate([k0[c], k[:, cols]], axis=0)
                both_v = jnp.concatenate([vt0[c], vt[c]], axis=1)
                stx[slot, c] = attend_pair(qin[slot, c], both_k, both_v, scale)
                sp_hop(c, slot, 2 + slot, 1).start()

        @pl.when(s == 2)
        def _():
            q_arrived(c, 1)
            stx[1, c] = attend_pair(qin[1, c], k[:, cols], vt[c], scale)
            sp_hop(c, 1, 3, 2).start()

        @pl.loop(0, db.shape[1])
        def _(b):
            dvt[b] = turned(db[1, b, :, cols])

        def cross_part(j):
            keys, vts, shards = [], [], []
            for which, span in ((0, 0), (0, 1), (1, 1)):
                blocks = [ids_s[j, which, span, n, 1] for n in range(NEIGH)]
                shards.append([ids_s[j, which, span, n, 0] for n in range(NEIGH)])
                keys.append(jnp.concatenate([db[0, b, :, cols] for b in blocks], axis=0))
                vts.append(jnp.concatenate([dvt[b] for b in blocks], axis=1))
            owned = []
            for n in range(NEIGH):
                early = jnp.broadcast_to(shards[0][n], (1, rows)) == d
                late = jnp.where(at_start, shards[1][n], shards[2][n]) == d
                late = jnp.logical_and(late, jnp.logical_or(at_start, s > 0))
                row = jnp.concatenate([jnp.where(early, 1, 0), jnp.where(late, 1, 0)], axis=1)
                owned.append(jnp.broadcast_to(row, (RETR, 2 * rows)))
            owned = jnp.concatenate(owned, axis=0) > 0
            asked = cqr[c] if j == 0 else cqin[j, c]
            return cross_pair(asked, keys, vts, owned, at_start, scale)

        cq_hop(c, 3).wait_recv()
        across, beside = cross_part(2), cross_part(3)
        ctx[3, c] = beside
        cp_hop(c, 3).start()
        cq_hop(c, 1).wait_recv()
        near, own = cross_part(1), cross_part(0)
        ctx[1, c] = near
        ctx[0, c] = own
        cp_hop(c, 1).start()
        cp_hop(c, 3).wait_recv()
        both = [across, cp[3, c]]
        ctx[2, c] = pack_piece([merge_pieces(both, h) for h in range(2)])
        cp_hop(c, 2).start()

    @pl.loop(0, chunks)
    def _(c):
        @pl.when(s >= 2)
        def _():
            sp_hop(c, 0, 2, 1).wait_recv()

        @pl.when(s == 3)
        def _():
            sp_hop(c, 0, 3, 2).wait_recv()

        cp_hop(c, 1).wait_recv()
        cp_hop(c, 2).wait_recv()
        self_pieces = [sp[i, c] for i in range(3)]
        cross_pieces = [ctx[0, c], cp[1, c], cp[2, c]]
        for h in range(2):
            back = (turn, rows - 1)[h]
            both = merge_pieces(self_pieces, h)[0].T
            both = both + pltpu.roll(merge_pieces(cross_pieces, h)[0].T, back, axis=0)
            att[:, pl.ds(pl.multiple_of(c * PAIR + h * HD, HD), HD)] = both.astype(jnp.bfloat16)

    def tile_cols(t):
        return pl.ds(pl.multiple_of(t * TILE, TILE), TILE)

    w_copies[0].wait()

    @pl.loop(0, tiles)
    def _(t):
        ptx[t] = jnp.dot(
            att[...], w[0, :, tile_cols(t)], preferred_element_type=jnp.float32
        ).astype(jnp.bfloat16)
        p_hop(t).start()

    w_copies[1].wait()

    @pl.loop(0, tiles)
    def _(t):
        own = jnp.dot(att[...], w[1, :, tile_cols(t)], preferred_element_type=jnp.float32)
        p_hop(t).wait_recv()
        out[:, tile_cols(t)] = (own + prx[t].astype(jnp.float32)).astype(jnp.bfloat16)

    @pl.when(s < 3)
    def _():
        id_hop().wait_send()

    for j in range(1, dps):
        id_share(j).wait_send()

    @pl.loop(0, chunks)
    def _(c):
        @pl.when(s == 0)
        def _():
            kv_hop(c, 0).wait_send()
            kv_hop(c, 1).wait_send()

        @pl.when(s >= 2)
        def _():
            q_hop(c, 1).wait_send()

        @pl.when(s == 3)
        def _():
            q_hop(c, 2).wait_send()

        @pl.when(s == 1)
        def _():
            sp_hop(c, 0, 2, 1).wait_send()
            sp_hop(c, 1, 3, 1).wait_send()

        @pl.when(s == 2)
        def _():
            sp_hop(c, 1, 3, 2).wait_send()

        for j in range(1, dps):
            cq_hop(c, j).wait_send()
            cp_hop(c, j).wait_send()

    @pl.loop(0, tiles)
    def _(t):
        p_hop(t).wait_send()


def fused_device(queries, keys, values, cross_queries, neighbour_ids, database, out_weight):
    rows, feat = queries.shape[1:]
    dps = lax.axis_size("dp")
    chunks = feat // PAIR
    width = out_weight.shape[1]
    half = width // 2
    tiles = half // TILE
    ids = neighbour_ids[0]
    bf16 = jnp.bfloat16
    dma = pltpu.SemaphoreType.DMA
    vmem = pl.BlockSpec(memory_space=pltpu.VMEM)
    anywhere = pl.BlockSpec(memory_space=pl.ANY)
    scratch = [
        pltpu.VMEM((rows, feat), bf16),
        pltpu.VMEM((rows, feat), bf16),
        pltpu.VMEM((rows, feat), bf16),
        pltpu.VMEM((rows, feat), bf16),
        pltpu.VMEM((chunks, rows, PAIR), bf16),
        pltpu.VMEM((chunks, PAIR, rows), bf16),
        pltpu.VMEM((database.shape[2], PAIR, RETR), bf16),
        pltpu.VMEM(database.shape[1:], bf16),
        pltpu.VMEM((2, feat, half), bf16),
        pltpu.VMEM((chunks, rows, PAIR), bf16),
        pltpu.VMEM((chunks, PAIR, rows), bf16),
        pltpu.VMEM((2, chunks, rows, PAIR), bf16),
        pltpu.VMEM((dps, chunks, rows, PAIR), bf16),
        pltpu.VMEM((3, chunks, PIECE, rows), bf16),
        pltpu.VMEM((2, chunks, PIECE, rows), bf16),
        pltpu.VMEM((dps, chunks, PIECE, rows), bf16),
        pltpu.VMEM((dps, chunks, PIECE, rows), bf16),
        pltpu.VMEM((rows, feat), bf16),
        pltpu.VMEM((tiles, rows, TILE), bf16),
        pltpu.VMEM((tiles, rows, TILE), bf16),
        pltpu.VMEM((2,) + ids.shape, jnp.int32),
        pltpu.VMEM((dps, 2) + ids.shape, jnp.int32),
        pltpu.SMEM((dps, 2) + ids.shape, jnp.int32),
        dma((4,)), dma, dma((2,)), dma,
        dma((chunks, 2)), dma((chunks, 2)),
        dma((2, chunks)), dma((2, chunks)),
        dma((dps, chunks)), dma((dps, chunks)),
        dma((2, chunks)), dma((3, chunks)),
        dma((dps, chunks)), dma((dps, chunks)),
        dma, dma, dma((dps,)), dma((dps,)),
        dma((tiles,)), dma((tiles,)),
    ]
    flops = 2 * rows * feat * width + 2 * 2 * rows * feat * (8 * rows + dps * 6 * RETR)
    result = pl.pallas_call(
        layer_kernel,
        out_shape=jax.ShapeDtypeStruct((rows, half), bf16),
        in_specs=[anywhere] * 4 + [vmem] + [anywhere] * 2,
        out_specs=vmem,
        scratch_shapes=scratch,
        compiler_params=pltpu.CompilerParams(
            collective_id=0, has_side_effects=True, vmem_limit_bytes=60 * 1024 * 1024
        ),
        cost_estimate=pl.CostEstimate(
            flops=flops, bytes_accessed=2 * (feat * width + database.size), transcendentals=0
        ),
    )(queries[0], keys[0], values[0], cross_queries[0], ids, database[0], out_weight)
    return result[None]


def solution(mesh):
    placed = (
        P("dp", "seq", "mp"),
        P("dp", "seq", "mp"),
        P("dp", "seq", "mp"),
        P("dp", "seq", "mp"),
        P("dp", "seq", None, None),
        P("dp", None, None, None, "mp"),
        P("mp", None),
    )
    fits = mesh.shape["seq"] == 4 and mesh.shape["mp"] == 2 and mesh.shape["dp"] == 4
    return jax.shard_map(
        fused_device if fits else per_device,
        mesh=mesh,
        in_specs=placed,
        out_specs=P("dp", "seq", "mp"),
        check_vma=False,
    )
```

```python
import functools
import math

import jax
import jax.numpy as jnp
from jax import lax
from jax.experimental import pallas as pl
from jax.experimental.pallas import tpu as pltpu
from jax.sharding import PartitionSpec as P

HD = 128
SPAN = 64
NEIGH = 2
RETR = 128


masked_score = -1e30


def passed_along(value, axis, steps):
    count = lax.axis_size(axis)
    leading, last = (max(0, -steps), min(count, count - steps))
    return lax.ppermute(value, axis, [(source, source + steps) for source in range(leading, last)])


def fold_block(carry_state, query_rows, query_pos, key_rows, value_rows, key_pos, score_scale):
    summed, running_max, totals = carry_state
    scores = (
        jnp.einsum("qhe,khe->hqk", query_rows, key_rows, preferred_element_type=jnp.float32)
        * score_scale
    )
    allowed = (key_pos[None, :] <= query_pos[:, None])[None]
    scores = jnp.where(allowed, scores, masked_score)
    new_max = jnp.maximum(running_max, jnp.max(scores, axis=2))
    weights = jnp.where(allowed, jnp.exp(scores - new_max[:, :, None]), 0.0)
    totals = jnp.sum(weights, axis=2)
    summed = jnp.einsum(
        "hqk,khe->hqe", weights.astype(jnp.bfloat16), value_rows, preferred_element_type=jnp.float32
    )
    return (summed, new_max, totals)


def empty_state(heads_here, row_total):
    return (
        jnp.zeros((heads_here, row_total, HD), jnp.float32),
        jnp.full((heads_here, row_total), masked_score, jnp.float32),
        jnp.zeros((heads_here, row_total), jnp.float32),
    )


def finish_state(carry_state):
    summed, running_max, totals = carry_state
    normed = summed / totals[:, :, None]
    return jnp.transpose(normed, (1, 0, 2)).reshape(
        normed.shape[1], normed.shape[0] * normed.shape[2]
    )


def per_device(queries, keys, values, cross_queries, neighbour_ids, database, out_weight):
    row_count = queries.shape[1]
    feat_here = queries.shape[2]
    heads_here = feat_here // HD
    score_scale = 1.0 / math.sqrt(HD)
    seq_index = lax.axis_index("seq")
    own_first = seq_index * row_count
    own_pos = own_first + jnp.arange(row_count, dtype=jnp.int32)
    query_rows = queries[0].reshape(row_count, heads_here, HD)
    groups_list = [(query_rows, own_pos)]
    start_states = tuple(
        (empty_state(heads_here, group_pos.shape[0]) for group_rows, group_pos in groups_list)
    )
    key_block = lax.all_gather(keys, "seq", axis=1, tiled=True)[0]
    block_rows = key_block.shape[0]
    key_rows = key_block.reshape(block_rows, heads_here, HD)
    value_rows = lax.all_gather(values, "seq", axis=1, tiled=True)[0].reshape(
        block_rows, heads_here, HD
    )
    key_pos = jnp.arange(block_rows, dtype=jnp.int32)
    updated = []
    for carry_state, (group_rows, group_pos) in zip(start_states, groups_list):

        def visit_block(kept_state, group_rows=group_rows, group_pos=group_pos):
            return fold_block(
                kept_state, group_rows, group_pos, key_rows, value_rows, key_pos, score_scale
            )

        updated.append(visit_block(carry_state))
    states = tuple(updated)
    self_out = finish_state(states[0])
    id_pairs = neighbour_ids[0].reshape(-1, 2)
    shard_of = id_pairs[:, 0]
    block_of = id_pairs[:, 1]
    spans_here = neighbour_ids.shape[1]
    every_shard = lax.all_gather(database, "dp", axis=0, tiled=True)
    fetched = jnp.stack([every_shard[shard_of, 0, block_of], every_shard[shard_of, 1, block_of]])
    neighbour_rows = NEIGH * RETR
    grouped = fetched.reshape(2, spans_here, neighbour_rows, heads_here, HD)
    previous = passed_along(grouped[:, spans_here - 1], "seq", 1)
    extended = jnp.concatenate([previous[:, None], grouped], axis=1)
    padded = jnp.concatenate(
        [
            jnp.zeros((1, feat_here), jnp.bfloat16),
            cross_queries[0],
            jnp.zeros((SPAN - 1, feat_here), jnp.bfloat16),
        ],
        axis=0,
    )
    padded = padded.reshape(spans_here + 1, SPAN, heads_here, HD)
    scores = (
        jnp.einsum("gqhe,gkhe->ghqk", padded, extended[0], preferred_element_type=jnp.float32)
        * score_scale
    )
    row_max = jnp.max(scores, axis=3, keepdims=True)
    weights = jnp.exp(scores - row_max)
    totals = jnp.sum(weights, axis=3)
    summed_cross = jnp.einsum(
        "ghqk,gkhe->gqhe",
        weights.astype(jnp.bfloat16),
        extended[1],
        preferred_element_type=jnp.float32,
    )
    cross_out = summed_cross / jnp.transpose(totals, (0, 2, 1))[:, :, :, None]
    valid = ((jnp.arange(spans_here + 1) > 0) | (seq_index > 0)).astype(jnp.float32)
    cross_out = cross_out * valid[:, None, None, None]
    cross_out = cross_out.reshape((spans_here + 1) * SPAN, feat_here)[1 : 1 + row_count]
    attended = (self_out + cross_out).astype(jnp.bfloat16)
    own_sums = lax.psum_scatter(
        lax.dot_general(
            out_weight, attended, (((0,), (1,)), ((), ())), preferred_element_type=jnp.float32
        ).astype(jnp.bfloat16),
        "mp",
        scatter_dimension=0,
        tiled=True,
    )
    return jnp.transpose(own_sums)[None]

NEG = -1e30
LOG2E = 1.4426950408889634
PAIR = 2 * HD
PIECE = PAIR + 16
TILE = 512
MESH = pl.DeviceIdType.MESH


def nt_dot(a, b):
    return lax.dot_general(a, b, (((1,), (1,)), ((), ())), preferred_element_type=jnp.float32)


def nn_dot(a, b):
    return jnp.dot(a, b, preferred_element_type=jnp.float32)


def pack_piece(parts):
    row = lax.broadcasted_iota(jnp.int32, (16, HD), 0)
    stats = jnp.zeros((16, HD), jnp.float32)
    for index, (_, lse) in enumerate(parts):
        rest = lse
        for term in range(3):
            rounded = rest.astype(jnp.bfloat16).astype(jnp.float32)
            stats = jnp.where(row == 3 * index + term, rounded, stats)
            rest = rest - rounded
    return jnp.concatenate(
        [parts[0][0].astype(jnp.bfloat16), parts[1][0].astype(jnp.bfloat16), stats.astype(jnp.bfloat16)],
        axis=0,
    )


def by_head(q):
    blank = jnp.zeros((q.shape[0], HD), q.dtype)
    return jnp.concatenate(
        [
            jnp.concatenate([q[:, :HD], blank], axis=1),
            jnp.concatenate([blank, q[:, HD:]], axis=1),
        ],
        axis=0,
    )


def weigh(scores, scale):
    top = jnp.max(scores, axis=0, keepdims=True)
    weights = jnp.exp2((scores - top) * scale)
    total = jnp.sum(weights, axis=0, keepdims=True)
    return weights.astype(jnp.bfloat16), top, total


def attend_pair(q, k, vt, scale, allowed=None):
    scores = nt_dot(k, by_head(q))
    if allowed is not None:
        scores = jnp.where(allowed, scores, NEG)
    low, top, total = weigh(scores, scale)
    lse = top * scale + jnp.log2(total)
    inverse = 1.0 / total
    rows = q.shape[0]
    parts = []
    for h in range(2):
        lanes = slice(h * rows, (h + 1) * rows)
        summed = nn_dot(vt[h * HD : (h + 1) * HD], low[:, lanes]) * inverse[:, lanes]
        parts.append((summed, lse[:, lanes]))
    return pack_piece(parts)


def cross_pair(q, keys, vts, owned, first, scale):
    few = q.shape[0] // 2
    early, late = by_head(q[:few]), by_head(q[few:])
    late = jnp.concatenate([late[few:], late[:few]], axis=0)
    scores = jnp.concatenate(
        [nt_dot(keys[0], early), jnp.where(first, nt_dot(keys[1], late), nt_dot(keys[2], late))], axis=1
    )
    scores = jnp.where(owned, scores, NEG)
    low, top, total = weigh(scores, scale)
    some = top > 0.5 * NEG
    lse = jnp.where(some, top * scale + jnp.log2(total), NEG)
    inverse = jnp.where(some, 1.0 / total, 0.0)
    lanes = 2 * few
    early = nn_dot(vts[0], low[:, :lanes]) * inverse[:, :lanes]
    late = jnp.where(first, nn_dot(vts[1], low[:, lanes:]), nn_dot(vts[2], low[:, lanes:]))
    late = late * inverse[:, lanes:]
    left = lax.broadcasted_iota(jnp.int32, (1, lanes), 1) < few
    return pack_piece(
        [
            (jnp.where(left, early[:HD], late[:HD]), jnp.where(left, lse[:, :lanes], lse[:, lanes:])),
            (jnp.where(left, late[HD:], early[HD:]), jnp.where(left, lse[:, lanes:], lse[:, :lanes])),
        ]
    )


def merge_pieces(pieces, h):
    lses = []
    for piece in pieces:
        stats = piece[PAIR:, :].astype(jnp.float32)
        lses.append(stats[3 * h : 3 * h + 1] + stats[3 * h + 1 : 3 * h + 2] + stats[3 * h + 2 : 3 * h + 3])
    top = functools.reduce(jnp.maximum, lses)
    shares = [jnp.exp2(lse - top) for lse in lses]
    total = functools.reduce(jnp.add, shares)
    inverse = 1.0 / total
    summed = 0.0
    for piece, share in zip(pieces, shares):
        summed = summed + piece[h * HD : (h + 1) * HD, :].astype(jnp.float32) * (share * inverse)
    return summed, jnp.maximum(top + jnp.log2(total), NEG)


def layer_kernel(
    q_hbm, k_hbm, v_hbm, cq_hbm, ids, db_hbm, w_hbm, out,
    q, k, v, cq, cqr, vt, dvt, db, w, k0, vt0, qin, cqin, sp, stx, cp, ctx, att, ptx, prx, ids_tx, ids_rx, ids_s,
    in_sem, db_sem, w_sem, ids_sem, kv_ss, kv_rs, q_ss, q_rs, cq_ss, cq_rs, sp_ss, sp_rs, cp_ss, cp_rs,
    i1_ss, i1_rs, i2_ss, i2_rs, p_ss, p_rs,
):
    d = lax.axis_index("dp")
    s = lax.axis_index("seq")
    m = lax.axis_index("mp")
    dps = cqin.shape[0]
    chunks = cqin.shape[1]
    rows = q.shape[0]
    half = out.shape[1]
    tiles = half // TILE
    scale = LOG2E / math.sqrt(HD)
    other = 1 - m

    def cols_of(c):
        return pl.ds(pl.multiple_of(c * PAIR, PAIR), PAIR)

    def remote(src, dst, ss, rs, **where):
        return pltpu.make_async_remote_copy(
            src_ref=src, dst_ref=dst, send_sem=ss, recv_sem=rs, device_id=where, device_id_type=MESH
        )

    in_copies = [
        pltpu.make_async_copy(src, dst, in_sem.at[i])
        for i, (src, dst) in enumerate(((v_hbm, v), (cq_hbm, cq), (q_hbm, q), (k_hbm, k)))
    ]
    for copy in in_copies:
        copy.start()
    db_copy = pltpu.make_async_copy(db_hbm, db, db_sem)
    db_copy.start()
    w_copies = [
        pltpu.make_async_copy(
            w_hbm.at[:, pl.ds(pl.multiple_of(side * half, TILE), half)], w.at[i], w_sem.at[i]
        )
        for i, side in enumerate((other, m))
    ]

    def peer(j):
        return (d, d + 1 - 2 * lax.rem(d, 2), lax.rem(d + 2, 4), 3 - d)[j]

    barrier = pltpu.get_barrier_semaphore()
    for j in range(1, dps):
        pl.semaphore_signal(barrier, inc=1, device_id={"dp": peer(j)}, device_id_type=MESH)
    for j in range(1, 4):
        pl.semaphore_signal(barrier, inc=1, device_id={"seq": lax.rem(s + j, 4)}, device_id_type=MESH)
    pl.semaphore_signal(barrier, inc=1, device_id={"mp": other}, device_id_type=MESH)

    def turned(block):
        return jnp.concatenate([block[:, :HD].T, block[:, HD:].T], axis=0)

    turn = SPAN - 1
    few = rows // 2
    in_copies[0].wait()
    in_copies[1].wait()

    @pl.loop(0, chunks)
    def _(c):
        moved = pltpu.roll(cq[:, cols_of(c)].astype(jnp.float32), rows - turn, axis=0)
        cqr[c] = moved.astype(jnp.bfloat16)
        vt[c] = turned(v[:, cols_of(c)])

    pl.semaphore_wait(barrier, dps + 3)

    def id_hop():
        return remote(ids, ids_tx.at[1], i1_ss, i1_rs, seq=lax.rem(s + 1, 4))

    def kv_hop(c, which):
        src, dst = ((k_hbm.at[:, cols_of(c)], k0), (vt.at[c], vt0))[which]
        return remote(src, dst.at[c], kv_ss.at[c, which], kv_rs.at[c, which], seq=1)

    def q_hop(c, dest):
        slot = jnp.maximum(s - 2, 0)
        return remote(q_hbm.at[:, cols_of(c)], qin.at[slot, c], q_ss.at[dest - 1, c], q_rs.at[slot, c], seq=dest)

    def q_arrived(c, slot):
        remote(q_hbm.at[:, cols_of(c)], qin.at[slot, c], q_ss.at[0, c], q_rs.at[slot, c], seq=1).wait_recv()

    def cq_hop(c, j):
        src = cqin.at[2, c] if j == 3 else cqr.at[c]
        return remote(src, cqin.at[j, c], cq_ss.at[j, c], cq_rs.at[j, c], dp=peer(1 if j == 3 else j))

    def sp_hop(c, slot, dest, place):
        return remote(stx.at[slot, c], sp.at[place, c], sp_ss.at[slot, c], sp_rs.at[place, c], seq=dest)

    def cp_hop(c, j):
        return remote(
            ctx.at[j, c], cp.at[j, c], cp_ss.at[j, c], cp_rs.at[j, c], dp=peer(1 if j == 3 else j)
        )

    def id_share(j):
        return remote(ids_tx, ids_rx.at[j], i2_ss.at[j], i2_rs.at[j], dp=peer(j))

    def p_hop(t):
        return remote(ptx.at[t], prx.at[t], p_ss.at[t], p_rs.at[t], mp=other)

    @pl.when(s < 3)
    def _():
        id_hop().start()

    @pl.loop(0, chunks)
    def _(c):
        @pl.when(s == 0)
        def _():
            kv_hop(c, 0).start()
            kv_hop(c, 1).start()

        @pl.when(s >= 2)
        def _():
            q_hop(c, 1).start()

        @pl.when(s == 3)
        def _():
            q_hop(c, 2).start()

        cq_hop(c, 2).start()
        cq_hop(c, 1).start()

    for copy in w_copies:
        copy.start()

    ids_tx[0] = ids[...]

    @pl.when(s == 0)
    def _():
        ids_tx[1] = jnp.zeros_like(ids)

    @pl.when(s > 0)
    def _():
        id_hop().wait_recv()

    for j in range(1, dps):
        id_share(j).start()
    ids_rx[0] = ids_tx[...]

    neutral = jnp.concatenate(
        [jnp.zeros((PAIR, HD), jnp.bfloat16), jnp.full((16, HD), NEG, jnp.bfloat16)], axis=0
    )
    key_at = lax.broadcasted_iota(jnp.int32, (rows, 2 * rows), 0)
    query_at = lax.rem(lax.broadcasted_iota(jnp.int32, (rows, 2 * rows), 1), rows)
    causal = key_at <= query_at
    for copy in in_copies[2:]:
        copy.wait()

    @pl.loop(0, chunks)
    def _(c):
        cols = cols_of(c)
        sp[0, c] = attend_pair(q[:, cols], k[:, cols], vt[c], scale, causal)

        @pl.when(s < 1)
        def _():
            sp[1, c] = neutral

        @pl.when(s < 3)
        def _():
            sp[2, c] = neutral

    for j in range(1, dps):
        id_share(j).wait_recv()
    ids_copy = pltpu.make_async_copy(ids_rx, ids_s, ids_sem)
    ids_copy.start()
    ids_copy.wait()
    db_copy.wait()

    def forward(c):
        cq_hop(c, 2).wait_recv()
        cq_hop(c, 3).start()

    def send_merged(c):
        cp_hop(c, 3).wait_recv()
        both = [ctx[2, c], cp[3, c]]
        ctx[2, c] = pack_piece([merge_pieces(both, h) for h in range(2)])
        cp_hop(c, 2).start()

    forward(0)
    at_start = lax.rem(lax.broadcasted_iota(jnp.int32, (1, rows), 1), few) == 0

    @pl.loop(0, chunks)
    def _(c):
        cols = cols_of(c)

        @pl.when(s == 1)
        def _():
            kv_hop(c, 0).wait_recv()
            kv_hop(c, 1).wait_recv()
            sp[1, c] = attend_pair(q[:, cols], k0[c], vt0[c], scale)

            @pl.loop(0, 2)
            def _(slot):
                q_arrived(c, slot)
                both_k = jnp.concatenate([k0[c], k[:, cols]], axis=0)
                both_v = jnp.concatenate([vt0[c], vt[c]], axis=1)
                stx[slot, c] = attend_pair(qin[slot, c], both_k, both_v, scale)
                sp_hop(c, slot, 2 + slot, 1).start()

        @pl.when(s == 2)
        def _():
            q_arrived(c, 1)
            stx[1, c] = attend_pair(qin[1, c], k[:, cols], vt[c], scale)
            sp_hop(c, 1, 3, 2).start()

        @pl.loop(0, db.shape[1])
        def _(b):
            dvt[b] = turned(db[1, b, :, cols])

        def cross_part(j):
            keys, vts, shards = [], [], []
            for which, span in ((0, 0), (0, 1), (1, 1)):
                blocks = [ids_s[j, which, span, n, 1] for n in range(NEIGH)]
                shards.append([ids_s[j, which, span, n, 0] for n in range(NEIGH)])
                keys.append(jnp.concatenate([db[0, b, :, cols] for b in blocks], axis=0))
                vts.append(jnp.concatenate([dvt[b] for b in blocks], axis=1))
            owned = []
            for n in range(NEIGH):
                early = jnp.broadcast_to(shards[0][n], (1, rows)) == d
                late = jnp.where(at_start, shards[1][n], shards[2][n]) == d
                late = jnp.logical_and(late, jnp.logical_or(at_start, s > 0))
                row = jnp.concatenate([jnp.where(early, 1, 0), jnp.where(late, 1, 0)], axis=1)
                owned.append(jnp.broadcast_to(row, (RETR, 2 * rows)))
            owned = jnp.concatenate(owned, axis=0) > 0
            asked = cqr[c] if j == 0 else cqin[j, c]
            return cross_pair(asked, keys, vts, owned, at_start, scale)

        cq_hop(c, 3).wait_recv()
        across, beside = cross_part(2), cross_part(3)
        ctx[2, c] = across
        ctx[3, c] = beside
        cp_hop(c, 3).start()

        @pl.when(c + 1 < chunks)
        def _():
            forward(c + 1)

        @pl.when(c > 0)
        def _():
            send_merged(c - 1)

        cq_hop(c, 1).wait_recv()
        near, own = cross_part(1), cross_part(0)
        ctx[1, c] = near
        ctx[0, c] = own
        cp_hop(c, 1).start()

    send_merged(chunks - 1)

    @pl.loop(0, chunks)
    def _(c):
        @pl.when(s >= 2)
        def _():
            sp_hop(c, 0, 2, 1).wait_recv()

        @pl.when(s == 3)
        def _():
            sp_hop(c, 0, 3, 2).wait_recv()

        cp_hop(c, 1).wait_recv()
        cp_hop(c, 2).wait_recv()
        self_pieces = [sp[i, c] for i in range(3)]
        cross_pieces = [ctx[0, c], cp[1, c], cp[2, c]]
        for h in range(2):
            back = (turn, rows - 1)[h]
            both = merge_pieces(self_pieces, h)[0].T
            both = both + pltpu.roll(merge_pieces(cross_pieces, h)[0].T, back, axis=0)
            att[:, pl.ds(pl.multiple_of(c * PAIR + h * HD, HD), HD)] = both.astype(jnp.bfloat16)

    def tile_cols(t):
        return pl.ds(pl.multiple_of(t * TILE, TILE), TILE)

    w_copies[0].wait()

    @pl.loop(0, tiles)
    def _(t):
        ptx[t] = jnp.dot(
            att[...], w[0, :, tile_cols(t)], preferred_element_type=jnp.float32
        ).astype(jnp.bfloat16)
        p_hop(t).start()

    w_copies[1].wait()

    @pl.loop(0, tiles)
    def _(t):
        own = jnp.dot(att[...], w[1, :, tile_cols(t)], preferred_element_type=jnp.float32)
        p_hop(t).wait_recv()
        out[:, tile_cols(t)] = (own + prx[t].astype(jnp.float32)).astype(jnp.bfloat16)

    @pl.when(s < 3)
    def _():
        id_hop().wait_send()

    for j in range(1, dps):
        id_share(j).wait_send()

    @pl.loop(0, chunks)
    def _(c):
        @pl.when(s == 0)
        def _():
            kv_hop(c, 0).wait_send()
            kv_hop(c, 1).wait_send()

        @pl.when(s >= 2)
        def _():
            q_hop(c, 1).wait_send()

        @pl.when(s == 3)
        def _():
            q_hop(c, 2).wait_send()

        @pl.when(s == 1)
        def _():
            sp_hop(c, 0, 2, 1).wait_send()
            sp_hop(c, 1, 3, 1).wait_send()

        @pl.when(s == 2)
        def _():
            sp_hop(c, 1, 3, 2).wait_send()

        for j in range(1, dps):
            cq_hop(c, j).wait_send()
            cp_hop(c, j).wait_send()

    @pl.loop(0, tiles)
    def _(t):
        p_hop(t).wait_send()


def fused_device(queries, keys, values, cross_queries, neighbour_ids, database, out_weight):
    rows, feat = queries.shape[1:]
    dps = lax.axis_size("dp")
    chunks = feat // PAIR
    width = out_weight.shape[1]
    half = width // 2
    tiles = half // TILE
    ids = neighbour_ids[0]
    bf16 = jnp.bfloat16
    dma = pltpu.SemaphoreType.DMA
    vmem = pl.BlockSpec(memory_space=pltpu.VMEM)
    anywhere = pl.BlockSpec(memory_space=pl.ANY)
    scratch = [
        pltpu.VMEM((rows, feat), bf16),
        pltpu.VMEM((rows, feat), bf16),
        pltpu.VMEM((rows, feat), bf16),
        pltpu.VMEM((rows, feat), bf16),
        pltpu.VMEM((chunks, rows, PAIR), bf16),
        pltpu.VMEM((chunks, PAIR, rows), bf16),
        pltpu.VMEM((database.shape[2], PAIR, RETR), bf16),
        pltpu.VMEM(database.shape[1:], bf16),
        pltpu.VMEM((2, feat, half), bf16),
        pltpu.VMEM((chunks, rows, PAIR), bf16),
        pltpu.VMEM((chunks, PAIR, rows), bf16),
        pltpu.VMEM((2, chunks, rows, PAIR), bf16),
        pltpu.VMEM((dps, chunks, rows, PAIR), bf16),
        pltpu.VMEM((3, chunks, PIECE, rows), bf16),
        pltpu.VMEM((2, chunks, PIECE, rows), bf16),
        pltpu.VMEM((dps, chunks, PIECE, rows), bf16),
        pltpu.VMEM((dps, chunks, PIECE, rows), bf16),
        pltpu.VMEM((rows, feat), bf16),
        pltpu.VMEM((tiles, rows, TILE), bf16),
        pltpu.VMEM((tiles, rows, TILE), bf16),
        pltpu.VMEM((2,) + ids.shape, jnp.int32),
        pltpu.VMEM((dps, 2) + ids.shape, jnp.int32),
        pltpu.SMEM((dps, 2) + ids.shape, jnp.int32),
        dma((4,)), dma, dma((2,)), dma,
        dma((chunks, 2)), dma((chunks, 2)),
        dma((2, chunks)), dma((2, chunks)),
        dma((dps, chunks)), dma((dps, chunks)),
        dma((2, chunks)), dma((3, chunks)),
        dma((dps, chunks)), dma((dps, chunks)),
        dma, dma, dma((dps,)), dma((dps,)),
        dma((tiles,)), dma((tiles,)),
    ]
    flops = 2 * rows * feat * width + 2 * 2 * rows * feat * (8 * rows + dps * 6 * RETR)
    result = pl.pallas_call(
        layer_kernel,
        out_shape=jax.ShapeDtypeStruct((rows, half), bf16),
        in_specs=[anywhere] * 4 + [vmem] + [anywhere] * 2,
        out_specs=vmem,
        scratch_shapes=scratch,
        compiler_params=pltpu.CompilerParams(
            collective_id=0, has_side_effects=True, vmem_limit_bytes=60 * 1024 * 1024
        ),
        cost_estimate=pl.CostEstimate(
            flops=flops, bytes_accessed=2 * (feat * width + database.size), transcendentals=0
        ),
    )(queries[0], keys[0], values[0], cross_queries[0], ids, database[0], out_weight)
    return result[None]


def solution(mesh):
    placed = (
        P("dp", "seq", "mp"),
        P("dp", "seq", "mp"),
        P("dp", "seq", "mp"),
        P("dp", "seq", "mp"),
        P("dp", "seq", None, None),
        P("dp", None, None, None, "mp"),
        P("mp", None),
    )
    fits = mesh.shape["seq"] == 4 and mesh.shape["mp"] == 2 and mesh.shape["dp"] == 4
    return jax.shard_map(
        fused_device if fits else per_device,
        mesh=mesh,
        in_specs=placed,
        out_specs=P("dp", "seq", "mp"),
        check_vma=False,
    )
```

```python
import functools
import math

import jax
import jax.numpy as jnp
from jax import lax
from jax.experimental import pallas as pl
from jax.experimental.pallas import tpu as pltpu
from jax.sharding import PartitionSpec as P

HD = 128
SPAN = 64
NEIGH = 2
RETR = 128


masked_score = -1e30


def passed_along(value, axis, steps):
    count = lax.axis_size(axis)
    leading, last = (max(0, -steps), min(count, count - steps))
    return lax.ppermute(value, axis, [(source, source + steps) for source in range(leading, last)])


def fold_block(carry_state, query_rows, query_pos, key_rows, value_rows, key_pos, score_scale):
    summed, running_max, totals = carry_state
    scores = (
        jnp.einsum("qhe,khe->hqk", query_rows, key_rows, preferred_element_type=jnp.float32)
        * score_scale
    )
    allowed = (key_pos[None, :] <= query_pos[:, None])[None]
    scores = jnp.where(allowed, scores, masked_score)
    new_max = jnp.maximum(running_max, jnp.max(scores, axis=2))
    weights = jnp.where(allowed, jnp.exp(scores - new_max[:, :, None]), 0.0)
    totals = jnp.sum(weights, axis=2)
    summed = jnp.einsum(
        "hqk,khe->hqe", weights.astype(jnp.bfloat16), value_rows, preferred_element_type=jnp.float32
    )
    return (summed, new_max, totals)


def empty_state(heads_here, row_total):
    return (
        jnp.zeros((heads_here, row_total, HD), jnp.float32),
        jnp.full((heads_here, row_total), masked_score, jnp.float32),
        jnp.zeros((heads_here, row_total), jnp.float32),
    )


def finish_state(carry_state):
    summed, running_max, totals = carry_state
    normed = summed / totals[:, :, None]
    return jnp.transpose(normed, (1, 0, 2)).reshape(
        normed.shape[1], normed.shape[0] * normed.shape[2]
    )


def per_device(queries, keys, values, cross_queries, neighbour_ids, database, out_weight):
    row_count = queries.shape[1]
    feat_here = queries.shape[2]
    heads_here = feat_here // HD
    score_scale = 1.0 / math.sqrt(HD)
    seq_index = lax.axis_index("seq")
    own_first = seq_index * row_count
    own_pos = own_first + jnp.arange(row_count, dtype=jnp.int32)
    query_rows = queries[0].reshape(row_count, heads_here, HD)
    groups_list = [(query_rows, own_pos)]
    start_states = tuple(
        (empty_state(heads_here, group_pos.shape[0]) for group_rows, group_pos in groups_list)
    )
    key_block = lax.all_gather(keys, "seq", axis=1, tiled=True)[0]
    block_rows = key_block.shape[0]
    key_rows = key_block.reshape(block_rows, heads_here, HD)
    value_rows = lax.all_gather(values, "seq", axis=1, tiled=True)[0].reshape(
        block_rows, heads_here, HD
    )
    key_pos = jnp.arange(block_rows, dtype=jnp.int32)
    updated = []
    for carry_state, (group_rows, group_pos) in zip(start_states, groups_list):

        def visit_block(kept_state, group_rows=group_rows, group_pos=group_pos):
            return fold_block(
                kept_state, group_rows, group_pos, key_rows, value_rows, key_pos, score_scale
            )

        updated.append(visit_block(carry_state))
    states = tuple(updated)
    self_out = finish_state(states[0])
    id_pairs = neighbour_ids[0].reshape(-1, 2)
    shard_of = id_pairs[:, 0]
    block_of = id_pairs[:, 1]
    spans_here = neighbour_ids.shape[1]
    every_shard = lax.all_gather(database, "dp", axis=0, tiled=True)
    fetched = jnp.stack([every_shard[shard_of, 0, block_of], every_shard[shard_of, 1, block_of]])
    neighbour_rows = NEIGH * RETR
    grouped = fetched.reshape(2, spans_here, neighbour_rows, heads_here, HD)
    previous = passed_along(grouped[:, spans_here - 1], "seq", 1)
    extended = jnp.concatenate([previous[:, None], grouped], axis=1)
    padded = jnp.concatenate(
        [
            jnp.zeros((1, feat_here), jnp.bfloat16),
            cross_queries[0],
            jnp.zeros((SPAN - 1, feat_here), jnp.bfloat16),
        ],
        axis=0,
    )
    padded = padded.reshape(spans_here + 1, SPAN, heads_here, HD)
    scores = (
        jnp.einsum("gqhe,gkhe->ghqk", padded, extended[0], preferred_element_type=jnp.float32)
        * score_scale
    )
    row_max = jnp.max(scores, axis=3, keepdims=True)
    weights = jnp.exp(scores - row_max)
    totals = jnp.sum(weights, axis=3)
    summed_cross = jnp.einsum(
        "ghqk,gkhe->gqhe",
        weights.astype(jnp.bfloat16),
        extended[1],
        preferred_element_type=jnp.float32,
    )
    cross_out = summed_cross / jnp.transpose(totals, (0, 2, 1))[:, :, :, None]
    valid = ((jnp.arange(spans_here + 1) > 0) | (seq_index > 0)).astype(jnp.float32)
    cross_out = cross_out * valid[:, None, None, None]
    cross_out = cross_out.reshape((spans_here + 1) * SPAN, feat_here)[1 : 1 + row_count]
    attended = (self_out + cross_out).astype(jnp.bfloat16)
    own_sums = lax.psum_scatter(
        lax.dot_general(
            out_weight, attended, (((0,), (1,)), ((), ())), preferred_element_type=jnp.float32
        ).astype(jnp.bfloat16),
        "mp",
        scatter_dimension=0,
        tiled=True,
    )
    return jnp.transpose(own_sums)[None]

NEG = -1e30
LOG2E = 1.4426950408889634
PAIR = 2 * HD
PIECE = PAIR + 16
TILE = 256
MESH = pl.DeviceIdType.MESH


def nt_dot(a, b):
    return lax.dot_general(a, b, (((1,), (1,)), ((), ())), preferred_element_type=jnp.float32)


def nn_dot(a, b):
    return jnp.dot(a, b, preferred_element_type=jnp.float32)


def pack_piece(parts):
    row = lax.broadcasted_iota(jnp.int32, (16, HD), 0)
    stats = jnp.zeros((16, HD), jnp.float32)
    for index, (_, lse) in enumerate(parts):
        rest = lse
        for term in range(3):
            rounded = rest.astype(jnp.bfloat16).astype(jnp.float32)
            stats = jnp.where(row == 3 * index + term, rounded, stats)
            rest = rest - rounded
    return jnp.concatenate(
        [parts[0][0].astype(jnp.bfloat16), parts[1][0].astype(jnp.bfloat16), stats.astype(jnp.bfloat16)],
        axis=0,
    )


def by_head(q):
    blank = jnp.zeros((q.shape[0], HD), q.dtype)
    return jnp.concatenate(
        [
            jnp.concatenate([q[:, :HD], blank], axis=1),
            jnp.concatenate([blank, q[:, HD:]], axis=1),
        ],
        axis=0,
    )


def weigh(scores, scale):
    top = jnp.max(scores, axis=0, keepdims=True)
    weights = jnp.exp2((scores - top) * scale)
    total = jnp.sum(weights, axis=0, keepdims=True)
    return weights.astype(jnp.bfloat16), top, total


def attend_pair(q, k, vt, scale, allowed=None):
    scores = nt_dot(k, by_head(q))
    if allowed is not None:
        scores = jnp.where(allowed, scores, NEG)
    low, top, total = weigh(scores, scale)
    lse = top * scale + jnp.log2(total)
    inverse = 1.0 / total
    rows = q.shape[0]
    parts = []
    for h in range(2):
        lanes = slice(h * rows, (h + 1) * rows)
        summed = nn_dot(vt[h * HD : (h + 1) * HD], low[:, lanes]) * inverse[:, lanes]
        parts.append((summed, lse[:, lanes]))
    return pack_piece(parts)


def cross_pair(q, keys, vts, owned, first, scale):
    few = q.shape[0] // 2
    early, late = by_head(q[:few]), by_head(q[few:])
    late = jnp.concatenate([late[few:], late[:few]], axis=0)
    scores = jnp.concatenate(
        [nt_dot(keys[0], early), jnp.where(first, nt_dot(keys[1], late), nt_dot(keys[2], late))], axis=1
    )
    scores = jnp.where(owned, scores, NEG)
    low, top, total = weigh(scores, scale)
    some = top > 0.5 * NEG
    lse = jnp.where(some, top * scale + jnp.log2(total), NEG)
    inverse = jnp.where(some, 1.0 / total, 0.0)
    lanes = 2 * few
    early = nn_dot(vts[0], low[:, :lanes]) * inverse[:, :lanes]
    late = jnp.where(first, nn_dot(vts[1], low[:, lanes:]), nn_dot(vts[2], low[:, lanes:]))
    late = late * inverse[:, lanes:]
    left = lax.broadcasted_iota(jnp.int32, (1, lanes), 1) < few
    return pack_piece(
        [
            (jnp.where(left, early[:HD], late[:HD]), jnp.where(left, lse[:, :lanes], lse[:, lanes:])),
            (jnp.where(left, late[HD:], early[HD:]), jnp.where(left, lse[:, lanes:], lse[:, :lanes])),
        ]
    )


def merge_pieces(pieces, h):
    lses = []
    for piece in pieces:
        stats = piece[PAIR:, :].astype(jnp.float32)
        lses.append(stats[3 * h : 3 * h + 1] + stats[3 * h + 1 : 3 * h + 2] + stats[3 * h + 2 : 3 * h + 3])
    top = functools.reduce(jnp.maximum, lses)
    shares = [jnp.exp2(lse - top) for lse in lses]
    total = functools.reduce(jnp.add, shares)
    inverse = 1.0 / total
    summed = 0.0
    for piece, share in zip(pieces, shares):
        summed = summed + piece[h * HD : (h + 1) * HD, :].astype(jnp.float32) * (share * inverse)
    return summed, jnp.maximum(top + jnp.log2(total), NEG)


def layer_kernel(
    q_hbm, k_hbm, v_hbm, cq_hbm, ids, db_hbm, w_hbm, out,
    q, k, v, cq, cqr, vt, dvt, db, w, k0, vt0, qin, cqin, sp, stx, cp, ctx, att, ptx, prx, ids_tx, ids_rx, ids_s,
    in_sem, db_sem, w_sem, ids_sem, kv_ss, kv_rs, q_ss, q_rs, cq_ss, cq_rs, sp_ss, sp_rs, cp_ss, cp_rs,
    i1_ss, i1_rs, i2_ss, i2_rs, p_ss, p_rs,
):
    d = lax.axis_index("dp")
    s = lax.axis_index("seq")
    m = lax.axis_index("mp")
    dps = cqin.shape[0]
    chunks = cqin.shape[1]
    rows = q.shape[0]
    half = out.shape[1]
    tiles = half // TILE
    scale = LOG2E / math.sqrt(HD)
    other = 1 - m

    def cols_of(c):
        return pl.ds(pl.multiple_of(c * PAIR, PAIR), PAIR)

    def remote(src, dst, ss, rs, **where):
        return pltpu.make_async_remote_copy(
            src_ref=src, dst_ref=dst, send_sem=ss, recv_sem=rs, device_id=where, device_id_type=MESH
        )

    in_copies = [
        pltpu.make_async_copy(src, dst, in_sem.at[i])
        for i, (src, dst) in enumerate(((v_hbm, v), (cq_hbm, cq), (q_hbm, q), (k_hbm, k)))
    ]
    for copy in in_copies:
        copy.start()
    db_copy = pltpu.make_async_copy(db_hbm, db, db_sem)
    db_copy.start()
    w_copies = [
        pltpu.make_async_copy(
            w_hbm.at[:, pl.ds(pl.multiple_of(side * half, TILE), half)], w.at[i], w_sem.at[i]
        )
        for i, side in enumerate((other, m))
    ]

    def peer(j):
        return (d, d + 1 - 2 * lax.rem(d, 2), lax.rem(d + 2, 4), 3 - d)[j]

    barrier = pltpu.get_barrier_semaphore()
    for j in range(1, dps):
        pl.semaphore_signal(barrier, inc=1, device_id={"dp": peer(j)}, device_id_type=MESH)
    for j in range(1, 4):
        pl.semaphore_signal(barrier, inc=1, device_id={"seq": lax.rem(s + j, 4)}, device_id_type=MESH)
    pl.semaphore_signal(barrier, inc=1, device_id={"mp": other}, device_id_type=MESH)

    def turned(block):
        return jnp.concatenate([block[:, :HD].T, block[:, HD:].T], axis=0)

    turn = SPAN - 1
    few = rows // 2
    in_copies[0].wait()
    in_copies[1].wait()

    @pl.loop(0, chunks)
    def _(c):
        moved = pltpu.roll(cq[:, cols_of(c)].astype(jnp.float32), rows - turn, axis=0)
        cqr[c] = moved.astype(jnp.bfloat16)
        vt[c] = turned(v[:, cols_of(c)])

    pl.semaphore_wait(barrier, dps + 3)

    def id_hop():
        return remote(ids, ids_tx.at[1], i1_ss, i1_rs, seq=lax.rem(s + 1, 4))

    def kv_hop(c, which):
        src, dst = ((k_hbm.at[:, cols_of(c)], k0), (vt.at[c], vt0))[which]
        return remote(src, dst.at[c], kv_ss.at[c, which], kv_rs.at[c, which], seq=1)

    def q_hop(c, dest):
        slot = jnp.maximum(s - 2, 0)
        return remote(q_hbm.at[:, cols_of(c)], qin.at[slot, c], q_ss.at[dest - 1, c], q_rs.at[slot, c], seq=dest)

    def q_arrived(c, slot):
        remote(q_hbm.at[:, cols_of(c)], qin.at[slot, c], q_ss.at[0, c], q_rs.at[slot, c], seq=1).wait_recv()

    def cq_hop(c, j):
        src = cqin.at[2, c] if j == 3 else cqr.at[c]
        return remote(src, cqin.at[j, c], cq_ss.at[j, c], cq_rs.at[j, c], dp=peer(1 if j == 3 else j))

    def sp_hop(c, slot, dest, place):
        return remote(stx.at[slot, c], sp.at[place, c], sp_ss.at[slot, c], sp_rs.at[place, c], seq=dest)

    def cp_hop(c, j):
        return remote(
            ctx.at[j, c], cp.at[j, c], cp_ss.at[j, c], cp_rs.at[j, c], dp=peer(1 if j == 3 else j)
        )

    def id_share(j):
        return remote(ids_tx, ids_rx.at[j], i2_ss.at[j], i2_rs.at[j], dp=peer(j))

    def p_hop(t):
        return remote(ptx.at[t], prx.at[t], p_ss.at[t], p_rs.at[t], mp=other)

    @pl.when(s < 3)
    def _():
        id_hop().start()

    @pl.loop(0, chunks)
    def _(c):
        @pl.when(s == 0)
        def _():
            kv_hop(c, 0).start()
            kv_hop(c, 1).start()

        @pl.when(s >= 2)
        def _():
            q_hop(c, 1).start()

        @pl.when(s == 3)
        def _():
            q_hop(c, 2).start()

        cq_hop(c, 2).start()
        cq_hop(c, 1).start()

    for copy in w_copies:
        copy.start()

    ids_tx[0] = ids[...]

    @pl.when(s == 0)
    def _():
        ids_tx[1] = jnp.zeros_like(ids)

    @pl.when(s > 0)
    def _():
        id_hop().wait_recv()

    for j in range(1, dps):
        id_share(j).start()
    ids_rx[0] = ids_tx[...]

    neutral = jnp.concatenate(
        [jnp.zeros((PAIR, HD), jnp.bfloat16), jnp.full((16, HD), NEG, jnp.bfloat16)], axis=0
    )
    key_at = lax.broadcasted_iota(jnp.int32, (rows, 2 * rows), 0)
    query_at = lax.rem(lax.broadcasted_iota(jnp.int32, (rows, 2 * rows), 1), rows)
    causal = key_at <= query_at
    for copy in in_copies[2:]:
        copy.wait()

    @pl.loop(0, chunks)
    def _(c):
        cols = cols_of(c)
        sp[0, c] = attend_pair(q[:, cols], k[:, cols], vt[c], scale, causal)

        @pl.when(s < 1)
        def _():
            sp[1, c] = neutral

        @pl.when(s < 3)
        def _():
            sp[2, c] = neutral

    for j in range(1, dps):
        id_share(j).wait_recv()
    ids_copy = pltpu.make_async_copy(ids_rx, ids_s, ids_sem)
    ids_copy.start()
    ids_copy.wait()
    db_copy.wait()

    at_start = lax.rem(lax.broadcasted_iota(jnp.int32, (1, rows), 1), few) == 0

    @pl.loop(0, chunks)
    def _(c):
        cols = cols_of(c)
        cq_hop(c, 2).wait_recv()
        cq_hop(c, 3).start()

        @pl.when(s == 1)
        def _():
            kv_hop(c, 0).wait_recv()
            kv_hop(c, 1).wait_recv()
            sp[1, c] = attend_pair(q[:, cols], k0[c], vt0[c], scale)

            @pl.loop(0, 2)
            def _(slot):
                q_arrived(c, slot)
                both_k = jnp.concatenate([k0[c], k[:, cols]], axis=0)
                both_v = jnp.concatenate([vt0[c], vt[c]], axis=1)
                stx[slot, c] = attend_pair(qin[slot, c], both_k, both_v, scale)
                sp_hop(c, slot, 2 + slot, 1).start()

        @pl.when(s == 2)
        def _():
            q_arrived(c, 1)
            stx[1, c] = attend_pair(qin[1, c], k[:, cols], vt[c], scale)
            sp_hop(c, 1, 3, 2).start()

        @pl.loop(0, db.shape[1])
        def _(b):
            dvt[b] = turned(db[1, b, :, cols])

        def cross_part(j):
            keys, vts, shards = [], [], []
            for which, span in ((0, 0), (0, 1), (1, 1)):
                blocks = [ids_s[j, which, span, n, 1] for n in range(NEIGH)]
                shards.append([ids_s[j, which, span, n, 0] for n in range(NEIGH)])
                keys.append(jnp.concatenate([db[0, b, :, cols] for b in blocks], axis=0))
                vts.append(jnp.concatenate([dvt[b] for b in blocks], axis=1))
            owned = []
            for n in range(NEIGH):
                early = jnp.broadcast_to(shards[0][n], (1, rows)) == d
                late = jnp.where(at_start, shards[1][n], shards[2][n]) == d
                late = jnp.logical_and(late, jnp.logical_or(at_start, s > 0))
                row = jnp.concatenate([jnp.where(early, 1, 0), jnp.where(late, 1, 0)], axis=1)
                owned.append(jnp.broadcast_to(row, (RETR, 2 * rows)))
            owned = jnp.concatenate(owned, axis=0) > 0
            asked = cqr[c] if j == 0 else cqin[j, c]
            return cross_pair(asked, keys, vts, owned, at_start, scale)

        cq_hop(c, 3).wait_recv()
        across, beside = cross_part(2), cross_part(3)
        ctx[3, c] = beside
        cp_hop(c, 3).start()
        cq_hop(c, 1).wait_recv()
        near, own = cross_part(1), cross_part(0)
        ctx[1, c] = near
        ctx[0, c] = own
        cp_hop(c, 1).start()
        cp_hop(c, 3).wait_recv()
        both = [across, cp[3, c]]
        ctx[2, c] = pack_piece([merge_pieces(both, h) for h in range(2)])
        cp_hop(c, 2).start()

    @pl.loop(0, chunks)
    def _(c):
        @pl.when(s >= 2)
        def _():
            sp_hop(c, 0, 2, 1).wait_recv()

        @pl.when(s == 3)
        def _():
            sp_hop(c, 0, 3, 2).wait_recv()

        cp_hop(c, 1).wait_recv()
        cp_hop(c, 2).wait_recv()
        self_pieces = [sp[i, c] for i in range(3)]
        cross_pieces = [ctx[0, c], cp[1, c], cp[2, c]]
        for h in range(2):
            back = (turn, rows - 1)[h]
            both = merge_pieces(self_pieces, h)[0].T
            both = both + pltpu.roll(merge_pieces(cross_pieces, h)[0].T, back, axis=0)
            att[:, pl.ds(pl.multiple_of(c * PAIR + h * HD, HD), HD)] = both.astype(jnp.bfloat16)

    def tile_cols(t):
        return pl.ds(pl.multiple_of(t * TILE, TILE), TILE)

    w_copies[0].wait()

    @pl.loop(0, tiles)
    def _(t):
        ptx[t] = jnp.dot(
            att[...], w[0, :, tile_cols(t)], preferred_element_type=jnp.float32
        ).astype(jnp.bfloat16)
        p_hop(t).start()

    w_copies[1].wait()

    @pl.loop(0, tiles)
    def _(t):
        own = jnp.dot(att[...], w[1, :, tile_cols(t)], preferred_element_type=jnp.float32)
        p_hop(t).wait_recv()
        out[:, tile_cols(t)] = (own + prx[t].astype(jnp.float32)).astype(jnp.bfloat16)

    @pl.when(s < 3)
    def _():
        id_hop().wait_send()

    for j in range(1, dps):
        id_share(j).wait_send()

    @pl.loop(0, chunks)
    def _(c):
        @pl.when(s == 0)
        def _():
            kv_hop(c, 0).wait_send()
            kv_hop(c, 1).wait_send()

        @pl.when(s >= 2)
        def _():
            q_hop(c, 1).wait_send()

        @pl.when(s == 3)
        def _():
            q_hop(c, 2).wait_send()

        @pl.when(s == 1)
        def _():
            sp_hop(c, 0, 2, 1).wait_send()
            sp_hop(c, 1, 3, 1).wait_send()

        @pl.when(s == 2)
        def _():
            sp_hop(c, 1, 3, 2).wait_send()

        for j in range(1, dps):
            cq_hop(c, j).wait_send()
            cp_hop(c, j).wait_send()

    @pl.loop(0, tiles)
    def _(t):
        p_hop(t).wait_send()


def fused_device(queries, keys, values, cross_queries, neighbour_ids, database, out_weight):
    rows, feat = queries.shape[1:]
    dps = lax.axis_size("dp")
    chunks = feat // PAIR
    width = out_weight.shape[1]
    half = width // 2
    tiles = half // TILE
    ids = neighbour_ids[0]
    bf16 = jnp.bfloat16
    dma = pltpu.SemaphoreType.DMA
    vmem = pl.BlockSpec(memory_space=pltpu.VMEM)
    anywhere = pl.BlockSpec(memory_space=pl.ANY)
    scratch = [
        pltpu.VMEM((rows, feat), bf16),
        pltpu.VMEM((rows, feat), bf16),
        pltpu.VMEM((rows, feat), bf16),
        pltpu.VMEM((rows, feat), bf16),
        pltpu.VMEM((chunks, rows, PAIR), bf16),
        pltpu.VMEM((chunks, PAIR, rows), bf16),
        pltpu.VMEM((database.shape[2], PAIR, RETR), bf16),
        pltpu.VMEM(database.shape[1:], bf16),
        pltpu.VMEM((2, feat, half), bf16),
        pltpu.VMEM((chunks, rows, PAIR), bf16),
        pltpu.VMEM((chunks, PAIR, rows), bf16),
        pltpu.VMEM((2, chunks, rows, PAIR), bf16),
        pltpu.VMEM((dps, chunks, rows, PAIR), bf16),
        pltpu.VMEM((3, chunks, PIECE, rows), bf16),
        pltpu.VMEM((2, chunks, PIECE, rows), bf16),
        pltpu.VMEM((dps, chunks, PIECE, rows), bf16),
        pltpu.VMEM((dps, chunks, PIECE, rows), bf16),
        pltpu.VMEM((rows, feat), bf16),
        pltpu.VMEM((tiles, rows, TILE), bf16),
        pltpu.VMEM((tiles, rows, TILE), bf16),
        pltpu.VMEM((2,) + ids.shape, jnp.int32),
        pltpu.VMEM((dps, 2) + ids.shape, jnp.int32),
        pltpu.SMEM((dps, 2) + ids.shape, jnp.int32),
        dma((4,)), dma, dma((2,)), dma,
        dma((chunks, 2)), dma((chunks, 2)),
        dma((2, chunks)), dma((2, chunks)),
        dma((dps, chunks)), dma((dps, chunks)),
        dma((2, chunks)), dma((3, chunks)),
        dma((dps, chunks)), dma((dps, chunks)),
        dma, dma, dma((dps,)), dma((dps,)),
        dma((tiles,)), dma((tiles,)),
    ]
    flops = 2 * rows * feat * width + 2 * 2 * rows * feat * (8 * rows + dps * 6 * RETR)
    result = pl.pallas_call(
        layer_kernel,
        out_shape=jax.ShapeDtypeStruct((rows, half), bf16),
        in_specs=[anywhere] * 4 + [vmem] + [anywhere] * 2,
        out_specs=vmem,
        scratch_shapes=scratch,
        compiler_params=pltpu.CompilerParams(
            collective_id=0, has_side_effects=True, vmem_limit_bytes=60 * 1024 * 1024
        ),
        cost_estimate=pl.CostEstimate(
            flops=flops, bytes_accessed=2 * (feat * width + database.size), transcendentals=0
        ),
    )(queries[0], keys[0], values[0], cross_queries[0], ids, database[0], out_weight)
    return result[None]


def solution(mesh):
    placed = (
        P("dp", "seq", "mp"),
        P("dp", "seq", "mp"),
        P("dp", "seq", "mp"),
        P("dp", "seq", "mp"),
        P("dp", "seq", None, None),
        P("dp", None, None, None, "mp"),
        P("mp", None),
    )
    fits = mesh.shape["seq"] == 4 and mesh.shape["mp"] == 2 and mesh.shape["dp"] == 4
    return jax.shard_map(
        fused_device if fits else per_device,
        mesh=mesh,
        in_specs=placed,
        out_specs=P("dp", "seq", "mp"),
        check_vma=False,
    )
```
